128 devices in a mesh: ctx: 8 (over y, core), exp: 16 (over z, x).
Axes of the slice: x: 4, y: 4, z: 4, core: 2. Of those that a mesh axis runs over, the one named last changes fastest.
Arguments:
- stream_in: bfloat16 [16, 1024, 2560], P('exp', 'ctx'), may hold values from -1.75 to 1.75
- queries: bfloat16 [16, 1024, 12288], P('exp', 'ctx'), may hold values from -8 to 8
- latents: bfloat16 [16, 1024, 512], P('exp', 'ctx'), may hold values from -6 to 6
- key_rope: bfloat16 [16, 1024, 64], P('exp', 'ctx'), may hold values from -8 to 8
- w_uk: bfloat16 [512, 8192], P(None, 'ctx'), may hold values from -0.25 to 0.25
- w_uv: bfloat16 [512, 8192], P(None, 'ctx'), may hold values from -0.25 to 0.25
- w_o: bfloat16 [8192, 2560], P('ctx'), may hold values from -0.1875 to 0.1875
- norm_gain: float32 [2560], replicated, may hold values from 0.25 to 1.75
- expert_ids: int32 [16, 1024, 6], P('exp', 'ctx'), may hold values from 0 to 127, all different within a row; in each aligned block of 128 rows (0 to 127, 128 to 255, ..., all dimensions but the last counted through in order) at most 9 rows name the same one
- gate_weights: float32 [16, 1024, 6], P('exp', 'ctx'), may hold values from 0.05 to 0.45
- w_gate: bfloat16 [128, 2560, 768], P(('ctx', 'exp')), may hold values from -0.125 to 0.125
- w_up: bfloat16 [128, 2560, 768], P(('ctx', 'exp')), may hold values from -0.125 to 0.125
- w_down: bfloat16 [128, 768, 2560], P(('ctx', 'exp')), may hold values from -0.21875 to 0.21875
Outputs:
- layer_out: bfloat16 [16, 1024, 2560], P('exp', 'ctx')
The draws below stay inside these ranges and needn't reach their ends.
Inputs may be any that keep to these rules, and one draw needn't show every extreme that they name: `expert_ids`: each position names 6 different experts; among the positions of one source no expert is named more than 9 times, and in some sources an expert is named exactly 9 times.
All inputs are finite; a program needn't handle non-finite values.
Results may differ from the reference program's by a relative error of at most 0.023.
Values may be sent and summed in bfloat16 or wider, within the bound.
A program may use at most 128 MiB of HBM per device.

```python
import math
import jax
import jax.numpy as jnp
import numpy as np
from jax import lax

D = 2560
H = 64
NOPE = 128
ROPE = 64
VDIM = 128
KVL = 512
FF = 768
TOPK = 6
TOK_DEV = 128
SEQS = 16
LEN = 1024
HEADS_DEV = 8
EXPERTS = 128
CAP = 9
N_CTX = 8
DEVICES = 128


def draw_queries(key, part):
    key = jax.random.fold_in(key, 2)
    width = NOPE + ROPE
    base = jnp.clip(jax.random.normal(key, (SEQS, LEN, H, width), jnp.float32), -4.0, 4.0)
    return base.reshape(SEQS, LEN, H * width).astype(jnp.bfloat16)


def draw_key_rope(key, part):
    key = jax.random.fold_in(key, 3)
    base = jnp.clip(jax.random.normal(key, (SEQS, LEN, ROPE), jnp.float32), -4.0, 4.0)
    return base.astype(jnp.bfloat16)


def level_of(rng, shape, shards, least, top_value):
    factor_of, own = 1.0, jax.random.fold_in(rng, 6)
    for axis_at, parts in shards:
        draws = jnp.exp(jax.random.uniform(jax.random.fold_in(own, axis_at), (parts,), jnp.float32, least / len(shards), top_value / len(shards)))
        factor_of = factor_of * jnp.repeat(draws, shape[axis_at] // parts).reshape([-1 if axis == axis_at else 1 for axis in range(len(shape))])
    return factor_of


def deal_out(own_key, own, number, rows, amount, top, most, slope):
    ranking = jax.random.permutation(own_key, amount)
    crowded, common = portions_of(amount, rows * top, most, slope, True), portions_of(amount, rows * top, most, slope, False)
    places = jnp.arange(amount)

    def named(lengths, rotation):
        used = int((lengths > 0).sum())
        fixed = max(1, used // 4)
        moved = fixed + (places - fixed + rotation * (used - fixed)) % max(1, amount - fixed)
        return jnp.zeros((amount,), jnp.int32).at[ranking[jnp.where(places < fixed, places, moved)]].set(jnp.asarray(lengths, jnp.int32))

    lengths = jnp.where(number % 4 == 0, named(crowded, number // 4), named(common, number - number // 4 - 1))
    mixed = jax.random.permutation(jax.random.fold_in(own, 3), amount)
    source_of, taker = mixed[0:amount // 2 * 2:2], mixed[1:amount // 2 * 2:2]
    room = jnp.minimum(lengths[source_of] - 1, most - lengths[taker]) // 2
    room = jnp.where((source_of == ranking[0]) | (taker == ranking[0]) | (lengths[taker] == 0), 0, jnp.maximum(room, 0))
    moved = jax.random.randint(jax.random.fold_in(own, 4), (amount // 2,), 0, 1 << 20) % (room + 1)
    lengths = lengths.at[source_of].add(-moved).at[taker].add(moved)
    labels = jnp.searchsorted(jnp.cumsum(lengths), jnp.arange(rows * top), side="right").astype(jnp.int32)
    listing = labels.reshape(top, rows).T
    listing = listing[jax.random.permutation(jax.random.fold_in(own, 1), rows)]
    rotation = jax.random.randint(jax.random.fold_in(own, 2), (rows, 1), 0, top)
    return jnp.take_along_axis(listing, (jnp.arange(top)[None, :] + rotation) % top, axis=1)


def portions_of(count, total, limit, slope, full):
    portions = [(1 << 20) // math.isqrt(standing ** slope) + 1 for standing in range(1, count + 1)]
    largest = limit if full else min(limit, max(-(-total // count), total * portions[0] // sum(portions)))
    least = 1 if total - largest >= count - 1 else 0
    counts, surplus = [largest] + [least] * (count - 1), total - largest - least * (count - 1)
    while surplus > 0:
        candidates = [i for i in range(1, count) if counts[i] < largest] or [i for i in range(1, count) if counts[i] < limit]
        pool, remaining = sum([portions[i] for i in candidates]), surplus
        for i in candidates:
            addition = min(limit - counts[i], max(1, remaining * portions[i] // pool), surplus)
            counts[i] = counts[i] + addition
            surplus = surplus - addition
    return np.array(counts)


def centred(stream_key, dims, deviation, bound, cuts=(), dtype=jnp.bfloat16):
    loudness = level_of(stream_key, dims, cuts, -0.22, 0.18) if cuts else 1.0
    values = jax.random.normal(stream_key, dims, jnp.float32) * deviation * loudness
    return jnp.minimum(jnp.maximum(values, -bound), bound).astype(dtype)


def setup_inputs(seed: int = 0) -> dict:
    streams_of = jax.random.split(jax.random.key(seed), 14)
    stream_in = centred(streams_of[0], (SEQS, LEN, D), 0.3, 1.75, ((0, 16), (1, 8)))
    queries = draw_queries(jax.random.fold_in(streams_of[13], 71), 0)
    latents = centred(streams_of[2], (SEQS, LEN, KVL), 1.0, 6.0, ((0, 16), (1, 8)))
    key_rope = draw_key_rope(jax.random.fold_in(streams_of[13], 71), 0)
    w_uk = centred(streams_of[4], (KVL, H * NOPE), KVL ** -0.5, 0.25, ((1, 8),))
    w_uv = centred(streams_of[5], (KVL, H * VDIM), KVL ** -0.5, 0.25, ((1, 8),))
    w_o = centred(streams_of[6], (H * VDIM, D), (3.0 / (H * VDIM) ** 0.5), 0.1875, ((0, 8),))
    norm_gain = jnp.clip(1.0 + 0.15 * jax.random.normal(streams_of[7], (D,), jnp.float32), 0.25, 1.75)
    expert_ids_keys = jax.random.split(jax.random.fold_in(streams_of[8], 1), SEQS * LEN // TOK_DEV)
    expert_ids_turns = jax.random.permutation(jax.random.fold_in(streams_of[8], 3), SEQS * LEN // TOK_DEV)
    expert_ids = jax.vmap(lambda own, number: deal_out(jax.random.fold_in(streams_of[8], 2), own, number, TOK_DEV, EXPERTS, TOPK, CAP, 2))(expert_ids_keys, expert_ids_turns).reshape((SEQS, LEN, TOPK))
    gate_weights = jnp.clip(0.05 + 0.39999999 * jax.random.uniform(streams_of[9], (SEQS, LEN, TOPK), jnp.float32) ** level_of(streams_of[9], (SEQS, LEN, TOPK), ((0, 16), (1, 8)), -0.2, 0.2), 0.05, 0.45)
    w_gate = centred(streams_of[10], (EXPERTS, D, FF), D ** -0.5, 0.125, ((0, 128),))
    w_up = centred(streams_of[11], (EXPERTS, D, FF), D ** -0.5, 0.125, ((0, 128),))
    w_down = centred(streams_of[12], (EXPERTS, FF, D), FF ** -0.5, 0.21875, ((0, 128),))
    return dict(stream_in=stream_in, queries=queries, latents=latents, key_rope=key_rope, w_uk=w_uk, w_uv=w_uv, w_o=w_o, norm_gain=norm_gain, expert_ids=expert_ids, gate_weights=gate_weights, w_gate=w_gate, w_up=w_up, w_down=w_down)


def attend(query_seq, latent_seq, rope_seq, w_uk, w_uv, w_o):
    keys_nope = jnp.dot(latent_seq, w_uk, preferred_element_type=jnp.float32).astype(jnp.bfloat16)
    values = jnp.dot(latent_seq, w_uv, preferred_element_type=jnp.float32).astype(jnp.bfloat16)
    head_queries = query_seq.reshape(LEN, H, NOPE + ROPE).transpose(1, 0, 2)
    head_keys = keys_nope.reshape(LEN, H, NOPE).transpose(1, 0, 2)
    head_values = values.reshape(LEN, H, VDIM).transpose(1, 0, 2)
    score_scale = 1.0 / math.sqrt(NOPE + ROPE)
    causal = jnp.arange(LEN)[:, None] >= jnp.arange(LEN)[None, :]

    def one_head(head_parts):
        one_query, key_nope, one_value = head_parts
        key_full = jnp.concatenate([key_nope, rope_seq], axis=1)
        scores = jnp.dot(one_query, key_full.T, preferred_element_type=jnp.float32) * score_scale
        scores = jnp.where(causal, scores, -jnp.inf)
        row_peak = lax.optimization_barrier(jnp.max(scores, axis=1, keepdims=True))
        weights = jnp.exp(scores - row_peak)
        weights = (weights / lax.optimization_barrier(jnp.sum(weights, axis=1, keepdims=True))).astype(jnp.bfloat16)
        return jnp.dot(weights, one_value, preferred_element_type=jnp.float32).astype(jnp.bfloat16)
    heads_out = lax.map(one_head, (head_queries, head_keys, head_values))
    mixed_heads = heads_out.transpose(1, 0, 2).reshape(LEN, N_CTX, HEADS_DEV * VDIM).transpose(1, 0, 2)
    groups = w_o.reshape(N_CTX, HEADS_DEV * VDIM, D)

    def group_term(group_parts):
        return jnp.dot(group_parts[0], group_parts[1], preferred_element_type=jnp.float32).astype(jnp.bfloat16)
    terms = lax.map(group_term, (mixed_heads, groups))
    return lax.optimization_barrier(jnp.sum(terms.astype(jnp.float32), axis=0))

def by_device(array):
    rest = array.shape[2:]
    split = array.reshape((SEQS, N_CTX, TOK_DEV) + rest)
    return jnp.swapaxes(split, 0, 1).reshape((DEVICES, TOK_DEV) + rest)

def reference(stream_in, queries, latents, key_rope, w_uk, w_uv, w_o, norm_gain, expert_ids, gate_weights, w_gate, w_up, w_down):

    def one_sequence(seq_parts):
        return attend(seq_parts[0], seq_parts[1], seq_parts[2], w_uk, w_uv, w_o)
    attention = lax.map(one_sequence, (queries, latents, key_rope))
    hidden = (stream_in.astype(jnp.float32) + attention).astype(jnp.bfloat16)
    hidden_f = hidden.astype(jnp.float32)
    mean_square = lax.optimization_barrier(jnp.mean(hidden_f * hidden_f, axis=-1, keepdims=True))
    normed = (hidden_f * lax.rsqrt(mean_square + 1e-06) * norm_gain.astype(jnp.float32)).astype(jnp.bfloat16)
    token_rows = by_device(normed).reshape(DEVICES * TOK_DEV, D)
    route_ids = by_device(expert_ids).reshape(DEVICES, TOK_DEV * TOPK).astype(jnp.int32)
    gate_flat = by_device(gate_weights).reshape(DEVICES * TOK_DEV * TOPK).astype(jnp.float32)
    onehot = (route_ids[:, :, None] == jnp.arange(EXPERTS).astype(jnp.int32)[None, None, :]).astype(jnp.int32)
    slot_index = lax.optimization_barrier(jnp.sum(jnp.cumsum(onehot, axis=1) * onehot, axis=2)) - 1
    source = jnp.arange(DEVICES).astype(jnp.int32)[:, None]
    position = ((route_ids * DEVICES + source) * CAP + slot_index).reshape(-1).astype(jnp.int32)
    token_index = (source * TOK_DEV + jnp.arange(TOK_DEV * TOPK).astype(jnp.int32)[None, :] // TOPK).reshape(-1)
    source_rows = jnp.zeros((EXPERTS * DEVICES * CAP,), jnp.int32).at[position].set(token_index.astype(jnp.int32))
    source_rows = source_rows.reshape(EXPERTS, DEVICES * CAP)
    row_weights = jnp.zeros((EXPERTS * DEVICES * CAP,), jnp.float32).at[position].set(gate_flat)
    row_weights = row_weights.reshape(EXPERTS, DEVICES * CAP)

    def expert(running, expert_parts):
        slot_rows, weight, gate_w, up_w, down_w = expert_parts
        picked = token_rows[slot_rows]
        gate_part = jnp.dot(picked, gate_w, preferred_element_type=jnp.float32)
        up_part = jnp.dot(picked, up_w, preferred_element_type=jnp.float32)
        active = (jax.nn.silu(gate_part) * up_part).astype(jnp.bfloat16)
        result = jnp.dot(active, down_w, preferred_element_type=jnp.float32).astype(jnp.bfloat16)
        running = running.at[slot_rows].add(weight[:, None] * result.astype(jnp.float32))
        return (running, None)
    start_sum = jnp.zeros((DEVICES * TOK_DEV, D), jnp.float32)
    combined, _ = lax.scan(expert, start_sum, (source_rows, row_weights, w_gate, w_up, w_down))
    combined = jnp.swapaxes(combined.reshape(N_CTX, SEQS, TOK_DEV, D), 0, 1).reshape(SEQS, LEN, D)
    return (hidden.astype(jnp.float32) + combined).astype(jnp.bfloat16)
```

```python
import functools
import math

import jax
import jax.numpy as jnp
from jax import lax
from jax.experimental import pallas as pl
from jax.experimental.pallas import tpu as pltpu
from jax.sharding import PartitionSpec as P

NOPE = 128
ROPE = 64
VDIM = 128
KVL = 512
D = 2560
FF = 768
TOPK = 6
CAP = 9
TOK = 128
LEN = 1024
QW = 1536
RING = 4
ROWS = 72
CHUNKS = 5
CW = 256
HALF = 1280
CHIP = 256
LATW = 640
MESH = pl.DeviceIdType.MESH
BF = jnp.bfloat16
F32 = jnp.float32
ANY = pl.BlockSpec(memory_space=pl.ANY)
VM = pl.BlockSpec(memory_space=pltpu.VMEM)
DMA = pltpu.SemaphoreType.DMA


def place():
    c = lax.axis_index("ctx")
    e = lax.axis_index("exp")
    return c // 2, c % 2, e // RING, e % RING


def device(y, core, z, x):
    return (y * 2 + core, z * RING + x)


def step(v, d):
    return lax.rem(v + d, RING)


def remote(src, dst, send, recv, target):
    return pltpu.make_async_remote_copy(
        src_ref=src, dst_ref=dst, send_sem=send, recv_sem=recv, device_id=target, device_id_type=MESH
    )


def greet(targets):
    barrier = pltpu.get_barrier_semaphore()
    for target in targets:
        pl.semaphore_signal(barrier, inc=1, device_id=target, device_id_type=MESH)
    pl.semaphore_wait(barrier, len(targets))


def attention_kernel(
    q_hbm, lat_hbm, uk_ref, uv_ref, out_ref, qbuf, lat, kbuf, vbuf, q_send, q_recv, l_send, l_recv, own_sem
):
    y, core, z, x = place()
    me = y * 2 + core
    peers = [(dy, dc) for dy in (0, 1, 3, 2) for dc in (0, 1) if (dy, dc) != (0, 0)]
    greet([device(step(y, dy), lax.rem(core + dc, 2), z, x) for dy, dc in peers])

    def lat_copy(dy, dc):
        i = dy * 2 + dc
        target = device(step(y, dy), lax.rem(core + dc, 2), z, x)
        return remote(lat_hbm, lat.at[me], l_send.at[i], l_recv.at[i], target)

    def q_copy(dy, dc):
        i = dy * 2 + dc
        yy, cc = step(y, dy), lax.rem(core + dc, 2)
        columns = pl.ds(pl.multiple_of((yy * 2 + cc) * QW, 128), QW)
        return remote(q_hbm.at[:, columns], qbuf.at[me], q_send.at[i], q_recv.at[i], device(yy, cc, z, x))

    own_lat = pltpu.make_async_copy(lat_hbm, lat.at[me], own_sem.at[0])
    own_q = pltpu.make_async_copy(
        q_hbm.at[:, pl.ds(pl.multiple_of(me * QW, 128), QW)], qbuf.at[me], own_sem.at[1]
    )
    own_lat.start()
    own_q.start()
    for dy, dc in peers:
        lat_copy(dy, dc).start()
    for dy, dc in peers:
        q_copy(dy, dc).start()
    own_lat.wait()
    own_q.wait()
    for dy, dc in peers:
        lat_copy(dy, dc).wait()

    lane = lax.broadcasted_iota(jnp.int32, (CHIP, 128), 1)

    def project(b, carry):
        rows = pl.ds(pl.multiple_of(b * CHIP, CHIP), CHIP)
        block = lat[pl.ds(b * 2, 2)].reshape(CHIP, LATW)
        latent = block[:, :KVL]
        rope = block[:, KVL:].astype(F32)
        rope_low = jnp.where(lane < 64, rope, 0.0).astype(BF)
        rope_high = pltpu.roll(rope, 64, 1)
        for h in range(8):
            nope = jnp.dot(latent, uk_ref[:, h * 128 : h * 128 + 128], preferred_element_type=F32)
            if h % 2 == 0:
                kbuf[h, rows, 0:128] = nope.astype(BF)
                kbuf[h, rows, 128:256] = rope_low
            else:
                turned = pltpu.roll(nope, 64, 1)
                kbuf[h, rows, 0:128] = jnp.where(lane < 64, 0.0, turned).astype(BF)
                kbuf[h, rows, 128:256] = jnp.where(lane < 64, turned, rope_high).astype(BF)
        vbuf[rows, :] = jnp.dot(latent, uv_ref[...], preferred_element_type=F32).astype(BF)
        return carry

    lax.fori_loop(0, RING, project, 0)

    factor = 1.0 / math.sqrt(NOPE + ROPE) * math.log2(math.e)
    row_at = lax.broadcasted_iota(jnp.int32, (CHIP, CHIP), 0)
    col_at = lax.broadcasted_iota(jnp.int32, (CHIP, CHIP), 1)
    causal = row_at >= col_at

    def attend(block):
        length = (block + 1) * CHIP

        def pair(p, carry):
            columns = pl.ds(pl.multiple_of(p * 384, 128), 384)
            q = qbuf[block * 2 : block * 2 + 2, :, columns].reshape(CHIP, 384)
            outs = []
            for odd in range(2):
                query = q[:, odd * 128 : odd * 128 + 256]
                head = p * 2 + odd
                contract = (((1,), (1,)), ((), ()))
                last = lax.dot_general(
                    query, kbuf[head, length - CHIP : length], contract, preferred_element_type=F32
                )
                last = jnp.where(causal, last, -jnp.inf)
                peak = jnp.max(last, axis=1, keepdims=True)
                if block:
                    first = lax.dot_general(
                        query, kbuf[head, 0 : length - CHIP], contract, preferred_element_type=F32
                    )
                    peak = jnp.maximum(peak, jnp.max(first, axis=1, keepdims=True))
                values = pl.ds(pl.multiple_of(head * 128, 128), 128)
                weight = jnp.exp2((last - peak) * factor)
                total = jnp.sum(weight, axis=1, keepdims=True)
                result = jnp.dot(
                    weight.astype(BF), vbuf[length - CHIP : length, values], preferred_element_type=F32
                )
                if block:
                    weight = jnp.exp2((first - peak) * factor)
                    total += jnp.sum(weight, axis=1, keepdims=True)
                    result += jnp.dot(
                        weight.astype(BF), vbuf[0 : length - CHIP, values], preferred_element_type=F32
                    )
                outs.append((result / total).astype(BF))
            out_ref[block * CHIP : (block + 1) * CHIP, pl.ds(pl.multiple_of(p * 256, 256), 256)] = (
                jnp.concatenate(outs, axis=1)
            )
            return carry

        lax.fori_loop(0, 4, pair, 0)

    for dy in (0, 1, 3, 2):
        for dc in range(2):
            if (dy, dc) != (0, 0):
                q_copy((4 - dy) % 4, dc).wait_recv()
        source = lax.rem(y + dy, RING)
        for block in range(RING):
            pl.when(source == block)(functools.partial(attend, block))
    for dy, dc in peers:
        q_copy(dy, dc).wait_send()


def attention_call(queries, latrope, w_uk, w_uv):
    return pl.pallas_call(
        attention_kernel,
        out_shape=jax.ShapeDtypeStruct((LEN, 1024), BF),
        in_specs=[ANY, ANY, VM, VM],
        out_specs=VM,
        scratch_shapes=[
            pltpu.VMEM((8, TOK, QW), BF),
            pltpu.VMEM((8, TOK, LATW), BF),
            pltpu.VMEM((8, LEN, 256), BF),
            pltpu.VMEM((LEN, 1024), BF),
            DMA((8,)),
            DMA((8,)),
            DMA((8,)),
            DMA((8,)),
            DMA((2,)),
        ],
        compiler_params=pltpu.CompilerParams(
            collective_id=1, has_side_effects=True, vmem_limit_bytes=48 * 2**20
        ),
        name="attention",
    )(queries, latrope, w_uk, w_uv)


def exp_targets(y, core, z, x):
    found = [device(y, 1 - core, z, x)]
    for d in (1, 2, 3):
        found.append(device(step(y, d), core, z, x))
        found.append(device(y, core, step(z, d), x))
        found.append(device(y, core, z, step(x, d)))
    return found


def first_phase(j, spot, src, mid, send, recv, own):
    y, core, z, x = spot
    copies = []
    for d in (1, 3, 2):
        xx, zz = step(x, d), step(z, d)
        copies.append(
            remote(src.at[j, 0, :, xx], mid.at[j, 0, x], send.at[j, d], recv.at[j, d], device(y, core, z, xx))
        )
        copies.append(
            remote(
                src.at[j, 1, zz], mid.at[j, 1, z], send.at[j, 3 + d], recv.at[j, 3 + d], device(y, core, zz, x)
            )
        )
    copies.append(pltpu.make_async_copy(src.at[j, 0, :, x], mid.at[j, 0, x], own.at[j, 0]))
    copies.append(pltpu.make_async_copy(src.at[j, 1, z], mid.at[j, 1, z], own.at[j, 1]))
    return copies


def second_phase(j, spot, mid, dst, send, recv, own):
    y, core, z, x = spot
    copies = []
    for d in (1, 3, 2):
        xx, zz = step(x, d), step(z, d)
        copies.append(
            remote(mid.at[j, 0, :, zz], dst.at[j, 0, z], send.at[j, d], recv.at[j, d], device(y, core, zz, x))
        )
        copies.append(
            remote(
                mid.at[j, 1, :, xx],
                dst.at[j, 1, :, x],
                send.at[j, 3 + d],
                recv.at[j, 3 + d],
                device(y, core, z, xx),
            )
        )
    copies.append(pltpu.make_async_copy(mid.at[j, 0, :, z], dst.at[j, 0, z], own.at[j, 0]))
    copies.append(pltpu.make_async_copy(mid.at[j, 1, :, x], dst.at[j, 1, :, x], own.at[j, 1]))
    return copies


def pipeline(stages):
    depth = len(stages)

    def turn(t, carry):
        for at in range(depth - 1, -1, -1):
            j = t - at

            @pl.when((j >= 0) & (j < CHUNKS))
            def _(at=at, j=j):
                stages[at](j)

        return carry

    lax.fori_loop(0, CHUNKS + depth - 1, turn, 0)


def start_all(copies):
    for copy in copies:
        copy.start()


def wait_all(copies):
    for copy in copies:
        copy.wait()


def dispatch_kernel(
    mixed_hbm, wo_hbm, stream_hbm, gm_ref, x_out, hown_ref,
    mixed, wo, p_own, p_sib, r_core, rs_buf, hbuf, gs, t1, sx,
    in_sem, wo_sem, st_sem, c1_s, c1_r, rs_s, rs_r, ag_s, ag_r, c2_s, c2_r, p1_s, p1_r, p2_s, p2_r, o1, o2,
):
    spot = place()
    y, core, z, x = spot
    sibling = device(y, 1 - core, z, x)

    def columns(half, j):
        return pl.ds(pl.multiple_of(half * HALF + j * CW, 128), CW)

    def wo_copy(j, side):
        half = core if side == 0 else 1 - core
        return pltpu.make_async_copy(wo_hbm.at[:, columns(half, j)], wo.at[j, side], wo_sem.at[j, side])

    def half_of(which):
        return pl.ds(pl.multiple_of(which * HALF, 128), HALF)

    mixed_copy = pltpu.make_async_copy(mixed_hbm, mixed, in_sem.at[0])
    stream_copy = pltpu.make_async_copy(stream_hbm.at[:, half_of(core)], sx.at[core], in_sem.at[1])
    mixed_copy.start()
    stream_copy.start()
    for j in range(CHUNKS):
        for side in range(2):
            wo_copy(j, side).start()
    greet(exp_targets(y, core, z, x))
    stream_send = remote(
        stream_hbm.at[:, half_of(1 - core)], sx.at[core], st_sem.at[0], st_sem.at[1], sibling
    )
    stream_send.start()
    mixed_copy.wait()
    stream_copy.wait()

    def core_sum(j):
        return remote(p_sib.at[j], r_core.at[j], c1_s.at[j], c1_r.at[j], sibling)

    def rows_of(which):
        return pl.ds(pl.multiple_of(which * CHIP, CHIP), CHIP)

    def scatter(j):
        return [
            remote(
                p_own.at[j, rows_of(step(y, d))],
                rs_buf.at[j, d - 1],
                rs_s.at[j, d],
                rs_r.at[j, d],
                device(step(y, d), core, z, x),
            )
            for d in (1, 3, 2)
        ]

    def spread(j):
        return [
            remote(
                hbuf.at[j, core, rows_of(y)],
                hbuf.at[j, core, rows_of(y)],
                ag_s.at[j, d],
                ag_r.at[j, d],
                device(step(y, d), core, z, x),
            )
            for d in (1, 3, 2)
        ]

    def core_share(j):
        return remote(hbuf.at[j, core], hbuf.at[j, core], c2_s.at[j], c2_r.at[j], sibling)

    def one(j):
        return first_phase(j, spot, gs, t1, p1_s, p1_r, o1)

    def two(j):
        return second_phase(j, spot, t1, x_out, p2_s, p2_r, o2)

    def project(j):
        for side in range(2):
            wo_copy(j, side).wait()

        def block(b, carry):
            rows = rows_of(b)
            left = mixed[rows, :]
            p_sib[j, rows] = jnp.dot(left, wo[j, 1], preferred_element_type=F32).astype(BF)
            p_own[j, rows] = jnp.dot(left, wo[j, 0], preferred_element_type=F32).astype(BF)
            return carry

        lax.fori_loop(0, RING, block, 0)
        core_sum(j).start()

    def add_core(j):
        core_sum(j).wait()
        p_own[j] = (p_own[j].astype(F32) + r_core[j].astype(F32)).astype(BF)
        start_all(scatter(j))

    def finish_hidden(j):
        wait_all(scatter(j))
        total = p_own[j, rows_of(y)].astype(F32)
        for i in range(3):
            total += rs_buf[j, i].astype(F32)
        stream = sx[:, :, pl.ds(pl.multiple_of(j * CW, 128), CW)].reshape(CHIP, CW)
        hidden = (stream.astype(F32) + total).astype(BF)
        hbuf[j, core, rows_of(y)] = hidden
        hown_ref[j] = hidden
        start_all(spread(j))

    def share(j):
        wait_all(spread(j))
        core_share(j).start()

    def pick(j):
        core_share(j).wait()

        def block(b, carry):
            left = gm_ref[pl.ds(pl.multiple_of(b * 288, 16), 288), :]
            for half in range(2):
                picked = jnp.dot(left, hbuf[j, half], preferred_element_type=F32)
                gs[j, half, b] = picked.reshape(RING, ROWS, CW).astype(BF)
            return carry

        lax.fori_loop(0, RING, block, 0)
        start_all(one(j))

    def forward(j):
        wait_all(one(j))
        start_all(two(j))

    def drain(j, carry):
        wait_all(two(j))
        return carry

    stream_send.wait()
    pipeline([project, add_core, finish_hidden, share, pick, forward])
    lax.fori_loop(0, CHUNKS, drain, 0)


def dispatch_call(mixed, w_o, stream, gm):
    grid_rows = (CHUNKS, 2, RING, RING, ROWS, CW)
    return pl.pallas_call(
        dispatch_kernel,
        out_shape=(jax.ShapeDtypeStruct(grid_rows, BF), jax.ShapeDtypeStruct((CHUNKS, CHIP, CW), BF)),
        in_specs=[ANY, ANY, ANY, VM],
        out_specs=(ANY, VM),
        scratch_shapes=[
            pltpu.VMEM((LEN, 1024), BF),
            pltpu.VMEM((CHUNKS, 2, 1024, CW), BF),
            pltpu.VMEM((CHUNKS, LEN, CW), BF),
            pltpu.VMEM((CHUNKS, LEN, CW), BF),
            pltpu.VMEM((CHUNKS, LEN, CW), BF),
            pltpu.VMEM((CHUNKS, 3, CHIP, CW), BF),
            pltpu.VMEM((CHUNKS, 2, LEN, CW), BF),
            pltpu.VMEM(grid_rows, BF),
            pltpu.VMEM(grid_rows, BF),
            pltpu.VMEM((2, TOK, HALF), BF),
            DMA((2,)),
            DMA((CHUNKS, 2)),
            DMA((2,)),
            DMA((CHUNKS,)),
            DMA((CHUNKS,)),
            DMA((CHUNKS, 4)),
            DMA((CHUNKS, 4)),
            DMA((CHUNKS, 4)),
            DMA((CHUNKS, 4)),
            DMA((CHUNKS,)),
            DMA((CHUNKS,)),
            DMA((CHUNKS, 7)),
            DMA((CHUNKS, 7)),
            DMA((CHUNKS, 7)),
            DMA((CHUNKS, 7)),
            DMA((CHUNKS, 2)),
            DMA((CHUNKS, 2)),
        ],
        compiler_params=pltpu.CompilerParams(
            collective_id=2, has_side_effects=True, vmem_limit_bytes=60 * 2**20
        ),
        name="dispatch",
    )(mixed, w_o, stream, gm)


def expert_kernel(
    x_hbm, wg_hbm, wu_hbm, wd_hbm, gain_ref, wc_hbm, hown_ref, out_ref,
    xbuf, wg, wu, wd, act, t1, back, wc, p_own, p_sib, r_core, rs_buf, swap,
    in_sem, w_sem, c1_s, c1_r, rs_s, rs_r, sw_s, sw_r, p1_s, p1_r, p2_s, p2_r, o1, o2,
):
    spot = place()
    y, core, z, x = spot
    sibling = device(y, 1 - core, z, x)
    loads = [
        pltpu.make_async_copy(x_hbm, xbuf, in_sem.at[0]),
        pltpu.make_async_copy(wg_hbm, wg, w_sem.at[0]),
        pltpu.make_async_copy(wu_hbm, wu, w_sem.at[1]),
    ]
    later = [
        pltpu.make_async_copy(wd_hbm, wd, w_sem.at[2]),
        pltpu.make_async_copy(wc_hbm, wc, in_sem.at[1]),
    ]
    start_all(loads)
    start_all(later)
    greet(exp_targets(y, core, z, x))
    wait_all(loads)

    def rows_of(which):
        return pl.ds(pl.multiple_of(which * CHIP, CHIP), CHIP)

    def hidden_units(b, carry):
        squares = jnp.zeros((288, 1), F32)
        for j in range(CHUNKS):
            for half in range(2):
                part = xbuf[j, half, b].astype(F32).reshape(288, CW)
                squares += jnp.sum(part * part, axis=1, keepdims=True)
        scale = lax.rsqrt(squares * (1.0 / D) + 1e-06)
        gate = jnp.zeros((288, FF), F32)
        up = jnp.zeros((288, FF), F32)
        for half in range(2):
            parts = []
            for j in range(CHUNKS):
                at = half * HALF + j * CW
                part = xbuf[j, half, b].astype(F32).reshape(288, CW)
                parts.append((part * scale * gain_ref[:, at : at + CW]).astype(BF))
            left = jnp.concatenate(parts, axis=1)
            gate += jnp.dot(left, wg[half * HALF : (half + 1) * HALF], preferred_element_type=F32)
            up += jnp.dot(left, wu[half * HALF : (half + 1) * HALF], preferred_element_type=F32)
        act[pl.ds(pl.multiple_of(b * 288, 16), 288), :] = (gate / (1.0 + jnp.exp(-gate)) * up).astype(BF)
        return carry

    lax.fori_loop(0, RING, hidden_units, 0)
    wait_all(later)

    def one(j):
        return first_phase(j, spot, xbuf, t1, p1_s, p1_r, o1)

    def two(j):
        return second_phase(j, spot, t1, back, p2_s, p2_r, o2)

    def core_sum(j):
        return remote(p_sib.at[j], r_core.at[j], c1_s.at[j], c1_r.at[j], sibling)

    def scatter(j):
        return [
            remote(
                p_own.at[j, rows_of(step(y, d))],
                rs_buf.at[j, d - 1],
                rs_s.at[j, d],
                rs_r.at[j, d],
                device(step(y, d), core, z, x),
            )
            for d in (1, 3, 2)
        ]

    def exchange(j):
        return remote(swap.at[j, 1], swap.at[j, 2], sw_s.at[j], sw_r.at[j], sibling)

    def columns(half, j):
        return pl.ds(pl.multiple_of(half * HALF + j * CW, 128), CW)

    def down(j):
        def block(b, carry):
            left = act[pl.ds(pl.multiple_of(b * 288, 16), 288), :]
            for half in range(2):
                result = jnp.dot(left, wd[:, columns(half, j)], preferred_element_type=F32)
                xbuf[j, half, b] = result.reshape(RING, ROWS, CW).astype(BF)
            return carry

        lax.fori_loop(0, RING, block, 0)
        start_all(one(j))

    def forward(j):
        wait_all(one(j))
        start_all(two(j))

    def combine(j):
        wait_all(two(j))
        own = back[j, core].reshape(1152, CW)
        other = back[j, 1 - core].reshape(1152, CW)

        def block(b, carry):
            rows = rows_of(b)
            left = wc[rows, :]
            p_sib[j, rows] = jnp.dot(left, other, preferred_element_type=F32).astype(BF)
            p_own[j, rows] = jnp.dot(left, own, preferred_element_type=F32).astype(BF)
            return carry

        lax.fori_loop(0, RING, block, 0)
        core_sum(j).start()

    def add_core(j):
        core_sum(j).wait()
        p_own[j] = (p_own[j].astype(F32) + r_core[j].astype(F32)).astype(BF)
        start_all(scatter(j))

    def finish(j):
        wait_all(scatter(j))
        total = p_own[j, rows_of(y)].astype(F32)
        for i in range(3):
            total += rs_buf[j, i].astype(F32)
        total = (hown_ref[j].astype(F32) + total).astype(BF)
        mine = jnp.where(core == 0, total[:TOK], total[TOK:])
        theirs = jnp.where(core == 0, total[TOK:], total[:TOK])
        swap[j, 1] = theirs
        exchange(j).start()
        out_ref[:, columns(core, j)] = mine

    def land(j):
        exchange(j).wait()
        out_ref[:, columns(1 - core, j)] = swap[j, 2]

    pipeline([down, forward, combine, add_core, finish, land])


def expert_call(x, w_gate, w_up, w_down, gain, wc, hown):
    grid_rows = (CHUNKS, 2, RING, RING, ROWS, CW)
    return pl.pallas_call(
        expert_kernel,
        out_shape=jax.ShapeDtypeStruct((TOK, D), BF),
        in_specs=[ANY, ANY, ANY, ANY, VM, ANY, VM],
        out_specs=VM,
        scratch_shapes=[
            pltpu.VMEM(grid_rows, BF),
            pltpu.VMEM((D, FF), BF),
            pltpu.VMEM((D, FF), BF),
            pltpu.VMEM((FF, D), BF),
            pltpu.VMEM((1152, FF), BF),
            pltpu.VMEM(grid_rows, BF),
            pltpu.VMEM(grid_rows, BF),
            pltpu.VMEM((LEN, 1152), BF),
            pltpu.VMEM((CHUNKS, LEN, CW), BF),
            pltpu.VMEM((CHUNKS, LEN, CW), BF),
            pltpu.VMEM((CHUNKS, LEN, CW), BF),
            pltpu.VMEM((CHUNKS, 3, CHIP, CW), BF),
            pltpu.VMEM((CHUNKS, 3, TOK, CW), BF),
            DMA((2,)),
            DMA((3,)),
            DMA((CHUNKS,)),
            DMA((CHUNKS,)),
            DMA((CHUNKS, 4)),
            DMA((CHUNKS, 4)),
            DMA((CHUNKS,)),
            DMA((CHUNKS,)),
            DMA((CHUNKS, 7)),
            DMA((CHUNKS, 7)),
            DMA((CHUNKS, 7)),
            DMA((CHUNKS, 7)),
            DMA((CHUNKS, 2)),
            DMA((CHUNKS, 2)),
        ],
        compiler_params=pltpu.CompilerParams(
            collective_id=3, has_side_effects=True, vmem_limit_bytes=62 * 2**20
        ),
        name="experts",
    )(x, w_gate, w_up, w_down, gain, wc, hown)


def routing(expert_ids, gate_weights):
    ids = lax.all_gather(expert_ids, "ctx", axis=0, tiled=True)
    gates = lax.all_gather(gate_weights, "ctx", axis=0, tiled=True)
    first = lax.axis_index("ctx") * 16
    hit = ids[:, :, None] == (first + jnp.arange(16))[None, None, :]
    named = jnp.any(hit, axis=1)
    gate = jnp.sum(jnp.where(hit, gates[:, :, None], 0.0), axis=1)
    blocks = named.astype(BF).reshape(8, TOK, 16)
    earlier = (jnp.arange(TOK)[:, None] > jnp.arange(TOK)[None, :]).astype(BF)
    slot = jnp.einsum("ij,bje->bie", earlier, blocks, preferred_element_type=F32)
    spot = jnp.arange(8, dtype=F32)[:, None, None] * CAP + slot
    spot = jnp.where(named, spot.reshape(LEN, 16), -1.0)
    rows = jnp.arange(ROWS, dtype=F32)
    gm = (spot.T[:, None, :] == rows[None, :, None]).astype(BF).reshape(1152, LEN)
    widen = (jnp.arange(16)[:, None] == (jnp.arange(1152) // ROWS)[None, :]).astype(BF)
    wide = jnp.dot(spot.astype(BF), widen, preferred_element_type=F32)
    gate_wide = jnp.dot(gate.astype(BF), widen, preferred_element_type=F32)
    at = (jnp.arange(1152) % ROWS).astype(F32)
    wc = jnp.where(wide == at[None, :], gate_wide, 0.0).astype(BF)
    return gm, wc


def local(
    stream_in,
    queries,
    latents,
    key_rope,
    w_uk,
    w_uv,
    w_o,
    norm_gain,
    expert_ids,
    gate_weights,
    w_gate,
    w_up,
    w_down,
):
    gm, wc = routing(expert_ids[0], gate_weights[0])
    latrope = jnp.concatenate([latents[0], key_rope[0], jnp.zeros((TOK, 64), BF)], axis=1)
    mixed = attention_call(queries[0], latrope, w_uk, w_uv)
    arrived, hown = dispatch_call(mixed, w_o, stream_in[0], gm)
    out = expert_call(arrived, w_gate[0], w_up[0], w_down[0], norm_gain[None, :], wc, hown)
    return out[None]


def solution(mesh):
    return jax.shard_map(
        local,
        mesh=mesh,
        in_specs=(
            P("exp", "ctx", None),
            P("exp", "ctx", None),
            P("exp", "ctx", None),
            P("exp", "ctx", None),
            P(None, "ctx"),
            P(None, "ctx"),
            P("ctx", None),
            P(),
            P("exp", "ctx", None),
            P("exp", "ctx", None),
            P(("ctx", "exp"), None, None),
            P(("ctx", "exp"), None, None),
            P(("ctx", "exp"), None, None),
        ),
        out_specs=P("exp", "ctx", None),
        check_vma=False,
    )
```

```python
import functools
import math

import jax
import jax.numpy as jnp
from jax import lax
from jax.experimental import pallas as pl
from jax.experimental.pallas import tpu as pltpu
from jax.sharding import PartitionSpec as P

NOPE = 128
ROPE = 64
VDIM = 128
KVL = 512
D = 2560
FF = 768
TOPK = 6
CAP = 9
TOK = 128
LEN = 1024
QW = 1536
RING = 4
ROWS = 72
CHUNKS = 10
CW = 128
HALF = 1280
CHIP = 256
LATW = 640
MESH = pl.DeviceIdType.MESH
BF = jnp.bfloat16
F32 = jnp.float32
ANY = pl.BlockSpec(memory_space=pl.ANY)
VM = pl.BlockSpec(memory_space=pltpu.VMEM)
DMA = pltpu.SemaphoreType.DMA


def place():
    c = lax.axis_index("ctx")
    e = lax.axis_index("exp")
    return c // 2, c % 2, e // RING, e % RING


def device(y, core, z, x):
    return (y * 2 + core, z * RING + x)


def step(v, d):
    return lax.rem(v + d, RING)


def remote(src, dst, send, recv, target):
    return pltpu.make_async_remote_copy(
        src_ref=src, dst_ref=dst, send_sem=send, recv_sem=recv, device_id=target, device_id_type=MESH
    )


def greet(targets):
    barrier = pltpu.get_barrier_semaphore()
    for target in targets:
        pl.semaphore_signal(barrier, inc=1, device_id=target, device_id_type=MESH)
    pl.semaphore_wait(barrier, len(targets))


def attention_kernel(
    q_hbm, lat_hbm, uk_ref, uv_ref, out_ref, route_ref,
    qbuf, lat, kbuf, vbuf, q_send, q_recv, l_send, l_recv, own_sem,
):
    y, core, z, x = place()
    me = y * 2 + core
    peers = [(dy, dc) for dy in (0, 1, 3, 2) for dc in (0, 1) if (dy, dc) != (0, 0)]
    greet([device(step(y, dy), lax.rem(core + dc, 2), z, x) for dy, dc in peers])

    def lat_copy(dy):
        return remote(lat_hbm, lat.at[me], l_send.at[dy], l_recv.at[dy], device(step(y, dy), core, z, x))

    def lat_share(dy):
        block = lat.at[step(y, dy) * 2 + core]
        return remote(block, block, l_send.at[4 + dy], l_recv.at[4 + dy], device(y, 1 - core, z, x))

    def q_copy(dy, dc):
        i = dy * 2 + dc
        yy, cc = step(y, dy), lax.rem(core + dc, 2)
        columns = pl.ds(pl.multiple_of((yy * 2 + cc) * QW, 128), QW)
        return remote(q_hbm.at[:, columns], qbuf.at[me], q_send.at[i], q_recv.at[i], device(yy, cc, z, x))

    own_lat = pltpu.make_async_copy(lat_hbm, lat.at[me], own_sem.at[0])
    own_q = pltpu.make_async_copy(
        q_hbm.at[:, pl.ds(pl.multiple_of(me * QW, 128), QW)], qbuf.at[me], own_sem.at[1]
    )
    own_lat.start()
    own_q.start()
    for dy in (1, 3, 2):
        lat_copy(dy).start()
    for dy, dc in peers:
        q_copy(dy, dc).start()
    own_lat.wait()
    lat_share(0).start()
    for dy in (1, 3, 2):
        lat_copy(4 - dy).wait_recv()
        lat_share(dy).start()
    for dy in (0, 1, 3, 2):
        lat_share(dy).wait()
    for dy in (1, 3, 2):
        lat_copy(dy).wait_send()
    own_q.wait()

    lane = lax.broadcasted_iota(jnp.int32, (CHIP, 128), 1)

    def project(b, carry):
        rows = pl.ds(pl.multiple_of(b * CHIP, CHIP), CHIP)
        block = lat[pl.ds(b * 2, 2)].reshape(CHIP, LATW)
        latent = block[:, :KVL]
        route_ref[rows, :] = block[:, KVL:]
        rope = block[:, KVL:].astype(F32)
        rope_low = jnp.where(lane < 64, rope, 0.0).astype(BF)
        rope_high = pltpu.roll(rope, 64, 1)
        for h in range(8):
            nope = jnp.dot(latent, uk_ref[:, h * 128 : h * 128 + 128], preferred_element_type=F32)
            if h % 2 == 0:
                kbuf[h, rows, 0:128] = nope.astype(BF)
                kbuf[h, rows, 128:256] = rope_low
            else:
                turned = pltpu.roll(nope, 64, 1)
                kbuf[h, rows, 0:128] = jnp.where(lane < 64, 0.0, turned).astype(BF)
                kbuf[h, rows, 128:256] = jnp.where(lane < 64, turned, rope_high).astype(BF)
        vbuf[rows, :] = jnp.dot(latent, uv_ref[...], preferred_element_type=F32).astype(BF)
        return carry

    lax.fori_loop(0, RING, project, 0)

    factor = 1.0 / math.sqrt(NOPE + ROPE) * math.log2(math.e)
    row_at = lax.broadcasted_iota(jnp.int32, (CHIP, CHIP), 0)
    col_at = lax.broadcasted_iota(jnp.int32, (CHIP, CHIP), 1)
    causal = row_at >= col_at

    def attend(block):
        length = (block + 1) * CHIP

        def pair(p, carry):
            columns = pl.ds(pl.multiple_of(p * 384, 128), 384)
            q = qbuf[block * 2 : block * 2 + 2, :, columns].reshape(CHIP, 384)
            outs = []
            for odd in range(2):
                query = q[:, odd * 128 : odd * 128 + 256]
                head = p * 2 + odd
                contract = (((1,), (1,)), ((), ()))
                last = lax.dot_general(
                    query, kbuf[head, length - CHIP : length], contract, preferred_element_type=F32
                )
                last = jnp.where(causal, last, -jnp.inf)
                peak = jnp.max(last, axis=1, keepdims=True)
                if block:
                    first = lax.dot_general(
                        query, kbuf[head, 0 : length - CHIP], contract, preferred_element_type=F32
                    )
                    peak = jnp.maximum(peak, jnp.max(first, axis=1, keepdims=True))
                values = pl.ds(pl.multiple_of(head * 128, 128), 128)
                weight = jnp.exp2((last - peak) * factor)
                total = jnp.sum(weight, axis=1, keepdims=True)
                result = jnp.dot(
                    weight.astype(BF), vbuf[length - CHIP : length, values], preferred_element_type=F32
                )
                if block:
                    weight = jnp.exp2((first - peak) * factor)
                    total += jnp.sum(weight, axis=1, keepdims=True)
                    result += jnp.dot(
                        weight.astype(BF), vbuf[0 : length - CHIP, values], preferred_element_type=F32
                    )
                outs.append((result / total).astype(BF))
            out_ref[block * CHIP : (block + 1) * CHIP, pl.ds(pl.multiple_of(p * 256, 256), 256)] = (
                jnp.concatenate(outs, axis=1)
            )
            return carry

        lax.fori_loop(0, 4, pair, 0)

    for dy in (0, 1, 3, 2):
        for dc in range(2):
            if (dy, dc) != (0, 0):
                q_copy((4 - dy) % 4, dc).wait_recv()
        source = lax.rem(y + dy, RING)
        for block in range(RING):
            pl.when(source == block)(functools.partial(attend, block))
    for dy, dc in peers:
        q_copy(dy, dc).wait_send()


def attention_call(queries, latrope, w_uk, w_uv):
    return pl.pallas_call(
        attention_kernel,
        out_shape=(jax.ShapeDtypeStruct((LEN, 1024), BF), jax.ShapeDtypeStruct((LEN, 128), BF)),
        in_specs=[ANY, ANY, VM, VM],
        out_specs=(VM, VM),
        scratch_shapes=[
            pltpu.VMEM((8, TOK, QW), BF),
            pltpu.VMEM((8, TOK, LATW), BF),
            pltpu.VMEM((8, LEN, 256), BF),
            pltpu.VMEM((LEN, 1024), BF),
            DMA((8,)),
            DMA((8,)),
            DMA((8,)),
            DMA((8,)),
            DMA((2,)),
        ],
        compiler_params=pltpu.CompilerParams(
            collective_id=1, has_side_effects=True, vmem_limit_bytes=48 * 2**20
        ),
        name="attention",
    )(queries, latrope, w_uk, w_uv)


def exp_targets(y, core, z, x):
    found = [device(y, 1 - core, z, x)]
    for d in (1, 2, 3):
        found.append(device(step(y, d), core, z, x))
        found.append(device(y, core, step(z, d), x))
        found.append(device(y, core, z, step(x, d)))
    return found


def first_phase(j, spot, src, mid, send, recv, own):
    y, core, z, x = spot
    copies = []
    for d in (1, 3, 2):
        xx, zz = step(x, d), step(z, d)
        copies.append(
            remote(src.at[j, 0, :, xx], mid.at[j, 0, x], send.at[j, d], recv.at[j, d], device(y, core, z, xx))
        )
        copies.append(
            remote(
                src.at[j, 1, zz], mid.at[j, 1, z], send.at[j, 3 + d], recv.at[j, 3 + d], device(y, core, zz, x)
            )
        )
    copies.append(pltpu.make_async_copy(src.at[j, 0, :, x], mid.at[j, 0, x], own.at[j, 0]))
    copies.append(pltpu.make_async_copy(src.at[j, 1, z], mid.at[j, 1, z], own.at[j, 1]))
    return copies


def second_phase(j, spot, mid, dst, send, recv, own):
    y, core, z, x = spot
    copies = []
    for d in (1, 3, 2):
        xx, zz = step(x, d), step(z, d)
        copies.append(
            remote(mid.at[j, 0, :, zz], dst.at[j, 0, z], send.at[j, d], recv.at[j, d], device(y, core, zz, x))
        )
        copies.append(
            remote(
                mid.at[j, 1, :, xx],
                dst.at[j, 1, :, x],
                send.at[j, 3 + d],
                recv.at[j, 3 + d],
                device(y, core, z, xx),
            )
        )
    copies.append(pltpu.make_async_copy(mid.at[j, 0, :, z], dst.at[j, 0, z], own.at[j, 0]))
    copies.append(pltpu.make_async_copy(mid.at[j, 1, :, x], dst.at[j, 1, :, x], own.at[j, 1]))
    return copies


def pipeline(stages):
    def turn(t, carry):
        for lag, stage in reversed(stages):
            j = t - lag

            @pl.when((j >= 0) & (j < CHUNKS))
            def _(stage=stage, j=j):
                stage(j)

        return carry

    lax.fori_loop(0, CHUNKS + stages[-1][0], turn, 0)


def start_all(copies):
    for copy in copies:
        copy.start()


def wait_all(copies):
    for copy in copies:
        copy.wait()


def moe_kernel(
    mixed_hbm, wo_hbm, stream_hbm, route_ref, wg_hbm, wu_hbm, wd_hbm, gain_ref, out_ref,
    mixed, late, p_own, p_sib, r_core, rs_buf, hbuf, gs, t1, xbuf, pickers, wg, wu, wd, sx, hown, swap, spots,
    in_sem, wo_sem, w_sem, st_sem, c1_s, c1_r, rs_s, rs_r, ag_s, ag_r, c2_s, c2_r, p1_s, p1_r, p2_s, p2_r,
    d1_s, d1_r, d2_s, d2_r, c3_s, c3_r, fs_s, fs_r, sw_s, sw_r, o1, o2, o3, o4,
):
    spot = place()
    y, core, z, x = spot
    sibling = device(y, 1 - core, z, x)

    def columns(half, j):
        return pl.ds(pl.multiple_of(half * HALF + j * CW, 128), CW)

    def wo_copy(j, side):
        half = core if side == 0 else 1 - core
        return pltpu.make_async_copy(
            wo_hbm.at[:, :, :, columns(half, j)], late.at[j, side, :, :, 0:64], wo_sem.at[j, side]
        )

    def half_of(which):
        return pl.ds(pl.multiple_of(which * HALF, 128), HALF)

    mixed_copy = pltpu.make_async_copy(mixed_hbm, mixed.at[0:LEN], in_sem.at[0])
    stream_copy = pltpu.make_async_copy(stream_hbm.at[:, half_of(core)], sx.at[core], in_sem.at[1])
    weights = [
        pltpu.make_async_copy(wg_hbm, wg, w_sem.at[0]),
        pltpu.make_async_copy(wu_hbm, wu, w_sem.at[1]),
        pltpu.make_async_copy(wd_hbm, wd, w_sem.at[2]),
    ]
    mixed_copy.start()
    stream_copy.start()

    def load_wo(j, carry):
        for side in range(2):
            wo_copy(j, side).start()
        return carry

    lax.fori_loop(0, CHUNKS, load_wo, 0)
    start_all(weights)
    greet(exp_targets(y, core, z, x))
    stream_send = remote(
        stream_hbm.at[:, half_of(1 - core)], sx.at[core], st_sem.at[0], st_sem.at[1], sibling
    )
    stream_send.start()
    mixed_copy.wait()
    stream_copy.wait()

    def rows_of(which):
        return pl.ds(pl.multiple_of(which * CHIP, CHIP), CHIP)

    def core_sum(j, send, recv):
        return remote(p_sib.at[j], r_core.at[j], send.at[j], recv.at[j], sibling)

    def scatter(j, send, recv):
        return [
            remote(
                p_own.at[j, rows_of(step(y, d))],
                rs_buf.at[j, d - 1],
                send.at[j, d],
                recv.at[j, d],
                device(step(y, d), core, z, x),
            )
            for d in (1, 3, 2)
        ]

    def spread(j):
        block = hbuf.at[j, core, y, :, 0:64]
        return [
            remote(block, block, ag_s.at[j, d], ag_r.at[j, d], device(step(y, d), core, z, x))
            for d in (1, 3, 2)
        ]

    def core_share(j):
        block = hbuf.at[j, core, :, :, 0:64]
        return remote(block, block, c2_s.at[j], c2_r.at[j], sibling)

    def gather_row():
        row = lax.broadcasted_iota(jnp.int32, (1152, 128), 0)
        low = lax.broadcasted_iota(jnp.int32, (1152, 128), 1) * ROWS
        inside = (row >= low) & (row < low + ROWS)
        member = jnp.where(inside, 1.0, 0.0).astype(BF)
        at = jnp.sum(jnp.where(inside, row - low, 0).astype(F32), axis=1, keepdims=True)
        return member, at

    def route_spots():
        lane = lax.broadcasted_iota(jnp.int32, (TOK, 128), 1)
        first = ((y * 2 + core) * 16).astype(F32)
        wanted = jnp.where(lane < 16, lane.astype(F32) + first, -1.0)
        earlier = lax.broadcasted_iota(jnp.int32, (TOK, 128), 0) > lane
        earlier = jnp.where(earlier, 1.0, 0.0).astype(BF)
        for b in range(8):
            rows = slice(b * TOK, (b + 1) * TOK)
            route = route_ref[rows, :].astype(F32)
            named = jnp.zeros((TOK, 128), F32)
            gate = jnp.zeros((TOK, 128), F32)
            for k in range(TOPK):
                hit = route[:, 64 + k : 65 + k] == wanted
                named = jnp.where(hit, 1.0, named)
                gate = jnp.where(hit, route[:, 64 + TOPK + k : 65 + TOPK + k], gate)
            slot = jnp.dot(earlier, named.astype(BF), preferred_element_type=F32)
            spots[0, rows, :] = jnp.where(named > 0.0, slot + (b * CAP), -1.0).astype(BF)
            spots[1, rows, :] = gate.astype(BF)

    def pickers_in():
        member, at = gather_row()
        for b in range(RING):
            rows = slice(b * 288, (b + 1) * 288)
            wide = lax.dot_general(
                member[rows], spots[0], (((1,), (1,)), ((), ())), preferred_element_type=F32
            )
            pickers[rows, 0:LEN] = jnp.where(wide == at[rows], 1.0, 0.0).astype(BF)

    def pickers_out():
        low = lax.broadcasted_iota(jnp.int32, (128, 1152), 0) * ROWS
        row = lax.broadcasted_iota(jnp.int32, (128, 1152), 1)
        inside = (row >= low) & (row < low + ROWS)
        member = jnp.where(inside, 1.0, 0.0).astype(BF)
        at = jnp.sum(jnp.where(inside, row - low, 0).astype(F32), axis=0, keepdims=True)
        for b in range(RING):
            rows = slice(b * CHIP, (b + 1) * CHIP)
            wide = jnp.dot(spots[0, rows, :], member, preferred_element_type=F32)
            gate = jnp.dot(spots[1, rows, :], member, preferred_element_type=F32)
            pickers[rows, :] = jnp.where(wide == at, gate, 0.0).astype(BF)

    def one(j):
        return first_phase(j, spot, gs, t1, p1_s, p1_r, o1)

    def two(j):
        return second_phase(j, spot, t1, xbuf, p2_s, p2_r, o2)

    def project(j):
        for side in range(2):
            wo_copy(j, side).wait()
        own = late[j, 0, :, :, 0:64].reshape(1024, CW)
        other = late[j, 1, :, :, 0:64].reshape(1024, CW)
        both = jnp.concatenate([own, other], axis=1)

        def block(b, carry):
            rows = rows_of(b)
            product = jnp.dot(mixed[rows, :], both, preferred_element_type=F32).astype(BF)
            p_own[j, rows] = product[:, :CW]
            p_sib[j, rows] = product[:, CW:]
            return carry

        lax.fori_loop(0, RING, block, 0)
        core_sum(j, c1_s, c1_r).start()

    def add_core(j):
        core_sum(j, c1_s, c1_r).wait()
        p_own[j] = (p_own[j].astype(F32) + r_core[j].astype(F32)).astype(BF)
        start_all(scatter(j, rs_s, rs_r))

    def chip_total(j):
        total = p_own[j, rows_of(y)].astype(F32)
        for i in range(3):
            total += rs_buf[j, i].astype(F32)
        return total

    def finish_hidden(j):
        wait_all(scatter(j, rs_s, rs_r))
        stream = sx[:, :, pl.ds(pl.multiple_of(j * CW, 128), CW)].reshape(CHIP, CW)
        hidden = (stream.astype(F32) + chip_total(j)).astype(BF)
        hbuf[j, core, y, :, 0:64] = hidden.reshape(RING, 64, CW)
        hown[j] = hidden
        start_all(spread(j))

    def share(j):
        wait_all(spread(j))
        core_share(j).start()

    def pick(j):
        core_share(j).wait()
        both = jnp.concatenate(
            [hbuf[j, half, :, :, 0:64].reshape(1024, CW) for half in range(2)], axis=1
        )

        def block(b, carry):
            left = pickers[pl.ds(pl.multiple_of(b * 288, 16), 288), 0:LEN]
            picked = jnp.dot(left, both, preferred_element_type=F32).reshape(RING, ROWS, 2 * CW)
            gs[j, 0, b] = picked[:, :, :CW].astype(BF)
            gs[j, 1, b] = picked[:, :, CW:].astype(BF)
            return carry

        lax.fori_loop(0, RING, block, 0)
        start_all(one(j))

    def forward(j):
        wait_all(one(j))
        start_all(two(j))

    def drain(j):
        wait_all(two(j))

    def prepare(j):
        pl.when(j == 0)(route_spots)
        pl.when(j == 1)(pickers_in)

    stream_send.wait()
    pipeline(
        [
            (0, project),
            (1, add_core),
            (1, prepare),
            (3, finish_hidden),
            (5, share),
            (6, pick),
            (8, forward),
            (10, drain),
        ]
    )
    wait_all(weights)

    def hidden_units(b, carry):
        squares = jnp.zeros((288, 1), F32)
        for j in range(CHUNKS):
            for half in range(2):
                part = xbuf[j, half, b].astype(F32).reshape(288, CW)
                squares += jnp.sum(part * part, axis=1, keepdims=True)
        scale = lax.rsqrt(squares * (1.0 / D) + 1e-06)
        gate = jnp.zeros((288, FF), F32)
        up = jnp.zeros((288, FF), F32)
        for half in range(2):
            parts = []
            for j in range(CHUNKS):
                at = half * HALF + j * CW
                part = xbuf[j, half, b].astype(F32).reshape(288, CW)
                parts.append((part * scale * gain_ref[:, at : at + CW]).astype(BF))
            left = jnp.concatenate(parts, axis=1)
            gate += jnp.dot(left, wg[half * HALF : (half + 1) * HALF], preferred_element_type=F32)
            up += jnp.dot(left, wu[half * HALF : (half + 1) * HALF], preferred_element_type=F32)
        mixed[pl.ds(pl.multiple_of(b * 288, 16), 288), 0:FF] = (
            gate / (1.0 + jnp.exp(-gate)) * up
        ).astype(BF)
        return carry

    lax.fori_loop(0, RING, hidden_units, 0)

    def back_one(j):
        return first_phase(j, spot, gs, late, d1_s, d1_r, o3)

    def back_two(j):
        return second_phase(j, spot, late, hbuf, d2_s, d2_r, o4)

    def exchange(j):
        return remote(swap.at[j, 0], swap.at[j, 1], sw_s.at[j], sw_r.at[j], sibling)

    def down(j):
        both = jnp.concatenate([wd[:, columns(half, j)] for half in range(2)], axis=1)

        def block(b, carry):
            left = mixed[pl.ds(pl.multiple_of(b * 288, 16), 288), 0:FF]
            result = jnp.dot(left, both, preferred_element_type=F32).reshape(RING, ROWS, 2 * CW)
            gs[j, 0, b] = result[:, :, :CW].astype(BF)
            gs[j, 1, b] = result[:, :, CW:].astype(BF)
            return carry

        lax.fori_loop(0, RING, block, 0)
        start_all(back_one(j))

    def back_forward(j):
        wait_all(back_one(j))
        start_all(back_two(j))

    def combine(j):
        wait_all(back_two(j))
        both = jnp.concatenate(
            [
                hbuf[j, core].astype(F32).reshape(1152, CW).astype(BF),
                hbuf[j, 1 - core].astype(F32).reshape(1152, CW).astype(BF),
            ],
            axis=1,
        )

        def block(b, carry):
            rows = rows_of(b)
            product = jnp.dot(pickers[rows, :], both, preferred_element_type=F32).astype(BF)
            p_own[j, rows] = product[:, :CW]
            p_sib[j, rows] = product[:, CW:]
            return carry

        lax.fori_loop(0, RING, block, 0)
        core_sum(j, c3_s, c3_r).start()

    def add_back(j):
        core_sum(j, c3_s, c3_r).wait()
        p_own[j] = (p_own[j].astype(F32) + r_core[j].astype(F32)).astype(BF)
        start_all(scatter(j, fs_s, fs_r))

    def finish(j):
        wait_all(scatter(j, fs_s, fs_r))
        total = (hown[j].astype(F32) + chip_total(j)).astype(BF)
        swap[j, 0] = jnp.where(core == 0, total[TOK:], total[:TOK])
        exchange(j).start()
        out_ref[:, columns(core, j)] = jnp.where(core == 0, total[:TOK], total[TOK:])

    def land(j):
        exchange(j).wait()
        out_ref[:, columns(1 - core, j)] = swap[j, 1]

    def prepare_back(j):
        pl.when(j == 0)(pickers_out)

    pipeline(
        [
            (0, down),
            (1, prepare_back),
            (2, back_forward),
            (4, combine),
            (5, add_back),
            (7, finish),
            (8, land),
        ]
    )


def moe_call(mixed, w_o, stream, route, w_gate, w_up, w_down, gain):
    grid_rows = (CHUNKS, 2, RING, RING, ROWS, CW)
    one = DMA((CHUNKS,))
    ring = DMA((CHUNKS, 4))
    phase = DMA((CHUNKS, 7))
    return pl.pallas_call(
        moe_kernel,
        out_shape=jax.ShapeDtypeStruct((TOK, D), BF),
        in_specs=[ANY, ANY, ANY, VM, ANY, ANY, ANY, VM],
        out_specs=VM,
        scratch_shapes=[
            pltpu.VMEM((1152, 1024), BF),
            pltpu.VMEM(grid_rows, BF),
            pltpu.VMEM((CHUNKS, LEN, CW), BF),
            pltpu.VMEM((CHUNKS, LEN, CW), BF),
            pltpu.VMEM((CHUNKS, LEN, CW), BF),
            pltpu.VMEM((CHUNKS, 3, CHIP, CW), BF),
            pltpu.VMEM(grid_rows, BF),
            pltpu.VMEM(grid_rows, BF),
            pltpu.VMEM(grid_rows, BF),
            pltpu.VMEM(grid_rows, BF),
            pltpu.VMEM((1152, 1152), BF),
            pltpu.VMEM((D, FF), BF),
            pltpu.VMEM((D, FF), BF),
            pltpu.VMEM((FF, D), BF),
            pltpu.VMEM((2, TOK, HALF), BF),
            pltpu.VMEM((CHUNKS, CHIP, CW), BF),
            pltpu.VMEM((CHUNKS, 2, TOK, CW), BF),
            pltpu.VMEM((2, LEN, 128), BF),
            DMA((2,)),
            DMA((CHUNKS, 2)),
            DMA((3,)),
            DMA((2,)),
            *[one, one, ring, ring, ring, ring, one, one],
            *[phase] * 8,
            *[one, one, ring, ring, one, one],
            *[DMA((CHUNKS, 2))] * 4,
        ],
        compiler_params=pltpu.CompilerParams(
            collective_id=2, has_side_effects=True, vmem_limit_bytes=63 * 2**20
        ),
        name="moe",
    )(mixed, w_o, stream, route, w_gate, w_up, w_down, gain)


def local(
    stream_in,
    queries,
    latents,
    key_rope,
    w_uk,
    w_uv,
    w_o,
    norm_gain,
    expert_ids,
    gate_weights,
    w_gate,
    w_up,
    w_down,
):
    packed = jnp.concatenate(
        [latents[0], key_rope[0], expert_ids[0].astype(BF), gate_weights[0].astype(BF), jnp.zeros((TOK, 52), BF)],
        axis=1,
    )
    mixed, route = attention_call(queries[0], packed, w_uk, w_uv)
    blocks = w_o.reshape(RING, RING, 64, D)
    out = moe_call(
        mixed, blocks, stream_in[0], route, w_gate[0], w_up[0], w_down[0], norm_gain[None, :]
    )
    return out[None]


def solution(mesh):
    return jax.shard_map(
        local,
        mesh=mesh,
        in_specs=(
            P("exp", "ctx", None),
            P("exp", "ctx", None),
            P("exp", "ctx", None),
            P("exp", "ctx", None),
            P(None, "ctx"),
            P(None, "ctx"),
            P("ctx", None),
            P(),
            P("exp", "ctx", None),
            P("exp", "ctx", None),
            P(("ctx", "exp"), None, None),
            P(("ctx", "exp"), None, None),
            P(("ctx", "exp"), None, None),
        ),
        out_specs=P("exp", "ctx", None),
        check_vma=False,
    )
```

```python
import functools
import math

import jax
import jax.numpy as jnp
from jax import lax
from jax.experimental import pallas as pl
from jax.experimental.pallas import tpu as pltpu
from jax.sharding import PartitionSpec as P

NOPE = 128
ROPE = 64
VDIM = 128
KVL = 512
D = 2560
FF = 768
TOPK = 6
CAP = 9
TOK = 128
LEN = 1024
QW = 1536
RING = 4
ROWS = 72
CHUNKS = 10
CW = 128
SLOTS = 4
HALF = 1280
CHIP = 256
LATW = 640
MESH = pl.DeviceIdType.MESH
BF = jnp.bfloat16
F32 = jnp.float32
ANY = pl.BlockSpec(memory_space=pl.ANY)
VM = pl.BlockSpec(memory_space=pltpu.VMEM)
DMA = pltpu.SemaphoreType.DMA


def place():
    c = lax.axis_index("ctx")
    e = lax.axis_index("exp")
    return c // 2, c % 2, e // RING, e % RING


def device(y, core, z, x):
    return (y * 2 + core, z * RING + x)


def step(v, d):
    return lax.rem(v + d, RING)


def remote(src, dst, send, recv, target):
    return pltpu.make_async_remote_copy(
        src_ref=src, dst_ref=dst, send_sem=send, recv_sem=recv, device_id=target, device_id_type=MESH
    )


def greet(targets):
    barrier = pltpu.get_barrier_semaphore()
    for target in targets:
        pl.semaphore_signal(barrier, inc=1, device_id=target, device_id_type=MESH)
    pl.semaphore_wait(barrier, len(targets))


def attention_kernel(
    q_hbm, lat_hbm, uk_ref, uv_ref, out_ref, route_ref,
    qbuf, lat, kbuf, vbuf, q_send, q_recv, l_send, l_recv, own_sem,
):
    y, core, z, x = place()
    me = y * 2 + core
    peers = [(dy, dc) for dy in (0, 1, 3, 2) for dc in (0, 1) if (dy, dc) != (0, 0)]
    greet([device(step(y, dy), lax.rem(core + dc, 2), z, x) for dy, dc in peers])

    def lat_copy(dy):
        return remote(lat_hbm, lat.at[me], l_send.at[dy], l_recv.at[dy], device(step(y, dy), core, z, x))

    def lat_share(dy):
        block = lat.at[step(y, dy) * 2 + core]
        return remote(block, block, l_send.at[4 + dy], l_recv.at[4 + dy], device(y, 1 - core, z, x))

    def q_copy(dy, dc):
        i = dy * 2 + dc
        yy, cc = step(y, dy), lax.rem(core + dc, 2)
        columns = pl.ds(pl.multiple_of((yy * 2 + cc) * QW, 128), QW)
        return remote(q_hbm.at[:, columns], qbuf.at[me], q_send.at[i], q_recv.at[i], device(yy, cc, z, x))

    own_lat = pltpu.make_async_copy(lat_hbm, lat.at[me], own_sem.at[0])
    own_q = pltpu.make_async_copy(
        q_hbm.at[:, pl.ds(pl.multiple_of(me * QW, 128), QW)], qbuf.at[me], own_sem.at[1]
    )
    own_lat.start()
    own_q.start()
    for dy in (1, 3, 2):
        lat_copy(dy).start()
    for dy, dc in peers:
        q_copy(dy, dc).start()
    own_lat.wait()
    lat_share(0).start()
    for dy in (1, 3, 2):
        lat_copy(4 - dy).wait_recv()
        lat_share(dy).start()
    for dy in (0, 1, 3, 2):
        lat_share(dy).wait()
    for dy in (1, 3, 2):
        lat_copy(dy).wait_send()
    own_q.wait()

    lane = lax.broadcasted_iota(jnp.int32, (CHIP, 128), 1)

    def project(b, carry):
        rows = pl.ds(pl.multiple_of(b * CHIP, CHIP), CHIP)
        block = lat[pl.ds(b * 2, 2)].reshape(CHIP, LATW)
        latent = block[:, :KVL]
        route_ref[rows, :] = block[:, KVL:]
        rope = block[:, KVL:].astype(F32)
        rope_low = jnp.where(lane < 64, rope, 0.0).astype(BF)
        rope_high = pltpu.roll(rope, 64, 1)
        for h in range(8):
            nope = jnp.dot(latent, uk_ref[:, h * 128 : h * 128 + 128], preferred_element_type=F32)
            if h % 2 == 0:
                kbuf[h, rows, 0:128] = nope.astype(BF)
                kbuf[h, rows, 128:256] = rope_low
            else:
                turned = pltpu.roll(nope, 64, 1)
                kbuf[h, rows, 0:128] = jnp.where(lane < 64, 0.0, turned).astype(BF)
                kbuf[h, rows, 128:256] = jnp.where(lane < 64, turned, rope_high).astype(BF)
        vbuf[rows, :] = jnp.dot(latent, uv_ref[...], preferred_element_type=F32).astype(BF)
        return carry

    lax.fori_loop(0, RING, project, 0)

    factor = 1.0 / math.sqrt(NOPE + ROPE) * math.log2(math.e)
    row_at = lax.broadcasted_iota(jnp.int32, (CHIP, CHIP), 0)
    col_at = lax.broadcasted_iota(jnp.int32, (CHIP, CHIP), 1)
    causal = row_at >= col_at

    def attend(block):
        length = (block + 1) * CHIP

        def pair(p, carry):
            columns = pl.ds(pl.multiple_of(p * 384, 128), 384)
            q = qbuf[block * 2 : block * 2 + 2, :, columns].reshape(CHIP, 384)
            outs = []
            for odd in range(2):
                query = q[:, odd * 128 : odd * 128 + 256]
                head = p * 2 + odd
                contract = (((1,), (1,)), ((), ()))
                last = lax.dot_general(
                    query, kbuf[head, length - CHIP : length], contract, preferred_element_type=F32
                )
                last = jnp.where(causal, last, -jnp.inf)
                peak = jnp.max(last, axis=1, keepdims=True)
                if block:
                    first = lax.dot_general(
                        query, kbuf[head, 0 : length - CHIP], contract, preferred_element_type=F32
                    )
                    peak = jnp.maximum(peak, jnp.max(first, axis=1, keepdims=True))
                values = pl.ds(pl.multiple_of(head * 128, 128), 128)
                weight = jnp.exp2((last - peak) * factor)
                total = jnp.sum(weight, axis=1, keepdims=True)
                result = jnp.dot(
                    weight.astype(BF), vbuf[length - CHIP : length, values], preferred_element_type=F32
                )
                if block:
                    weight = jnp.exp2((first - peak) * factor)
                    total += jnp.sum(weight, axis=1, keepdims=True)
                    result += jnp.dot(
                        weight.astype(BF), vbuf[0 : length - CHIP, values], preferred_element_type=F32
                    )
                outs.append((result / total).astype(BF))
            out_ref[block * CHIP : (block + 1) * CHIP, pl.ds(pl.multiple_of(p * 256, 256), 256)] = (
                jnp.concatenate(outs, axis=1)
            )
            return carry

        lax.fori_loop(0, 4, pair, 0)

    for dy in (0, 1, 3, 2):
        for dc in range(2):
            if (dy, dc) != (0, 0):
                q_copy((4 - dy) % 4, dc).wait_recv()
        source = lax.rem(y + dy, RING)
        for block in range(RING):
            pl.when(source == block)(functools.partial(attend, block))
    for dy, dc in peers:
        q_copy(dy, dc).wait_send()


def attention_call(queries, latrope, w_uk, w_uv):
    return pl.pallas_call(
        attention_kernel,
        out_shape=(jax.ShapeDtypeStruct((LEN, 1024), BF), jax.ShapeDtypeStruct((LEN, 128), BF)),
        in_specs=[ANY, ANY, VM, VM],
        out_specs=(VM, VM),
        scratch_shapes=[
            pltpu.VMEM((8, TOK, QW), BF),
            pltpu.VMEM((8, TOK, LATW), BF),
            pltpu.VMEM((8, LEN, 256), BF),
            pltpu.VMEM((LEN, 1024), BF),
            DMA((8,)),
            DMA((8,)),
            DMA((8,)),
            DMA((8,)),
            DMA((2,)),
        ],
        compiler_params=pltpu.CompilerParams(
            collective_id=1, has_side_effects=True, vmem_limit_bytes=48 * 2**20
        ),
        name="attention",
    )(queries, latrope, w_uk, w_uv)


def exp_targets(y, core, z, x):
    found = [device(y, 1 - core, z, x)]
    for d in (1, 2, 3):
        found.append(device(step(y, d), core, z, x))
        found.append(device(y, core, step(z, d), x))
        found.append(device(y, core, z, step(x, d)))
    return found


def first_phase(j, spot, src, mid, send, recv, own):
    y, core, z, x = spot
    cut = lax.rem(j, SLOTS)
    copies = []
    for d in (1, 3, 2):
        xx, zz = step(x, d), step(z, d)
        copies.append(
            remote(src.at[cut, 0, :, xx], mid.at[j, 0, x], send.at[j, d], recv.at[j, d], device(y, core, z, xx))
        )
        copies.append(
            remote(
                src.at[cut, 1, zz], mid.at[j, 1, z], send.at[j, 3 + d], recv.at[j, 3 + d], device(y, core, zz, x)
            )
        )
    copies.append(pltpu.make_async_copy(src.at[cut, 0, :, x], mid.at[j, 0, x], own.at[j, 0]))
    copies.append(pltpu.make_async_copy(src.at[cut, 1, z], mid.at[j, 1, z], own.at[j, 1]))
    return copies


def second_phase(j, spot, mid, dst, send, recv, own):
    y, core, z, x = spot
    copies = []
    for d in (1, 3, 2):
        xx, zz = step(x, d), step(z, d)
        copies.append(
            remote(mid.at[j, 0, :, zz], dst.at[j, 0, z], send.at[j, d], recv.at[j, d], device(y, core, zz, x))
        )
        copies.append(
            remote(
                mid.at[j, 1, :, xx],
                dst.at[j, 1, :, x],
                send.at[j, 3 + d],
                recv.at[j, 3 + d],
                device(y, core, z, xx),
            )
        )
    copies.append(pltpu.make_async_copy(mid.at[j, 0, :, z], dst.at[j, 0, z], own.at[j, 0]))
    copies.append(pltpu.make_async_copy(mid.at[j, 1, :, x], dst.at[j, 1, :, x], own.at[j, 1]))
    return copies


def pipeline(stages):
    def turn(t, carry):
        for lag, stage in reversed(stages):
            j = t - lag

            @pl.when((j >= 0) & (j < CHUNKS))
            def _(stage=stage, j=j):
                stage(j)

        return carry

    lax.fori_loop(0, CHUNKS + stages[-1][0], turn, 0)


def start_all(copies):
    for copy in copies:
        copy.start()


def wait_all(copies):
    for copy in copies:
        copy.wait()


def moe_kernel(
    mixed_hbm, wo_hbm, stream_hbm, route_ref, wg_hbm, wu_hbm, wd_hbm, gain_ref, out_ref,
    mixed, late, p_own, p_sib, r_core, rs_buf, hbuf, gs, t1, xbuf, pickers, wg, wu, wd, sx, hown, swap, spots, units, squares,
    in_sem, wo_sem, w_sem, st_sem, c1_s, c1_r, rs_s, rs_r, ag_s, ag_r, c2_s, c2_r, p1_s, p1_r, p2_s, p2_r,
    d1_s, d1_r, d2_s, d2_r, c3_s, c3_r, fs_s, fs_r, sw_s, sw_r, o1, o2, o3, o4,
):
    spot = place()
    y, core, z, x = spot
    sibling = device(y, 1 - core, z, x)

    def columns(half, j):
        return pl.ds(pl.multiple_of(half * HALF + j * CW, 128), CW)

    def wo_copy(j, side):
        half = core if side == 0 else 1 - core
        return pltpu.make_async_copy(
            wo_hbm.at[:, :, :, columns(half, j)], late.at[j, side, :, :, 0:64], wo_sem.at[j, side]
        )

    def half_of(which):
        return pl.ds(pl.multiple_of(which * HALF, 128), HALF)

    mixed_copy = pltpu.make_async_copy(mixed_hbm, mixed.at[0:LEN], in_sem.at[0])
    stream_copy = pltpu.make_async_copy(stream_hbm.at[:, half_of(core)], sx.at[core], in_sem.at[1])
    weights = [
        pltpu.make_async_copy(wg_hbm, wg, w_sem.at[0]),
        pltpu.make_async_copy(wu_hbm, wu, w_sem.at[1]),
        pltpu.make_async_copy(wd_hbm, wd, w_sem.at[2]),
    ]
    mixed_copy.start()
    stream_copy.start()

    def load_wo(j, carry):
        for side in range(2):
            wo_copy(j, side).start()
        return carry

    lax.fori_loop(0, CHUNKS, load_wo, 0)
    start_all(weights)
    greet(exp_targets(y, core, z, x))
    stream_send = remote(
        stream_hbm.at[:, half_of(1 - core)], sx.at[core], st_sem.at[0], st_sem.at[1], sibling
    )
    stream_send.start()
    mixed_copy.wait()
    stream_copy.wait()

    def rows_of(which):
        return pl.ds(pl.multiple_of(which * CHIP, CHIP), CHIP)

    def core_sum(j, send, recv):
        slot = lax.rem(j, 2)
        return remote(p_sib.at[slot], r_core.at[slot], send.at[j], recv.at[j], sibling)

    def scatter(j, send, recv):
        return [
            remote(
                p_own.at[lax.rem(j, SLOTS), rows_of(step(y, d))],
                rs_buf.at[lax.rem(j, SLOTS), d - 1],
                send.at[j, d],
                recv.at[j, d],
                device(step(y, d), core, z, x),
            )
            for d in (1, 3, 2)
        ]

    def spread(j):
        block = hbuf.at[j, core, y, :, 0:64]
        return [
            remote(block, block, ag_s.at[j, d], ag_r.at[j, d], device(step(y, d), core, z, x))
            for d in (1, 3, 2)
        ]

    def core_share(j):
        block = hbuf.at[j, core, :, :, 0:64]
        return remote(block, block, c2_s.at[j], c2_r.at[j], sibling)

    def gather_row():
        row = lax.broadcasted_iota(jnp.int32, (1152, 128), 0)
        low = lax.broadcasted_iota(jnp.int32, (1152, 128), 1) * ROWS
        inside = (row >= low) & (row < low + ROWS)
        member = jnp.where(inside, 1.0, 0.0).astype(BF)
        at = jnp.sum(jnp.where(inside, row - low, 0).astype(F32), axis=1, keepdims=True)
        return member, at

    def route_spots():
        lane = lax.broadcasted_iota(jnp.int32, (TOK, 128), 1)
        first = ((y * 2 + core) * 16).astype(F32)
        wanted = jnp.where(lane < 16, lane.astype(F32) + first, -1.0)
        earlier = lax.broadcasted_iota(jnp.int32, (TOK, 128), 0) > lane
        earlier = jnp.where(earlier, 1.0, 0.0).astype(BF)
        for b in range(8):
            rows = slice(b * TOK, (b + 1) * TOK)
            route = route_ref[rows, :].astype(F32)
            named = jnp.zeros((TOK, 128), F32)
            gate = jnp.zeros((TOK, 128), F32)
            for k in range(TOPK):
                hit = route[:, 64 + k : 65 + k] == wanted
                named = jnp.where(hit, 1.0, named)
                gate = jnp.where(hit, route[:, 64 + TOPK + k : 65 + TOPK + k], gate)
            slot = jnp.dot(earlier, named.astype(BF), preferred_element_type=F32)
            spots[0, rows, :] = jnp.where(named > 0.0, slot + (b * CAP), -1.0).astype(BF)
            spots[1, rows, :] = gate.astype(BF)

    def pickers_in():
        member, at = gather_row()
        for b in range(RING):
            rows = slice(b * 288, (b + 1) * 288)
            wide = lax.dot_general(
                member[rows], spots[0], (((1,), (1,)), ((), ())), preferred_element_type=F32
            )
            pickers[rows, 0:LEN] = jnp.where(wide == at[rows], 1.0, 0.0).astype(BF)

    def pickers_out():
        low = lax.broadcasted_iota(jnp.int32, (128, 1152), 0) * ROWS
        row = lax.broadcasted_iota(jnp.int32, (128, 1152), 1)
        inside = (row >= low) & (row < low + ROWS)
        member = jnp.where(inside, 1.0, 0.0).astype(BF)
        at = jnp.sum(jnp.where(inside, row - low, 0).astype(F32), axis=0, keepdims=True)
        for b in range(RING):
            rows = slice(b * CHIP, (b + 1) * CHIP)
            wide = jnp.dot(spots[0, rows, :], member, preferred_element_type=F32)
            gate = jnp.dot(spots[1, rows, :], member, preferred_element_type=F32)
            pickers[rows, :] = jnp.where(wide == at, gate, 0.0).astype(BF)

    def one(j):
        return first_phase(j, spot, gs, t1, p1_s, p1_r, o1)

    def two(j):
        return second_phase(j, spot, t1, xbuf, p2_s, p2_r, o2)

    def project(j):
        for side in range(2):
            wo_copy(j, side).wait()
        own = late[j, 0, :, :, 0:64].reshape(1024, CW)
        other = late[j, 1, :, :, 0:64].reshape(1024, CW)
        both = jnp.concatenate([own, other], axis=1)

        def block(b, carry):
            rows = rows_of(b)
            product = jnp.dot(mixed[rows, :], both, preferred_element_type=F32).astype(BF)
            p_own[lax.rem(j, SLOTS), rows] = product[:, :CW]
            p_sib[lax.rem(j, 2), rows] = product[:, CW:]
            return carry

        lax.fori_loop(0, RING, block, 0)
        core_sum(j, c1_s, c1_r).start()

    def add_core(j):
        core_sum(j, c1_s, c1_r).wait()
        slot = lax.rem(j, SLOTS)
        p_own[slot] = (p_own[slot].astype(F32) + r_core[lax.rem(j, 2)].astype(F32)).astype(BF)
        start_all(scatter(j, rs_s, rs_r))

    def chip_total(j):
        slot = lax.rem(j, SLOTS)
        total = p_own[slot, rows_of(y)].astype(F32)
        for i in range(3):
            total += rs_buf[slot, i].astype(F32)
        return total

    def finish_hidden(j):
        wait_all(scatter(j, rs_s, rs_r))
        stream = sx[:, :, pl.ds(pl.multiple_of(j * CW, 128), CW)].reshape(CHIP, CW)
        hidden = (stream.astype(F32) + chip_total(j)).astype(BF)
        hbuf[j, core, y, :, 0:64] = hidden.reshape(RING, 64, CW)
        hown[j] = hidden
        start_all(spread(j))

    def share(j):
        wait_all(spread(j))
        core_share(j).start()

    def pick(j):
        core_share(j).wait()
        both = jnp.concatenate(
            [hbuf[j, half, :, :, 0:64].reshape(1024, CW) for half in range(2)], axis=1
        )

        def block(b, carry):
            left = pickers[pl.ds(pl.multiple_of(b * 288, 16), 288), 0:LEN]
            picked = jnp.dot(left, both, preferred_element_type=F32).reshape(RING, ROWS, 2 * CW)
            gs[lax.rem(j, SLOTS), 0, b] = picked[:, :, :CW].astype(BF)
            gs[lax.rem(j, SLOTS), 1, b] = picked[:, :, CW:].astype(BF)
            return carry

        lax.fori_loop(0, RING, block, 0)
        start_all(one(j))

    def forward(j):
        wait_all(one(j))
        start_all(two(j))

    def drain(j):
        wait_all(two(j))

        @pl.when(j == 0)
        def _():
            wait_all(weights)

        gains = [gain_ref[pl.ds(half * CHUNKS + j, 1), :] for half in range(2)]
        firsts = [pl.ds(pl.multiple_of(half * HALF + j * CW, 128), CW) for half in range(2)]
        right_gate = jnp.concatenate([wg[rows, :] for rows in firsts], axis=0)
        right_up = jnp.concatenate([wu[rows, :] for rows in firsts], axis=0)

        def block(b, carry):
            rows = pl.ds(pl.multiple_of(b * 288, 16), 288)
            parts = [xbuf[j, half, b].astype(F32).reshape(288, CW) for half in range(2)]
            squares[rows, :] += parts[0] * parts[0] + parts[1] * parts[1]
            left = jnp.concatenate([(p * g).astype(BF) for p, g in zip(parts, gains)], axis=1)
            units[rows, 0:FF] += jnp.dot(left, right_gate, preferred_element_type=F32)
            units[rows, FF : 2 * FF] += jnp.dot(left, right_up, preferred_element_type=F32)
            return carry

        lax.fori_loop(0, RING, block, 0)

    def clear():
        units[...] = jnp.zeros((1152, 2 * FF), F32)
        squares[...] = jnp.zeros((1152, CW), F32)

    def prepare(j):
        pl.when(j == 0)(route_spots)
        pl.when(j == 1)(pickers_in)
        pl.when(j == 2)(clear)

    stream_send.wait()
    pipeline(
        [
            (0, project),
            (1, add_core),
            (1, prepare),
            (3, finish_hidden),
            (5, share),
            (6, pick),
            (8, forward),
            (10, drain),
        ]
    )

    def hidden_units(b, carry):
        rows = pl.ds(pl.multiple_of(b * 144, 16), 144)
        total = jnp.sum(squares[rows, :], axis=1, keepdims=True)
        scale = lax.rsqrt(total * (1.0 / D) + 1e-06)
        gate = units[rows, 0:FF] * scale
        up = units[rows, FF : 2 * FF] * scale
        mixed[rows, 0:FF] = (gate / (1.0 + jnp.exp(-gate)) * up).astype(BF)
        return carry

    lax.fori_loop(0, 8, hidden_units, 0)

    def back_one(j):
        return first_phase(j, spot, gs, late, d1_s, d1_r, o3)

    def back_two(j):
        return second_phase(j, spot, late, hbuf, d2_s, d2_r, o4)

    def exchange(j):
        slot = lax.rem(j, 2)
        return remote(swap.at[slot, 0], swap.at[slot, 1], sw_s.at[j], sw_r.at[j], sibling)

    def down(j):
        both = jnp.concatenate([wd[:, columns(half, j)] for half in range(2)], axis=1)

        def block(b, carry):
            left = mixed[pl.ds(pl.multiple_of(b * 288, 16), 288), 0:FF]
            result = jnp.dot(left, both, preferred_element_type=F32).reshape(RING, ROWS, 2 * CW)
            gs[lax.rem(j, SLOTS), 0, b] = result[:, :, :CW].astype(BF)
            gs[lax.rem(j, SLOTS), 1, b] = result[:, :, CW:].astype(BF)
            return carry

        lax.fori_loop(0, RING, block, 0)
        start_all(back_one(j))

    def back_forward(j):
        wait_all(back_one(j))
        start_all(back_two(j))

    def combine(j):
        wait_all(back_two(j))
        both = jnp.concatenate(
            [
                hbuf[j, core].astype(F32).reshape(1152, CW).astype(BF),
                hbuf[j, 1 - core].astype(F32).reshape(1152, CW).astype(BF),
            ],
            axis=1,
        )

        def block(b, carry):
            rows = rows_of(b)
            product = jnp.dot(pickers[rows, :], both, preferred_element_type=F32).astype(BF)
            p_own[lax.rem(j, SLOTS), rows] = product[:, :CW]
            p_sib[lax.rem(j, 2), rows] = product[:, CW:]
            return carry

        lax.fori_loop(0, RING, block, 0)
        core_sum(j, c3_s, c3_r).start()

    def add_back(j):
        core_sum(j, c3_s, c3_r).wait()
        slot = lax.rem(j, SLOTS)
        p_own[slot] = (p_own[slot].astype(F32) + r_core[lax.rem(j, 2)].astype(F32)).astype(BF)
        start_all(scatter(j, fs_s, fs_r))

    def finish(j):
        wait_all(scatter(j, fs_s, fs_r))
        total = (hown[j].astype(F32) + chip_total(j)).astype(BF)
        swap[lax.rem(j, 2), 0] = jnp.where(core == 0, total[TOK:], total[:TOK])
        exchange(j).start()
        out_ref[:, columns(core, j)] = jnp.where(core == 0, total[:TOK], total[TOK:])

    def land(j):
        exchange(j).wait()
        out_ref[:, columns(1 - core, j)] = swap[lax.rem(j, 2), 1]

    def prepare_back(j):
        pl.when(j == 0)(pickers_out)

    pipeline(
        [
            (0, down),
            (1, prepare_back),
            (2, back_forward),
            (4, combine),
            (5, add_back),
            (7, finish),
            (8, land),
        ]
    )


def moe_call(mixed, w_o, stream, route, w_gate, w_up, w_down, gain):
    grid_rows = (CHUNKS, 2, RING, RING, ROWS, CW)
    one = DMA((CHUNKS,))
    ring = DMA((CHUNKS, 4))
    phase = DMA((CHUNKS, 7))
    return pl.pallas_call(
        moe_kernel,
        out_shape=jax.ShapeDtypeStruct((TOK, D), BF),
        in_specs=[ANY, ANY, ANY, VM, ANY, ANY, ANY, VM],
        out_specs=VM,
        scratch_shapes=[
            pltpu.VMEM((1152, 1024), BF),
            pltpu.VMEM(grid_rows, BF),
            pltpu.VMEM((SLOTS, LEN, CW), BF),
            pltpu.VMEM((2, LEN, CW), BF),
            pltpu.VMEM((2, LEN, CW), BF),
            pltpu.VMEM((SLOTS, 3, CHIP, CW), BF),
            pltpu.VMEM(grid_rows, BF),
            pltpu.VMEM((SLOTS, *grid_rows[1:]), BF),
            pltpu.VMEM(grid_rows, BF),
            pltpu.VMEM(grid_rows, BF),
            pltpu.VMEM((1152, 1152), BF),
            pltpu.VMEM((D, FF), BF),
            pltpu.VMEM((D, FF), BF),
            pltpu.VMEM((FF, D), BF),
            pltpu.VMEM((2, TOK, HALF), BF),
            pltpu.VMEM((CHUNKS, CHIP, CW), BF),
            pltpu.VMEM((2, 2, TOK, CW), BF),
            pltpu.VMEM((2, LEN, 128), BF),
            pltpu.VMEM((1152, 2 * FF), F32),
            pltpu.VMEM((1152, CW), F32),
            DMA((2,)),
            DMA((CHUNKS, 2)),
            DMA((3,)),
            DMA((2,)),
            *[one, one, ring, ring, ring, ring, one, one],
            *[phase] * 8,
            *[one, one, ring, ring, one, one],
            *[DMA((CHUNKS, 2))] * 4,
        ],
        compiler_params=pltpu.CompilerParams(
            collective_id=2, has_side_effects=True, vmem_limit_bytes=63 * 2**20
        ),
        name="moe",
    )(mixed, w_o, stream, route, w_gate, w_up, w_down, gain)


def local(
    stream_in,
    queries,
    latents,
    key_rope,
    w_uk,
    w_uv,
    w_o,
    norm_gain,
    expert_ids,
    gate_weights,
    w_gate,
    w_up,
    w_down,
):
    packed = jnp.concatenate(
        [latents[0], key_rope[0], expert_ids[0].astype(BF), gate_weights[0].astype(BF), jnp.zeros((TOK, 52), BF)],
        axis=1,
    )
    mixed, route = attention_call(queries[0], packed, w_uk, w_uv)
    blocks = w_o.reshape(RING, RING, 64, D)
    out = moe_call(
        mixed, blocks, stream_in[0], route, w_gate[0], w_up[0], w_down[0], norm_gain.reshape(2 * CHUNKS, CW)
    )
    return out[None]


def solution(mesh):
    return jax.shard_map(
        local,
        mesh=mesh,
        in_specs=(
            P("exp", "ctx", None),
            P("exp", "ctx", None),
            P("exp", "ctx", None),
            P("exp", "ctx", None),
            P(None, "ctx"),
            P(None, "ctx"),
            P("ctx", None),
            P(),
            P("exp", "ctx", None),
            P("exp", "ctx", None),
            P(("ctx", "exp"), None, None),
            P(("ctx", "exp"), None, None),
            P(("ctx", "exp"), None, None),
        ),
        out_specs=P("exp", "ctx", None),
        check_vma=False,
    )
```

```python
import functools
import math

import jax
import jax.numpy as jnp
from jax import lax
from jax.experimental import pallas as pl
from jax.experimental.pallas import tpu as pltpu
from jax.sharding import PartitionSpec as P

NOPE = 128
ROPE = 64
VDIM = 128
KVL = 512
D = 2560
FF = 768
TOPK = 6
CAP = 9
TOK = 128
LEN = 1024
QW = 1536
RING = 4
ROWS = 72
CHUNKS = 10
CW = 128
SLOTS = 4
ROWS_IN = 5
HALF = 1280
CHIP = 256
LATW = 640
MESH = pl.DeviceIdType.MESH
BF = jnp.bfloat16
F32 = jnp.float32
ANY = pl.BlockSpec(memory_space=pl.ANY)
VM = pl.BlockSpec(memory_space=pltpu.VMEM)
DMA = pltpu.SemaphoreType.DMA


def place():
    c = lax.axis_index("ctx")
    e = lax.axis_index("exp")
    return c // 2, c % 2, e // RING, e % RING


def device(y, core, z, x):
    return (y * 2 + core, z * RING + x)


def step(v, d):
    return lax.rem(v + d, RING)


def remote(src, dst, send, recv, target):
    return pltpu.make_async_remote_copy(
        src_ref=src, dst_ref=dst, send_sem=send, recv_sem=recv, device_id=target, device_id_type=MESH
    )


def greet(targets):
    barrier = pltpu.get_barrier_semaphore()
    for target in targets:
        pl.semaphore_signal(barrier, inc=1, device_id=target, device_id_type=MESH)
    pl.semaphore_wait(barrier, len(targets))


def exp_targets(y, core, z, x):
    found = [device(y, 1 - core, z, x)]
    for d in (1, 2, 3):
        found.append(device(step(y, d), core, z, x))
        found.append(device(y, core, step(z, d), x))
        found.append(device(y, core, z, step(x, d)))
    return found


def first_phase(j, spot, src, mid, send, recv, own):
    y, core, z, x = spot
    cut = lax.rem(j, SLOTS)
    copies = []
    for d in (1, 3, 2):
        xx, zz = step(x, d), step(z, d)
        copies.append(
            remote(src.at[cut, 0, :, xx], mid.at[j, 0, x], send.at[j, d], recv.at[j, d], device(y, core, z, xx))
        )
        copies.append(
            remote(
                src.at[cut, 1, zz], mid.at[j, 1, z], send.at[j, 3 + d], recv.at[j, 3 + d], device(y, core, zz, x)
            )
        )
    copies.append(pltpu.make_async_copy(src.at[cut, 0, :, x], mid.at[j, 0, x], own.at[j, 0]))
    copies.append(pltpu.make_async_copy(src.at[cut, 1, z], mid.at[j, 1, z], own.at[j, 1]))
    return copies


def second_phase(j, spot, mid, dst, cut, send, recv, own):
    y, core, z, x = spot
    copies = []
    for d in (1, 3, 2):
        xx, zz = step(x, d), step(z, d)
        copies.append(
            remote(mid.at[j, 0, :, zz], dst.at[cut, 0, z], send.at[j, d], recv.at[j, d], device(y, core, zz, x))
        )
        copies.append(
            remote(
                mid.at[j, 1, :, xx],
                dst.at[cut, 1, :, x],
                send.at[j, 3 + d],
                recv.at[j, 3 + d],
                device(y, core, z, xx),
            )
        )
    copies.append(pltpu.make_async_copy(mid.at[j, 0, :, z], dst.at[cut, 0, z], own.at[j, 0]))
    copies.append(pltpu.make_async_copy(mid.at[j, 1, :, x], dst.at[cut, 1, :, x], own.at[j, 1]))
    return copies


def pipeline(stages):
    def turn(t, carry):
        for lag, stage in reversed(stages):
            j = t - lag

            @pl.when((j >= 0) & (j < CHUNKS))
            def _(stage=stage, j=j):
                stage(j)

        return carry

    lax.fori_loop(0, CHUNKS + stages[-1][0], turn, 0)


def start_all(copies):
    for copy in copies:
        copy.start()


def wait_all(copies):
    for copy in copies:
        copy.wait()


def moe_kernel(
    q_hbm, lat_hbm, uk_hbm, uv_hbm, wo_hbm, stream_hbm, wg_hbm, wu_hbm, wd_hbm, gain_ref, out_ref,
    qbuf, lat, q_send, q_recv, l_send, l_recv, own_sem,
    mixed, late, p_own, p_sib, r_core, rs_buf, hbuf, gs, t1, xbuf, pickers, wg, wu, wd, sx, hown, swap, spots,
    in_sem, wo_sem, w_sem, st_sem, c1_s, c1_r, rs_s, rs_r, ag_s, ag_r, c2_s, c2_r, p1_s, p1_r, p2_s, p2_r,
    d1_s, d1_r, d2_s, d2_r, c3_s, c3_r, fs_s, fs_r, sw_s, sw_r, o1, o2, o3, o4,
):
    spot = place()
    y, core, z, x = spot
    sibling = device(y, 1 - core, z, x)

    def columns(half, j):
        return pl.ds(pl.multiple_of(half * HALF + j * CW, 128), CW)

    def wo_copy(j, side):
        half = core if side == 0 else 1 - core
        return pltpu.make_async_copy(
            wo_hbm.at[:, :, :, columns(half, j)], late.at[j, side, :, :, 0:64], wo_sem.at[j, side]
        )

    def half_of(which):
        return pl.ds(pl.multiple_of(which * HALF, 128), HALF)

    stream_copy = pltpu.make_async_copy(stream_hbm.at[:, half_of(core)], sx.at[core], in_sem.at[1])
    weights = [
        pltpu.make_async_copy(wg_hbm, wg, w_sem.at[0]),
        pltpu.make_async_copy(wu_hbm, wu, w_sem.at[1]),
        pltpu.make_async_copy(wd_hbm, wd, w_sem.at[2]),
    ]
    me = y * 2 + core

    def lat_copy(dy):
        return remote(lat_hbm, lat.at[me], l_send.at[dy], l_recv.at[dy], device(step(y, dy), core, z, x))

    def lat_share(dy):
        block = lat.at[step(y, dy) * 2 + core]
        return remote(block, block, l_send.at[4 + dy], l_recv.at[4 + dy], device(y, 1 - core, z, x))

    def q_copy(dy, dc):
        i = dy * 2 + dc
        yy, cc = step(y, dy), lax.rem(core + dc, 2)
        columns = pl.ds(pl.multiple_of((yy * 2 + cc) * QW, 128), QW)
        return remote(q_hbm.at[:, columns], qbuf.at[me], q_send.at[i], q_recv.at[i], device(yy, cc, z, x))

    peers = [(dy, dc) for dy in (0, 1, 3, 2) for dc in (0, 1) if (dy, dc) != (0, 0)]
    own_lat = pltpu.make_async_copy(lat_hbm, lat.at[me], own_sem.at[0])
    own_q = pltpu.make_async_copy(
        q_hbm.at[:, pl.ds(pl.multiple_of(me * QW, 128), QW)], qbuf.at[me], own_sem.at[1]
    )
    own_lat.start()
    own_q.start()
    greet(exp_targets(y, core, z, x) + [device(step(y, d), 1 - core, z, x) for d in (1, 2, 3)])
    for dy in (1, 3, 2):
        lat_copy(dy).start()
    for dy, dc in peers:
        q_copy(dy, dc).start()
    stream_copy.start()

    def load_wo(j, carry):
        for side in range(2):
            wo_copy(j, side).start()
        return carry

    stream_send = remote(
        stream_hbm.at[:, half_of(1 - core)], sx.at[core], st_sem.at[0], st_sem.at[1], sibling
    )
    stream_send.start()
    stream_copy.wait()

    def rows_of(which):
        return pl.ds(pl.multiple_of(which * CHIP, CHIP), CHIP)

    def core_sum(j, send, recv):
        slot = lax.rem(j, 2)
        return remote(p_sib.at[slot], r_core.at[slot], send.at[j], recv.at[j], sibling)

    def scatter(j, send, recv):
        return [
            remote(
                p_own.at[lax.rem(j, SLOTS), rows_of(step(y, d))],
                rs_buf.at[lax.rem(j, SLOTS), d - 1],
                send.at[j, d],
                recv.at[j, d],
                device(step(y, d), core, z, x),
            )
            for d in (1, 3, 2)
        ]

    def spread(j):
        block = hbuf.at[j, core, y, :, 0:64]
        return [
            remote(block, block, ag_s.at[j, d], ag_r.at[j, d], device(step(y, d), core, z, x))
            for d in (1, 3, 2)
        ]

    def core_share(j):
        block = hbuf.at[j, core, :, :, 0:64]
        return remote(block, block, c2_s.at[j], c2_r.at[j], sibling)

    def gather_row():
        row = lax.broadcasted_iota(jnp.int32, (1152, 128), 0)
        low = lax.broadcasted_iota(jnp.int32, (1152, 128), 1) * ROWS
        inside = (row >= low) & (row < low + ROWS)
        member = jnp.where(inside, 1.0, 0.0).astype(BF)
        at = jnp.sum(jnp.where(inside, row - low, 0).astype(F32), axis=1, keepdims=True)
        return member, at

    def route_spots():
        lane = lax.broadcasted_iota(jnp.int32, (TOK, 128), 1)
        first = ((y * 2 + core) * 16).astype(F32)
        wanted = jnp.where(lane < 16, lane.astype(F32) + first, -1.0)
        earlier = lax.broadcasted_iota(jnp.int32, (TOK, 128), 0) > lane
        earlier = jnp.where(earlier, 1.0, 0.0).astype(BF)
        for b in range(8):
            rows = slice(b * TOK, (b + 1) * TOK)
            route = lat[b, :, KVL:].astype(F32)
            named = jnp.zeros((TOK, 128), F32)
            gate = jnp.zeros((TOK, 128), F32)
            for k in range(TOPK):
                hit = route[:, 64 + k : 65 + k] == wanted
                named = jnp.where(hit, 1.0, named)
                gate = jnp.where(hit, route[:, 64 + TOPK + k : 65 + TOPK + k], gate)
            slot = jnp.dot(earlier, named.astype(BF), preferred_element_type=F32)
            spots[0, rows, :] = jnp.where(named > 0.0, slot + (b * CAP), -1.0).astype(BF)
            spots[1, rows, :] = gate.astype(BF)

    def pickers_in():
        member, at = gather_row()
        for b in range(RING):
            rows = slice(b * 288, (b + 1) * 288)
            wide = lax.dot_general(
                member[rows], spots[0], (((1,), (1,)), ((), ())), preferred_element_type=F32
            )
            pickers[rows, 0:LEN] = jnp.where(wide == at[rows], 1.0, 0.0).astype(BF)

    def pickers_out():
        low = lax.broadcasted_iota(jnp.int32, (128, 1152), 0) * ROWS
        row = lax.broadcasted_iota(jnp.int32, (128, 1152), 1)
        inside = (row >= low) & (row < low + ROWS)
        member = jnp.where(inside, 1.0, 0.0).astype(BF)
        at = jnp.sum(jnp.where(inside, row - low, 0).astype(F32), axis=0, keepdims=True)
        for b in range(RING):
            rows = slice(b * CHIP, (b + 1) * CHIP)
            wide = jnp.dot(spots[0, rows, :], member, preferred_element_type=F32)
            gate = jnp.dot(spots[1, rows, :], member, preferred_element_type=F32)
            pickers[rows, :] = jnp.where(wide == at, gate, 0.0).astype(BF)

    def attention(kbuf, vbuf, uk_ref, uv_ref, u_sem):
        projections = [
            pltpu.make_async_copy(uk_hbm, uk_ref, u_sem.at[0]),
            pltpu.make_async_copy(uv_hbm, uv_ref, u_sem.at[1]),
        ]
        start_all(projections)
        own_lat.wait()
        lat_share(0).start()
        for dy in (1, 3, 2):
            lat_copy(4 - dy).wait_recv()
            lat_share(dy).start()
        for dy in (0, 1, 3, 2):
            lat_share(dy).wait()
        for dy in (1, 3, 2):
            lat_copy(dy).wait_send()
        own_q.wait()
        lax.fori_loop(0, CHUNKS, load_wo, 0)
        start_all(weights)

        wait_all(projections)
        lane = lax.broadcasted_iota(jnp.int32, (CHIP, 128), 1)

        def project(b, carry):
            rows = pl.ds(pl.multiple_of(b * CHIP, CHIP), CHIP)
            block = lat[pl.ds(b * 2, 2)].reshape(CHIP, LATW)
            latent = block[:, :KVL]
            rope = block[:, KVL:].astype(F32)
            rope_low = jnp.where(lane < 64, rope, 0.0).astype(BF)
            rope_high = pltpu.roll(rope, 64, 1)
            for h in range(8):
                nope = jnp.dot(latent, uk_ref[:, h * 128 : h * 128 + 128], preferred_element_type=F32)
                if h % 2 == 0:
                    kbuf[h, rows, 0:128] = nope.astype(BF)
                    kbuf[h, rows, 128:256] = rope_low
                else:
                    turned = pltpu.roll(nope, 64, 1)
                    kbuf[h, rows, 0:128] = jnp.where(lane < 64, 0.0, turned).astype(BF)
                    kbuf[h, rows, 128:256] = jnp.where(lane < 64, turned, rope_high).astype(BF)
            vbuf[rows, :] = jnp.dot(latent, uv_ref[...], preferred_element_type=F32).astype(BF)
            return carry

        lax.fori_loop(0, RING, project, 0)

        route_spots()
        pickers_in()
        factor = 1.0 / math.sqrt(NOPE + ROPE) * math.log2(math.e)
        row_at = lax.broadcasted_iota(jnp.int32, (CHIP, CHIP), 0)
        col_at = lax.broadcasted_iota(jnp.int32, (CHIP, CHIP), 1)
        causal = row_at >= col_at

        def attend(block):
            length = (block + 1) * CHIP

            def pair(p, carry):
                columns = pl.ds(pl.multiple_of(p * 384, 128), 384)
                q = qbuf[block * 2 : block * 2 + 2, :, columns].reshape(CHIP, 384)
                outs = []
                for odd in range(2):
                    query = q[:, odd * 128 : odd * 128 + 256]
                    head = p * 2 + odd
                    contract = (((1,), (1,)), ((), ()))
                    last = lax.dot_general(
                        query, kbuf[head, length - CHIP : length], contract, preferred_element_type=F32
                    )
                    last = jnp.where(causal, last, -jnp.inf)
                    peak = jnp.max(last, axis=1, keepdims=True)
                    if block:
                        first = lax.dot_general(
                            query, kbuf[head, 0 : length - CHIP], contract, preferred_element_type=F32
                        )
                        peak = jnp.maximum(peak, jnp.max(first, axis=1, keepdims=True))
                    values = pl.ds(pl.multiple_of(head * 128, 128), 128)
                    weight = jnp.exp2((last - peak) * factor)
                    total = jnp.sum(weight, axis=1, keepdims=True)
                    result = jnp.dot(
                        weight.astype(BF), vbuf[length - CHIP : length, values], preferred_element_type=F32
                    )
                    if block:
                        weight = jnp.exp2((first - peak) * factor)
                        total += jnp.sum(weight, axis=1, keepdims=True)
                        result += jnp.dot(
                            weight.astype(BF), vbuf[0 : length - CHIP, values], preferred_element_type=F32
                        )
                    outs.append((result / total).astype(BF))
                mixed[block * CHIP : (block + 1) * CHIP, pl.ds(pl.multiple_of(p * 256, 256), 256)] = (
                    jnp.concatenate(outs, axis=1)
                )
                return carry

            lax.fori_loop(0, 4, pair, 0)

        for dy in (0, 1, 3, 2):
            for dc in range(2):
                if (dy, dc) != (0, 0):
                    q_copy((4 - dy) % 4, dc).wait_recv()
            source = lax.rem(y + dy, RING)
            for block in range(RING):
                pl.when(source == block)(functools.partial(attend, block))
        for dy, dc in peers:
            q_copy(dy, dc).wait_send()

    pl.run_scoped(
        attention,
        pltpu.VMEM((8, LEN, 256), BF),
        pltpu.VMEM((LEN, 1024), BF),
        pltpu.VMEM((KVL, 1024), BF),
        pltpu.VMEM((KVL, 1024), BF),
        DMA((2,)),
    )
    stream_send.wait()

    def experts(units, squares):
        def one(j):
            return first_phase(j, spot, gs, t1, p1_s, p1_r, o1)

        def two(j):
            return second_phase(j, spot, t1, xbuf, lax.rem(j, ROWS_IN), p2_s, p2_r, o2)

        def project(j):
            for side in range(2):
                wo_copy(j, side).wait()
            own = late[j, 0, :, :, 0:64].reshape(1024, CW)
            other = late[j, 1, :, :, 0:64].reshape(1024, CW)
            both = jnp.concatenate([own, other], axis=1)

            def block(b, carry):
                rows = rows_of(b)
                product = jnp.dot(mixed[rows, :], both, preferred_element_type=F32).astype(BF)
                p_own[lax.rem(j, SLOTS), rows] = product[:, :CW]
                p_sib[lax.rem(j, 2), rows] = product[:, CW:]
                return carry

            lax.fori_loop(0, RING, block, 0)
            core_sum(j, c1_s, c1_r).start()

        def add_core(j):
            core_sum(j, c1_s, c1_r).wait()
            slot = lax.rem(j, SLOTS)
            p_own[slot] = (p_own[slot].astype(F32) + r_core[lax.rem(j, 2)].astype(F32)).astype(BF)
            start_all(scatter(j, rs_s, rs_r))

        def chip_total(j):
            slot = lax.rem(j, SLOTS)
            total = p_own[slot, rows_of(y)].astype(F32)
            for i in range(3):
                total += rs_buf[slot, i].astype(F32)
            return total

        def finish_hidden(j):
            wait_all(scatter(j, rs_s, rs_r))
            stream = sx[:, :, pl.ds(pl.multiple_of(j * CW, 128), CW)].reshape(CHIP, CW)
            hidden = (stream.astype(F32) + chip_total(j)).astype(BF)
            hbuf[j, core, y, :, 0:64] = hidden.reshape(RING, 64, CW)
            hown[j] = hidden
            start_all(spread(j))

        def share(j):
            wait_all(spread(j))
            core_share(j).start()

        def pick(j):
            core_share(j).wait()
            both = jnp.concatenate(
                [hbuf[j, half, :, :, 0:64].reshape(1024, CW) for half in range(2)], axis=1
            )

            def block(b, carry):
                left = pickers[pl.ds(pl.multiple_of(b * 288, 16), 288), 0:LEN]
                picked = jnp.dot(left, both, preferred_element_type=F32).reshape(RING, ROWS, 2 * CW)
                gs[lax.rem(j, SLOTS), 0, b] = picked[:, :, :CW].astype(BF)
                gs[lax.rem(j, SLOTS), 1, b] = picked[:, :, CW:].astype(BF)
                return carry

            lax.fori_loop(0, RING, block, 0)
            start_all(one(j))

        def forward(j):
            wait_all(one(j))
            start_all(two(j))

        def drain(j):
            wait_all(two(j))

            @pl.when(j == 0)
            def _():
                wait_all(weights)

            gains = [gain_ref[pl.ds(half * CHUNKS + j, 1), :] for half in range(2)]
            firsts = [pl.ds(pl.multiple_of(half * HALF + j * CW, 128), CW) for half in range(2)]
            right_gate = jnp.concatenate([wg[rows, :] for rows in firsts], axis=0)
            right_up = jnp.concatenate([wu[rows, :] for rows in firsts], axis=0)

            def block(b, carry):
                rows = pl.ds(pl.multiple_of(b * 288, 16), 288)
                parts = [xbuf[lax.rem(j, ROWS_IN), half, b].astype(F32).reshape(288, CW) for half in range(2)]
                squares[rows, :] += parts[0] * parts[0] + parts[1] * parts[1]
                left = jnp.concatenate([(p * g).astype(BF) for p, g in zip(parts, gains)], axis=1)
                units[rows, 0:FF] += jnp.dot(left, right_gate, preferred_element_type=F32)
                units[rows, FF : 2 * FF] += jnp.dot(left, right_up, preferred_element_type=F32)
                return carry

            lax.fori_loop(0, RING, block, 0)

        def clear():
            units[...] = jnp.zeros((1152, 2 * FF), F32)
            squares[...] = jnp.zeros((1152, CW), F32)

        def prepare(j):
            pl.when(j == 2)(clear)

        pipeline(
            [
                (0, project),
                (1, add_core),
                (1, prepare),
                (3, finish_hidden),
                (5, share),
                (6, pick),
                (8, forward),
                (10, drain),
            ]
        )

        def hidden_units(b, carry):
            rows = pl.ds(pl.multiple_of(b * 144, 16), 144)
            total = jnp.sum(squares[rows, :], axis=1, keepdims=True)
            scale = lax.rsqrt(total * (1.0 / D) + 1e-06)
            gate = units[rows, 0:FF] * scale
            up = units[rows, FF : 2 * FF] * scale
            mixed[rows, 0:FF] = (gate / (1.0 + jnp.exp(-gate)) * up).astype(BF)
            return carry

        lax.fori_loop(0, 8, hidden_units, 0)

        def back_one(j):
            return first_phase(j, spot, gs, late, d1_s, d1_r, o3)

        def back_two(j):
            return second_phase(j, spot, late, hbuf, j, d2_s, d2_r, o4)

        def exchange(j):
            slot = lax.rem(j, 2)
            return remote(swap.at[slot, 0], swap.at[slot, 1], sw_s.at[j], sw_r.at[j], sibling)

        def down(j):
            both = jnp.concatenate([wd[:, columns(half, j)] for half in range(2)], axis=1)

            def block(b, carry):
                left = mixed[pl.ds(pl.multiple_of(b * 288, 16), 288), 0:FF]
                result = jnp.dot(left, both, preferred_element_type=F32).reshape(RING, ROWS, 2 * CW)
                gs[lax.rem(j, SLOTS), 0, b] = result[:, :, :CW].astype(BF)
                gs[lax.rem(j, SLOTS), 1, b] = result[:, :, CW:].astype(BF)
                return carry

            lax.fori_loop(0, RING, block, 0)
            start_all(back_one(j))

        def back_forward(j):
            wait_all(back_one(j))
            start_all(back_two(j))

        def combine(j):
            wait_all(back_two(j))
            both = jnp.concatenate(
                [
                    hbuf[j, core].astype(F32).reshape(1152, CW).astype(BF),
                    hbuf[j, 1 - core].astype(F32).reshape(1152, CW).astype(BF),
                ],
                axis=1,
            )

            def block(b, carry):
                rows = rows_of(b)
                product = jnp.dot(pickers[rows, :], both, preferred_element_type=F32).astype(BF)
                p_own[lax.rem(j, SLOTS), rows] = product[:, :CW]
                p_sib[lax.rem(j, 2), rows] = product[:, CW:]
                return carry

            lax.fori_loop(0, RING, block, 0)
            core_sum(j, c3_s, c3_r).start()

        def add_back(j):
            core_sum(j, c3_s, c3_r).wait()
            slot = lax.rem(j, SLOTS)
            p_own[slot] = (p_own[slot].astype(F32) + r_core[lax.rem(j, 2)].astype(F32)).astype(BF)
            start_all(scatter(j, fs_s, fs_r))

        def finish(j):
            wait_all(scatter(j, fs_s, fs_r))
            total = (hown[j].astype(F32) + chip_total(j)).astype(BF)
            swap[lax.rem(j, 2), 0] = jnp.where(core == 0, total[TOK:], total[:TOK])
            exchange(j).start()
            out_ref[:, columns(core, j)] = jnp.where(core == 0, total[:TOK], total[TOK:])

        def land(j):
            exchange(j).wait()
            out_ref[:, columns(1 - core, j)] = swap[lax.rem(j, 2), 1]

        def prepare_back(j):
            pl.when(j == 0)(pickers_out)

        pipeline(
            [
                (0, down),
                (1, prepare_back),
                (2, back_forward),
                (4, combine),
                (5, add_back),
                (7, finish),
                (8, land),
            ]
        )

    pl.run_scoped(experts, pltpu.VMEM((1152, 2 * FF), F32), pltpu.VMEM((1152, CW), F32))


def moe_call(queries, packed, w_uk, w_uv, w_o, stream, w_gate, w_up, w_down, gain):
    grid_rows = (CHUNKS, 2, RING, RING, ROWS, CW)
    one = DMA((CHUNKS,))
    ring = DMA((CHUNKS, 4))
    phase = DMA((CHUNKS, 7))
    return pl.pallas_call(
        moe_kernel,
        out_shape=jax.ShapeDtypeStruct((TOK, D), BF),
        in_specs=[ANY] * 9 + [VM],
        out_specs=VM,
        scratch_shapes=[
            pltpu.VMEM((8, TOK, QW), BF),
            pltpu.VMEM((8, TOK, LATW), BF),
            *[DMA((8,))] * 4,
            DMA((2,)),
            pltpu.VMEM((1152, 1024), BF),
            pltpu.VMEM(grid_rows, BF),
            pltpu.VMEM((SLOTS, LEN, CW), BF),
            pltpu.VMEM((2, LEN, CW), BF),
            pltpu.VMEM((2, LEN, CW), BF),
            pltpu.VMEM((SLOTS, 3, CHIP, CW), BF),
            pltpu.VMEM(grid_rows, BF),
            pltpu.VMEM((SLOTS, *grid_rows[1:]), BF),
            pltpu.VMEM(grid_rows, BF),
            pltpu.VMEM((ROWS_IN, *grid_rows[1:]), BF),
            pltpu.VMEM((1152, 1152), BF),
            pltpu.VMEM((D, FF), BF),
            pltpu.VMEM((D, FF), BF),
            pltpu.VMEM((FF, D), BF),
            pltpu.VMEM((2, TOK, HALF), BF),
            pltpu.VMEM((CHUNKS, CHIP, CW), BF),
            pltpu.VMEM((2, 2, TOK, CW), BF),
            pltpu.VMEM((2, LEN, 128), BF),
            DMA((2,)),
            DMA((CHUNKS, 2)),
            DMA((3,)),
            DMA((2,)),
            *[one, one, ring, ring, ring, ring, one, one],
            *[phase] * 8,
            *[one, one, ring, ring, one, one],
            *[DMA((CHUNKS, 2))] * 4,
        ],
        compiler_params=pltpu.CompilerParams(
            collective_id=2, has_side_effects=True, vmem_limit_bytes=63 * 2**20
        ),
        name="moe",
    )(queries, packed, w_uk, w_uv, w_o, stream, w_gate, w_up, w_down, gain)


def local(
    stream_in,
    queries,
    latents,
    key_rope,
    w_uk,
    w_uv,
    w_o,
    norm_gain,
    expert_ids,
    gate_weights,
    w_gate,
    w_up,
    w_down,
):
    packed = jnp.concatenate(
        [latents[0], key_rope[0], expert_ids[0].astype(BF), gate_weights[0].astype(BF), jnp.zeros((TOK, 52), BF)],
        axis=1,
    )
    blocks = w_o.reshape(RING, RING, 64, D)
    out = moe_call(
        queries[0],
        packed,
        w_uk,
        w_uv,
        blocks,
        stream_in[0],
        w_gate[0],
        w_up[0],
        w_down[0],
        norm_gain.reshape(2 * CHUNKS, CW),
    )
    return out[None]


def solution(mesh):
    return jax.shard_map(
        local,
        mesh=mesh,
        in_specs=(
            P("exp", "ctx", None),
            P("exp", "ctx", None),
            P("exp", "ctx", None),
            P("exp", "ctx", None),
            P(None, "ctx"),
            P(None, "ctx"),
            P("ctx", None),
            P(),
            P("exp", "ctx", None),
            P("exp", "ctx", None),
            P(("ctx", "exp"), None, None),
            P(("ctx", "exp"), None, None),
            P(("ctx", "exp"), None, None),
        ),
        out_specs=P("exp", "ctx", None),
        check_vma=False,
    )
```

```python
import functools
import math

import jax
import jax.numpy as jnp
from jax import lax
from jax.experimental import pallas as pl
from jax.experimental.pallas import tpu as pltpu
from jax.sharding import PartitionSpec as P

NOPE = 128
ROPE = 64
VDIM = 128
KVL = 512
D = 2560
FF = 768
TOPK = 6
CAP = 9
TOK = 128
LEN = 1024
QW = 1536
RING = 4
ROWS = 72
CHUNKS = 10
CW = 128
SLOTS = 4
ROWS_IN = 5
HALF = 1280
CHIP = 256
LATW = 640
MESH = pl.DeviceIdType.MESH
BF = jnp.bfloat16
F32 = jnp.float32
ANY = pl.BlockSpec(memory_space=pl.ANY)
VM = pl.BlockSpec(memory_space=pltpu.VMEM)
DMA = pltpu.SemaphoreType.DMA


def place():
    c = lax.axis_index("ctx")
    e = lax.axis_index("exp")
    return c // 2, c % 2, e // RING, e % RING


def device(y, core, z, x):
    return (y * 2 + core, z * RING + x)


def step(v, d):
    return lax.rem(v + d, RING)


def remote(src, dst, send, recv, target):
    return pltpu.make_async_remote_copy(
        src_ref=src, dst_ref=dst, send_sem=send, recv_sem=recv, device_id=target, device_id_type=MESH
    )


def greet(targets, meanwhile):
    barrier = pltpu.get_barrier_semaphore()
    for target in targets:
        pl.semaphore_signal(barrier, inc=1, device_id=target, device_id_type=MESH)
    meanwhile()
    pl.semaphore_wait(barrier, len(targets))


def exp_targets(y, core, z, x):
    found = [device(y, 1 - core, z, x)]
    for d in (1, 2, 3):
        found.append(device(step(y, d), core, z, x))
        found.append(device(y, core, step(z, d), x))
        found.append(device(y, core, z, step(x, d)))
    return found


def first_phase(j, spot, src, mid, send, recv, own):
    y, core, z, x = spot
    cut = lax.rem(j, SLOTS)
    copies = []
    for d in (1, 3, 2):
        xx, zz = step(x, d), step(z, d)
        copies.append(
            remote(src.at[cut, 0, :, xx], mid.at[j, 0, x], send.at[j, d], recv.at[j, d], device(y, core, z, xx))
        )
        copies.append(
            remote(
                src.at[cut, 1, zz], mid.at[j, 1, z], send.at[j, 3 + d], recv.at[j, 3 + d], device(y, core, zz, x)
            )
        )
    copies.append(pltpu.make_async_copy(src.at[cut, 0, :, x], mid.at[j, 0, x], own.at[j, 0]))
    copies.append(pltpu.make_async_copy(src.at[cut, 1, z], mid.at[j, 1, z], own.at[j, 1]))
    return copies


def second_phase(j, spot, mid, dst, cut, send, recv, own):
    y, core, z, x = spot
    copies = []
    for d in (1, 3, 2):
        xx, zz = step(x, d), step(z, d)
        copies.append(
            remote(mid.at[j, 0, :, zz], dst.at[cut, 0, z], send.at[j, d], recv.at[j, d], device(y, core, zz, x))
        )
        copies.append(
            remote(
                mid.at[j, 1, :, xx],
                dst.at[cut, 1, :, x],
                send.at[j, 3 + d],
                recv.at[j, 3 + d],
                device(y, core, z, xx),
            )
        )
    copies.append(pltpu.make_async_copy(mid.at[j, 0, :, z], dst.at[cut, 0, z], own.at[j, 0]))
    copies.append(pltpu.make_async_copy(mid.at[j, 1, :, x], dst.at[cut, 1, :, x], own.at[j, 1]))
    return copies


def pipeline(stages):
    def turn(t, carry):
        for lag, stage in reversed(stages):
            j = t - lag

            @pl.when((j >= 0) & (j < CHUNKS))
            def _(stage=stage, j=j):
                stage(j)

        return carry

    lax.fori_loop(0, CHUNKS + stages[-1][0], turn, 0)


def start_all(copies):
    for copy in copies:
        copy.start()


def wait_all(copies):
    for copy in copies:
        copy.wait()


def moe_kernel(
    q_hbm, lat_hbm, uk_hbm, uv_hbm, wo_hbm, stream_hbm, wg_hbm, wu_hbm, wd_hbm,
    gain_ref, rope_ref, ids_ref, gates_ref, out_ref,
    qbuf, lat, turned, q_send, q_recv, l_send, l_recv, own_sem,
    mixed, late, p_own, p_sib, r_core, rs_buf, hbuf, gs, t1, xbuf, pickers, wg, wu, wd, sx, hown, swap, spots,
    in_sem, wo_sem, w_sem, st_sem, c1_s, c1_r, rs_s, rs_r, ag_s, ag_r, c2_s, c2_r, p1_s, p1_r, p2_s, p2_r,
    d1_s, d1_r, d2_s, d2_r, c3_s, c3_r, fs_s, fs_r, sw_s, sw_r, o1, o2, o3, o4,
):
    spot = place()
    y, core, z, x = spot
    sibling = device(y, 1 - core, z, x)

    def columns(half, j):
        return pl.ds(pl.multiple_of(half * HALF + j * CW, 128), CW)

    def wo_copy(j, side):
        half = core if side == 0 else 1 - core
        return pltpu.make_async_copy(
            wo_hbm.at[:, :, :, columns(half, j)], late.at[j, side, :, :, 0:64], wo_sem.at[j, side]
        )

    def half_of(which):
        return pl.ds(pl.multiple_of(which * HALF, 128), HALF)

    stream_copy = pltpu.make_async_copy(stream_hbm.at[:, half_of(core)], sx.at[core], in_sem.at[1])
    weights = [
        pltpu.make_async_copy(wg_hbm, wg, w_sem.at[0]),
        pltpu.make_async_copy(wu_hbm, wu, w_sem.at[1]),
        pltpu.make_async_copy(wd_hbm, wd, w_sem.at[2]),
    ]
    me = y * 2 + core

    def lat_copy(dy):
        return remote(lat.at[me], lat.at[me], l_send.at[dy], l_recv.at[dy], device(step(y, dy), core, z, x))

    def lat_share(dy):
        block = lat.at[step(y, dy) * 2 + core]
        return remote(block, block, l_send.at[4 + dy], l_recv.at[4 + dy], device(y, 1 - core, z, x))

    def q_copy(dy, dc):
        i = dy * 2 + dc
        yy, cc = step(y, dy), lax.rem(core + dc, 2)
        columns = pl.ds(pl.multiple_of((yy * 2 + cc) * QW, 128), QW)
        return remote(q_hbm.at[:, columns], qbuf.at[me], q_send.at[i], q_recv.at[i], device(yy, cc, z, x))

    peers = [(dy, dc) for dy in (0, 1, 3, 2) for dc in (0, 1) if (dy, dc) != (0, 0)]
    own_lat = pltpu.make_async_copy(lat_hbm, lat.at[me, :, 0:KVL], own_sem.at[0])
    own_q = pltpu.make_async_copy(
        q_hbm.at[:, pl.ds(pl.multiple_of(me * QW, 128), QW)], qbuf.at[me], own_sem.at[1]
    )
    own_lat.start()
    own_q.start()

    def pack_side():
        turned[...] = jnp.zeros((128, TOK), F32)
        turned[0:ROPE, :] = rope_ref[...].astype(F32)
        for k in range(TOPK):
            turned[ROPE + k : ROPE + k + 1, :] = ids_ref[k].astype(F32)
            turned[ROPE + TOPK + k : ROPE + TOPK + k + 1, :] = gates_ref[k]
        lat[me, :, KVL:LATW] = jnp.transpose(turned[...]).astype(BF)
        own_lat.wait()

    greet(
        exp_targets(y, core, z, x) + [device(step(y, d), 1 - core, z, x) for d in (1, 2, 3)], pack_side
    )
    for dy in (1, 3, 2):
        lat_copy(dy).start()
    for dy, dc in peers:
        q_copy(dy, dc).start()
    stream_copy.start()

    def load_wo(j, carry):
        for side in range(2):
            wo_copy(j, side).start()
        return carry

    stream_send = remote(
        stream_hbm.at[:, half_of(1 - core)], sx.at[core], st_sem.at[0], st_sem.at[1], sibling
    )
    stream_send.start()
    stream_copy.wait()

    def rows_of(which):
        return pl.ds(pl.multiple_of(which * CHIP, CHIP), CHIP)

    def core_sum(j, send, recv):
        slot = lax.rem(j, 2)
        return remote(p_sib.at[slot], r_core.at[slot], send.at[j], recv.at[j], sibling)

    def scatter(j, send, recv):
        return [
            remote(
                p_own.at[lax.rem(j, SLOTS), rows_of(step(y, d))],
                rs_buf.at[lax.rem(j, SLOTS), d - 1],
                send.at[j, d],
                recv.at[j, d],
                device(step(y, d), core, z, x),
            )
            for d in (1, 3, 2)
        ]

    def spread(j):
        block = hbuf.at[j, core, y, :, 0:64]
        return [
            remote(block, block, ag_s.at[j, d], ag_r.at[j, d], device(step(y, d), core, z, x))
            for d in (1, 3, 2)
        ]

    def core_share(j):
        block = hbuf.at[j, core, :, :, 0:64]
        return remote(block, block, c2_s.at[j], c2_r.at[j], sibling)

    def gather_row():
        row = lax.broadcasted_iota(jnp.int32, (1152, 128), 0)
        low = lax.broadcasted_iota(jnp.int32, (1152, 128), 1) * ROWS
        inside = (row >= low) & (row < low + ROWS)
        member = jnp.where(inside, 1.0, 0.0).astype(BF)
        at = jnp.sum(jnp.where(inside, row - low, 0).astype(F32), axis=1, keepdims=True)
        return member, at

    def route_spots():
        lane = lax.broadcasted_iota(jnp.int32, (TOK, 128), 1)
        first = ((y * 2 + core) * 16).astype(F32)
        wanted = jnp.where(lane < 16, lane.astype(F32) + first, -1.0)
        earlier = lax.broadcasted_iota(jnp.int32, (TOK, 128), 0) > lane
        earlier = jnp.where(earlier, 1.0, 0.0).astype(BF)
        for b in range(8):
            rows = slice(b * TOK, (b + 1) * TOK)
            route = lat[b, :, KVL:].astype(F32)
            named = jnp.zeros((TOK, 128), F32)
            gate = jnp.zeros((TOK, 128), F32)
            for k in range(TOPK):
                hit = route[:, 64 + k : 65 + k] == wanted
                named = jnp.where(hit, 1.0, named)
                gate = jnp.where(hit, route[:, 64 + TOPK + k : 65 + TOPK + k], gate)
            slot = jnp.dot(earlier, named.astype(BF), preferred_element_type=F32)
            spots[0, rows, :] = jnp.where(named > 0.0, slot + (b * CAP), -1.0).astype(BF)
            spots[1, rows, :] = gate.astype(BF)

    def pickers_in():
        member, at = gather_row()
        for b in range(RING):
            rows = slice(b * 288, (b + 1) * 288)
            wide = lax.dot_general(
                member[rows], spots[0], (((1,), (1,)), ((), ())), preferred_element_type=F32
            )
            pickers[rows, 0:LEN] = jnp.where(wide == at[rows], 1.0, 0.0).astype(BF)

    def pickers_out():
        low = lax.broadcasted_iota(jnp.int32, (128, 1152), 0) * ROWS
        row = lax.broadcasted_iota(jnp.int32, (128, 1152), 1)
        inside = (row >= low) & (row < low + ROWS)
        member = jnp.where(inside, 1.0, 0.0).astype(BF)
        at = jnp.sum(jnp.where(inside, row - low, 0).astype(F32), axis=0, keepdims=True)
        for b in range(RING):
            rows = slice(b * CHIP, (b + 1) * CHIP)
            wide = jnp.dot(spots[0, rows, :], member, preferred_element_type=F32)
            gate = jnp.dot(spots[1, rows, :], member, preferred_element_type=F32)
            pickers[rows, :] = jnp.where(wide == at, gate, 0.0).astype(BF)

    def attention(kbuf, vbuf, uk_ref, uv_ref, u_sem):
        projections = [
            pltpu.make_async_copy(uk_hbm, uk_ref, u_sem.at[0]),
            pltpu.make_async_copy(uv_hbm, uv_ref, u_sem.at[1]),
        ]
        start_all(projections)
        lat_share(0).start()
        for dy in (1, 3, 2):
            lat_copy(4 - dy).wait_recv()
            lat_share(dy).start()
        for dy in (0, 1, 3, 2):
            lat_share(dy).wait()
        for dy in (1, 3, 2):
            lat_copy(dy).wait_send()
        own_q.wait()
        lax.fori_loop(0, CHUNKS, load_wo, 0)
        start_all(weights)

        wait_all(projections)
        lane = lax.broadcasted_iota(jnp.int32, (CHIP, 128), 1)

        def project(b, carry):
            rows = pl.ds(pl.multiple_of(b * CHIP, CHIP), CHIP)
            block = lat[pl.ds(b * 2, 2)].reshape(CHIP, LATW)
            latent = block[:, :KVL]
            rope = block[:, KVL:].astype(F32)
            rope_low = jnp.where(lane < 64, rope, 0.0).astype(BF)
            rope_high = pltpu.roll(rope, 64, 1)
            for h in range(8):
                nope = jnp.dot(latent, uk_ref[:, h * 128 : h * 128 + 128], preferred_element_type=F32)
                if h % 2 == 0:
                    kbuf[h, rows, 0:128] = nope.astype(BF)
                    kbuf[h, rows, 128:256] = rope_low
                else:
                    turned = pltpu.roll(nope, 64, 1)
                    kbuf[h, rows, 0:128] = jnp.where(lane < 64, 0.0, turned).astype(BF)
                    kbuf[h, rows, 128:256] = jnp.where(lane < 64, turned, rope_high).astype(BF)
            vbuf[rows, :] = jnp.dot(latent, uv_ref[...], preferred_element_type=F32).astype(BF)
            return carry

        lax.fori_loop(0, RING, project, 0)

        route_spots()
        pickers_in()
        factor = 1.0 / math.sqrt(NOPE + ROPE) * math.log2(math.e)
        row_at = lax.broadcasted_iota(jnp.int32, (CHIP, CHIP), 0)
        col_at = lax.broadcasted_iota(jnp.int32, (CHIP, CHIP), 1)
        causal = row_at >= col_at

        def attend(block):
            length = (block + 1) * CHIP

            def pair(p, carry):
                columns = pl.ds(pl.multiple_of(p * 384, 128), 384)
                q = qbuf[block * 2 : block * 2 + 2, :, columns].reshape(CHIP, 384)
                outs = []
                for odd in range(2):
                    query = q[:, odd * 128 : odd * 128 + 256]
                    head = p * 2 + odd
                    contract = (((1,), (1,)), ((), ()))
                    last = lax.dot_general(
                        query, kbuf[head, length - CHIP : length], contract, preferred_element_type=F32
                    )
                    last = jnp.where(causal, last, -jnp.inf)
                    peak = jnp.max(last, axis=1, keepdims=True)
                    if block:
                        first = lax.dot_general(
                            query, kbuf[head, 0 : length - CHIP], contract, preferred_element_type=F32
                        )
                        peak = jnp.maximum(peak, jnp.max(first, axis=1, keepdims=True))
                    values = pl.ds(pl.multiple_of(head * 128, 128), 128)
                    weight = jnp.exp2((last - peak) * factor)
                    total = jnp.sum(weight, axis=1, keepdims=True)
                    result = jnp.dot(
                        weight.astype(BF), vbuf[length - CHIP : length, values], preferred_element_type=F32
                    )
                    if block:
                        weight = jnp.exp2((first - peak) * factor)
                        total += jnp.sum(weight, axis=1, keepdims=True)
                        result += jnp.dot(
                            weight.astype(BF), vbuf[0 : length - CHIP, values], preferred_element_type=F32
                        )
                    outs.append((result / total).astype(BF))
                mixed[block * CHIP : (block + 1) * CHIP, pl.ds(pl.multiple_of(p * 256, 256), 256)] = (
                    jnp.concatenate(outs, axis=1)
                )
                return carry

            lax.fori_loop(0, 4, pair, 0)

        for dy in (0, 1, 3, 2):
            for dc in range(2):
                if (dy, dc) != (0, 0):
                    q_copy((4 - dy) % 4, dc).wait_recv()
            source = lax.rem(y + dy, RING)
            for block in range(RING):
                pl.when(source == block)(functools.partial(attend, block))
        for dy, dc in peers:
            q_copy(dy, dc).wait_send()

    pl.run_scoped(
        attention,
        pltpu.VMEM((8, LEN, 256), BF),
        pltpu.VMEM((LEN, 1024), BF),
        pltpu.VMEM((KVL, 1024), BF),
        pltpu.VMEM((KVL, 1024), BF),
        DMA((2,)),
    )
    stream_send.wait()

    def experts(units, squares):
        def one(j):
            return first_phase(j, spot, gs, t1, p1_s, p1_r, o1)

        def two(j):
            return second_phase(j, spot, t1, xbuf, lax.rem(j, ROWS_IN), p2_s, p2_r, o2)

        def project(j):
            for side in range(2):
                wo_copy(j, side).wait()
            own = late[j, 0, :, :, 0:64].reshape(1024, CW)
            other = late[j, 1, :, :, 0:64].reshape(1024, CW)
            both = jnp.concatenate([own, other], axis=1)

            def block(b, carry):
                rows = rows_of(b)
                product = jnp.dot(mixed[rows, :], both, preferred_element_type=F32).astype(BF)
                p_own[lax.rem(j, SLOTS), rows] = product[:, :CW]
                p_sib[lax.rem(j, 2), rows] = product[:, CW:]
                return carry

            lax.fori_loop(0, RING, block, 0)
            core_sum(j, c1_s, c1_r).start()

        def add_core(j):
            core_sum(j, c1_s, c1_r).wait()
            slot = lax.rem(j, SLOTS)
            p_own[slot] = (p_own[slot].astype(F32) + r_core[lax.rem(j, 2)].astype(F32)).astype(BF)
            start_all(scatter(j, rs_s, rs_r))

        def chip_total(j):
            slot = lax.rem(j, SLOTS)
            total = p_own[slot, rows_of(y)].astype(F32)
            for i in range(3):
                total += rs_buf[slot, i].astype(F32)
            return total

        def finish_hidden(j):
            wait_all(scatter(j, rs_s, rs_r))
            stream = sx[:, :, pl.ds(pl.multiple_of(j * CW, 128), CW)].reshape(CHIP, CW)
            hidden = (stream.astype(F32) + chip_total(j)).astype(BF)
            hbuf[j, core, y, :, 0:64] = hidden.reshape(RING, 64, CW)
            hown[j] = hidden
            start_all(spread(j))

        def share(j):
            wait_all(spread(j))
            core_share(j).start()

        def pick(j):
            core_share(j).wait()
            both = jnp.concatenate(
                [hbuf[j, half, :, :, 0:64].reshape(1024, CW) for half in range(2)], axis=1
            )

            def block(b, carry):
                left = pickers[pl.ds(pl.multiple_of(b * 288, 16), 288), 0:LEN]
                picked = jnp.dot(left, both, preferred_element_type=F32).reshape(RING, ROWS, 2 * CW)
                gs[lax.rem(j, SLOTS), 0, b] = picked[:, :, :CW].astype(BF)
                gs[lax.rem(j, SLOTS), 1, b] = picked[:, :, CW:].astype(BF)
                return carry

            lax.fori_loop(0, RING, block, 0)
            start_all(one(j))

        def forward(j):
            wait_all(one(j))
            start_all(two(j))

        def drain(j):
            wait_all(two(j))

            @pl.when(j == 0)
            def _():
                wait_all(weights)

            gains = [gain_ref[pl.ds(half * CHUNKS + j, 1), :] for half in range(2)]
            firsts = [pl.ds(pl.multiple_of(half * HALF + j * CW, 128), CW) for half in range(2)]
            right_gate = jnp.concatenate([wg[rows, :] for rows in firsts], axis=0)
            right_up = jnp.concatenate([wu[rows, :] for rows in firsts], axis=0)

            def block(b, carry):
                rows = pl.ds(pl.multiple_of(b * 288, 16), 288)
                parts = [xbuf[lax.rem(j, ROWS_IN), half, b].astype(F32).reshape(288, CW) for half in range(2)]
                squares[rows, :] += parts[0] * parts[0] + parts[1] * parts[1]
                left = jnp.concatenate([(p * g).astype(BF) for p, g in zip(parts, gains)], axis=1)
                units[rows, 0:FF] += jnp.dot(left, right_gate, preferred_element_type=F32)
                units[rows, FF : 2 * FF] += jnp.dot(left, right_up, preferred_element_type=F32)
                return carry

            lax.fori_loop(0, RING, block, 0)

        def clear():
            units[...] = jnp.zeros((1152, 2 * FF), F32)
            squares[...] = jnp.zeros((1152, CW), F32)

        def prepare(j):
            pl.when(j == 2)(clear)

        pipeline(
            [
                (0, project),
                (1, add_core),
                (1, prepare),
                (3, finish_hidden),
                (5, share),
                (6, pick),
                (8, forward),
                (10, drain),
            ]
        )

        def hidden_units(b, carry):
            rows = pl.ds(pl.multiple_of(b * 144, 16), 144)
            total = jnp.sum(squares[rows, :], axis=1, keepdims=True)
            scale = lax.rsqrt(total * (1.0 / D) + 1e-06)
            gate = units[rows, 0:FF] * scale
            up = units[rows, FF : 2 * FF] * scale
            mixed[rows, 0:FF] = (gate / (1.0 + jnp.exp(-gate)) * up).astype(BF)
            return carry

        lax.fori_loop(0, 8, hidden_units, 0)

        def back_one(j):
            return first_phase(j, spot, gs, late, d1_s, d1_r, o3)

        def back_two(j):
            return second_phase(j, spot, late, hbuf, j, d2_s, d2_r, o4)

        def exchange(j):
            slot = lax.rem(j, 2)
            return remote(swap.at[slot, 0], swap.at[slot, 1], sw_s.at[j], sw_r.at[j], sibling)

        def down(j):
            both = jnp.concatenate([wd[:, columns(half, j)] for half in range(2)], axis=1)

            def block(b, carry):
                left = mixed[pl.ds(pl.multiple_of(b * 288, 16), 288), 0:FF]
                result = jnp.dot(left, both, preferred_element_type=F32).reshape(RING, ROWS, 2 * CW)
                gs[lax.rem(j, SLOTS), 0, b] = result[:, :, :CW].astype(BF)
                gs[lax.rem(j, SLOTS), 1, b] = result[:, :, CW:].astype(BF)
                return carry

            lax.fori_loop(0, RING, block, 0)
            start_all(back_one(j))

        def back_forward(j):
            wait_all(back_one(j))
            start_all(back_two(j))

        def combine(j):
            wait_all(back_two(j))
            both = jnp.concatenate(
                [
                    hbuf[j, core].astype(F32).reshape(1152, CW).astype(BF),
                    hbuf[j, 1 - core].astype(F32).reshape(1152, CW).astype(BF),
                ],
                axis=1,
            )

            def block(b, carry):
                rows = rows_of(b)
                product = jnp.dot(pickers[rows, :], both, preferred_element_type=F32).astype(BF)
                p_own[lax.rem(j, SLOTS), rows] = product[:, :CW]
                p_sib[lax.rem(j, 2), rows] = product[:, CW:]
                return carry

            lax.fori_loop(0, RING, block, 0)
            core_sum(j, c3_s, c3_r).start()

        def add_back(j):
            core_sum(j, c3_s, c3_r).wait()
            slot = lax.rem(j, SLOTS)
            p_own[slot] = (p_own[slot].astype(F32) + r_core[lax.rem(j, 2)].astype(F32)).astype(BF)
            start_all(scatter(j, fs_s, fs_r))

        def finish(j):
            wait_all(scatter(j, fs_s, fs_r))
            total = (hown[j].astype(F32) + chip_total(j)).astype(BF)
            swap[lax.rem(j, 2), 0] = jnp.where(core == 0, total[TOK:], total[:TOK])
            exchange(j).start()
            out_ref[:, columns(core, j)] = jnp.where(core == 0, total[:TOK], total[TOK:])

        def land(j):
            exchange(j).wait()
            out_ref[:, columns(1 - core, j)] = swap[lax.rem(j, 2), 1]

        def prepare_back(j):
            pl.when(j == 0)(pickers_out)

        pipeline(
            [
                (0, down),
                (1, prepare_back),
                (2, back_forward),
                (4, combine),
                (5, add_back),
                (7, finish),
                (8, land),
            ]
        )

    pl.run_scoped(experts, pltpu.VMEM((1152, 2 * FF), F32), pltpu.VMEM((1152, CW), F32))


def moe_call(queries, latents, w_uk, w_uv, w_o, stream, w_gate, w_up, w_down, gain, rope, ids, gates):
    grid_rows = (CHUNKS, 2, RING, RING, ROWS, CW)
    one = DMA((CHUNKS,))
    ring = DMA((CHUNKS, 4))
    phase = DMA((CHUNKS, 7))
    return pl.pallas_call(
        moe_kernel,
        out_shape=jax.ShapeDtypeStruct((TOK, D), BF),
        in_specs=[ANY] * 9 + [VM] * 4,
        out_specs=VM,
        scratch_shapes=[
            pltpu.VMEM((8, TOK, QW), BF),
            pltpu.VMEM((8, TOK, LATW), BF),
            pltpu.VMEM((128, TOK), F32),
            *[DMA((8,))] * 4,
            DMA((2,)),
            pltpu.VMEM((1152, 1024), BF),
            pltpu.VMEM(grid_rows, BF),
            pltpu.VMEM((SLOTS, LEN, CW), BF),
            pltpu.VMEM((2, LEN, CW), BF),
            pltpu.VMEM((2, LEN, CW), BF),
            pltpu.VMEM((SLOTS, 3, CHIP, CW), BF),
            pltpu.VMEM(grid_rows, BF),
            pltpu.VMEM((SLOTS, *grid_rows[1:]), BF),
            pltpu.VMEM(grid_rows, BF),
            pltpu.VMEM((ROWS_IN, *grid_rows[1:]), BF),
            pltpu.VMEM((1152, 1152), BF),
            pltpu.VMEM((D, FF), BF),
            pltpu.VMEM((D, FF), BF),
            pltpu.VMEM((FF, D), BF),
            pltpu.VMEM((2, TOK, HALF), BF),
            pltpu.VMEM((CHUNKS, CHIP, CW), BF),
            pltpu.VMEM((2, 2, TOK, CW), BF),
            pltpu.VMEM((2, LEN, 128), BF),
            DMA((2,)),
            DMA((CHUNKS, 2)),
            DMA((3,)),
            DMA((2,)),
            *[one, one, ring, ring, ring, ring, one, one],
            *[phase] * 8,
            *[one, one, ring, ring, one, one],
            *[DMA((CHUNKS, 2))] * 4,
        ],
        compiler_params=pltpu.CompilerParams(
            collective_id=2, has_side_effects=True, vmem_limit_bytes=63 * 2**20
        ),
        name="moe",
    )(queries, latents, w_uk, w_uv, w_o, stream, w_gate, w_up, w_down, gain, rope, ids, gates)


def local(
    stream_in,
    queries,
    latents,
    key_rope,
    w_uk,
    w_uv,
    w_o,
    norm_gain,
    expert_ids,
    gate_weights,
    w_gate,
    w_up,
    w_down,
):
    blocks = w_o.reshape(RING, RING, 64, D)
    out = moe_call(
        queries[0],
        latents[0],
        w_uk,
        w_uv,
        blocks,
        stream_in[0],
        w_gate[0],
        w_up[0],
        w_down[0],
        norm_gain.reshape(2 * CHUNKS, CW),
        key_rope[0].T,
        jnp.transpose(expert_ids, (2, 0, 1)),
        jnp.transpose(gate_weights, (2, 0, 1)),
    )
    return out[None]


def solution(mesh):
    return jax.shard_map(
        local,
        mesh=mesh,
        in_specs=(
            P("exp", "ctx", None),
            P("exp", "ctx", None),
            P("exp", "ctx", None),
            P("exp", "ctx", None),
            P(None, "ctx"),
            P(None, "ctx"),
            P("ctx", None),
            P(),
            P("exp", "ctx", None),
            P("exp", "ctx", None),
            P(("ctx", "exp"), None, None),
            P(("ctx", "exp"), None, None),
            P(("ctx", "exp"), None, None),
        ),
        out_specs=P("exp", "ctx", None),
        check_vma=False,
    )
```

```python
import functools
import math

import jax
import jax.numpy as jnp
from jax import lax
from jax.experimental import pallas as pl
from jax.experimental.pallas import tpu as pltpu
from jax.sharding import PartitionSpec as P

NOPE = 128
ROPE = 64
VDIM = 128
KVL = 512
D = 2560
FF = 768
TOPK = 6
CAP = 9
TOK = 128
LEN = 1024
QW = 1536
RING = 4
ROWS = 72
CHUNKS = 10
CW = 128
SLOTS = 4
ROWS_IN = 5
HALF = 1280
CHIP = 256
LATW = 640
MESH = pl.DeviceIdType.MESH
BF = jnp.bfloat16
F32 = jnp.float32
ANY = pl.BlockSpec(memory_space=pl.ANY)
VM = pl.BlockSpec(memory_space=pltpu.VMEM)
DMA = pltpu.SemaphoreType.DMA


def place():
    c = lax.axis_index("ctx")
    e = lax.axis_index("exp")
    return c // 2, c % 2, e // RING, e % RING


def device(y, core, z, x):
    return (y * 2 + core, z * RING + x)


def step(v, d):
    return lax.rem(v + d, RING)


def remote(src, dst, send, recv, target):
    return pltpu.make_async_remote_copy(
        src_ref=src, dst_ref=dst, send_sem=send, recv_sem=recv, device_id=target, device_id_type=MESH
    )


def greet(targets, meanwhile):
    barrier = pltpu.get_barrier_semaphore()
    for target in targets:
        pl.semaphore_signal(barrier, inc=1, device_id=target, device_id_type=MESH)
    meanwhile()
    pl.semaphore_wait(barrier, len(targets))


def exp_targets(y, core, z, x):
    found = [device(y, 1 - core, z, x)]
    for d in (1, 2, 3):
        found.append(device(step(y, d), core, z, x))
        found.append(device(y, core, step(z, d), x))
        found.append(device(y, core, z, step(x, d)))
    return found


def first_phase(j, spot, src, mid, send, recv, own):
    y, core, z, x = spot
    cut = lax.rem(j, SLOTS)
    copies = []
    for d in (1, 3, 2):
        xx, zz = step(x, d), step(z, d)
        copies.append(
            remote(src.at[cut, 0, :, xx], mid.at[j, 0, x], send.at[j, d], recv.at[j, d], device(y, core, z, xx))
        )
        copies.append(
            remote(
                src.at[cut, 1, zz], mid.at[j, 1, z], send.at[j, 3 + d], recv.at[j, 3 + d], device(y, core, zz, x)
            )
        )
    copies.append(pltpu.make_async_copy(src.at[cut, 0, :, x], mid.at[j, 0, x], own.at[j, 0]))
    copies.append(pltpu.make_async_copy(src.at[cut, 1, z], mid.at[j, 1, z], own.at[j, 1]))
    return copies


def second_phase(j, spot, mid, dst, cut, send, recv, own):
    y, core, z, x = spot
    copies = []
    for d in (1, 3, 2):
        xx, zz = step(x, d), step(z, d)
        copies.append(
            remote(mid.at[j, 0, :, zz], dst.at[cut, 0, z], send.at[j, d], recv.at[j, d], device(y, core, zz, x))
        )
        copies.append(
            remote(
                mid.at[j, 1, :, xx],
                dst.at[cut, 1, :, x],
                send.at[j, 3 + d],
                recv.at[j, 3 + d],
                device(y, core, z, xx),
            )
        )
    copies.append(pltpu.make_async_copy(mid.at[j, 0, :, z], dst.at[cut, 0, z], own.at[j, 0]))
    copies.append(pltpu.make_async_copy(mid.at[j, 1, :, x], dst.at[cut, 1, :, x], own.at[j, 1]))
    return copies


def pipeline(stages):
    def turn(t, carry):
        for lag, stage in reversed(stages):
            j = t - lag

            @pl.when((j >= 0) & (j < CHUNKS))
            def _(stage=stage, j=j):
                stage(j)

        return carry

    lax.fori_loop(0, CHUNKS + stages[-1][0], turn, 0)


def start_all(copies):
    for copy in copies:
        copy.start()


def wait_all(copies):
    for copy in copies:
        copy.wait()


def moe_kernel(
    q_hbm, lat_hbm, uk_hbm, uv_hbm, wo_hbm, stream_hbm, wg_hbm, wu_hbm, wd_hbm,
    gain_ref, rope_ref, ids_ref, gates_ref, out_ref,
    qbuf, lat, turned, q_send, q_recv, l_send, l_recv, own_sem,
    mixed, late, p_own, p_sib, r_core, rs_buf, hbuf, gs, t1, xbuf, pickers, wg, wu, wd, sx, hown, fs_buf, spots,
    in_sem, wo_sem, w_sem, st_sem, c1_s, c1_r, rs_s, rs_r, ag_s, ag_r, c2_s, c2_r, p1_s, p1_r, p2_s, p2_r,
    d1_s, d1_r, d2_s, d2_r, c3_s, c3_r, fs_s, fs_r, o1, o2, o3, o4,
):
    spot = place()
    y, core, z, x = spot
    sibling = device(y, 1 - core, z, x)

    def columns(half, j):
        return pl.ds(pl.multiple_of(half * HALF + j * CW, 128), CW)

    def wo_copy(j, side):
        half = core if side == 0 else 1 - core
        return pltpu.make_async_copy(
            wo_hbm.at[:, :, :, columns(half, j)], late.at[j, side, :, :, 0:64], wo_sem.at[j, side]
        )

    def half_of(which):
        return pl.ds(pl.multiple_of(which * HALF, 128), HALF)

    stream_copy = pltpu.make_async_copy(stream_hbm.at[:, half_of(core)], sx.at[core], in_sem.at[1])
    weights = [
        pltpu.make_async_copy(wg_hbm, wg, w_sem.at[0]),
        pltpu.make_async_copy(wu_hbm, wu, w_sem.at[1]),
        pltpu.make_async_copy(wd_hbm, wd, w_sem.at[2]),
    ]
    me = y * 2 + core

    def lat_copy(dy):
        return remote(lat.at[me], lat.at[me], l_send.at[dy], l_recv.at[dy], device(step(y, dy), core, z, x))

    def lat_share(dy):
        block = lat.at[step(y, dy) * 2 + core]
        return remote(block, block, l_send.at[4 + dy], l_recv.at[4 + dy], device(y, 1 - core, z, x))

    def q_copy(dy, dc):
        i = dy * 2 + dc
        yy, cc = step(y, dy), lax.rem(core + dc, 2)
        columns = pl.ds(pl.multiple_of((yy * 2 + cc) * QW, 128), QW)
        return remote(q_hbm.at[:, columns], qbuf.at[me], q_send.at[i], q_recv.at[i], device(yy, cc, z, x))

    peers = [(dy, dc) for dy in (0, 1, 3, 2) for dc in (0, 1) if (dy, dc) != (0, 0)]
    own_lat = pltpu.make_async_copy(lat_hbm, lat.at[me, :, 0:KVL], own_sem.at[0])
    own_q = pltpu.make_async_copy(
        q_hbm.at[:, pl.ds(pl.multiple_of(me * QW, 128), QW)], qbuf.at[me], own_sem.at[1]
    )
    own_lat.start()
    own_q.start()

    def pack_side():
        turned[...] = jnp.zeros((128, TOK), F32)
        turned[0:ROPE, :] = rope_ref[...].astype(F32)
        for k in range(TOPK):
            turned[ROPE + k : ROPE + k + 1, :] = ids_ref[k].astype(F32)
            turned[ROPE + TOPK + k : ROPE + TOPK + k + 1, :] = gates_ref[k]
        lat[me, :, KVL:LATW] = jnp.transpose(turned[...]).astype(BF)
        own_lat.wait()

    greet(
        exp_targets(y, core, z, x) + [device(step(y, d), 1 - core, z, x) for d in (1, 2, 3)], pack_side
    )
    for dy in (1, 3, 2):
        lat_copy(dy).start()
    for dy, dc in peers:
        q_copy(dy, dc).start()
    stream_copy.start()

    def load_wo(j, carry):
        for side in range(2):
            wo_copy(j, side).start()
        return carry

    stream_send = remote(
        stream_hbm.at[:, half_of(1 - core)], sx.at[core], st_sem.at[0], st_sem.at[1], sibling
    )
    stream_send.start()
    stream_copy.wait()

    def rows_of(which):
        return pl.ds(pl.multiple_of(which * CHIP, CHIP), CHIP)

    def core_sum(j, send, recv):
        slot = lax.rem(j, 2)
        return remote(p_sib.at[slot], r_core.at[slot], send.at[j], recv.at[j], sibling)

    def scatter(j, send, recv):
        return [
            remote(
                p_own.at[lax.rem(j, SLOTS), rows_of(step(y, d))],
                rs_buf.at[lax.rem(j, SLOTS), d - 1],
                send.at[j, d],
                recv.at[j, d],
                device(step(y, d), core, z, x),
            )
            for d in (1, 3, 2)
        ]

    def spread(j):
        block = hbuf.at[j, core, y, :, 0:64]
        return [
            remote(block, block, ag_s.at[j, d], ag_r.at[j, d], device(step(y, d), core, z, x))
            for d in (1, 3, 2)
        ]

    def core_share(j):
        block = hbuf.at[j, core, :, :, 0:64]
        return remote(block, block, c2_s.at[j], c2_r.at[j], sibling)

    def gather_row():
        row = lax.broadcasted_iota(jnp.int32, (1152, 128), 0)
        low = lax.broadcasted_iota(jnp.int32, (1152, 128), 1) * ROWS
        inside = (row >= low) & (row < low + ROWS)
        member = jnp.where(inside, 1.0, 0.0).astype(BF)
        at = jnp.sum(jnp.where(inside, row - low, 0).astype(F32), axis=1, keepdims=True)
        return member, at

    def route_spots():
        lane = lax.broadcasted_iota(jnp.int32, (TOK, 128), 1)
        first = ((y * 2 + core) * 16).astype(F32)
        wanted = jnp.where(lane < 16, lane.astype(F32) + first, -1.0)
        earlier = lax.broadcasted_iota(jnp.int32, (TOK, 128), 0) > lane
        earlier = jnp.where(earlier, 1.0, 0.0).astype(BF)
        for b in range(8):
            rows = slice(b * TOK, (b + 1) * TOK)
            route = lat[b, :, KVL:].astype(F32)
            named = jnp.zeros((TOK, 128), F32)
            gate = jnp.zeros((TOK, 128), F32)
            for k in range(TOPK):
                hit = route[:, 64 + k : 65 + k] == wanted
                named = jnp.where(hit, 1.0, named)
                gate = jnp.where(hit, route[:, 64 + TOPK + k : 65 + TOPK + k], gate)
            slot = jnp.dot(earlier, named.astype(BF), preferred_element_type=F32)
            spots[0, rows, :] = jnp.where(named > 0.0, slot + (b * CAP), -1.0).astype(BF)
            spots[1, rows, :] = gate.astype(BF)

    def pickers_in():
        member, at = gather_row()
        for b in range(RING):
            rows = slice(b * 288, (b + 1) * 288)
            wide = lax.dot_general(
                member[rows], spots[0], (((1,), (1,)), ((), ())), preferred_element_type=F32
            )
            pickers[rows, 0:LEN] = jnp.where(wide == at[rows], 1.0, 0.0).astype(BF)

    def pickers_out():
        low = lax.broadcasted_iota(jnp.int32, (128, 1152), 0) * ROWS
        row = lax.broadcasted_iota(jnp.int32, (128, 1152), 1)
        inside = (row >= low) & (row < low + ROWS)
        member = jnp.where(inside, 1.0, 0.0).astype(BF)
        at = jnp.sum(jnp.where(inside, row - low, 0).astype(F32), axis=0, keepdims=True)
        for b in range(RING):
            rows = slice(b * CHIP, (b + 1) * CHIP)
            wide = jnp.dot(spots[0, rows, :], member, preferred_element_type=F32)
            gate = jnp.dot(spots[1, rows, :], member, preferred_element_type=F32)
            pickers[rows, :] = jnp.where(wide == at, gate, 0.0).astype(BF)

    def attention(kbuf, vbuf, uk_ref, uv_ref, u_sem):
        projections = [
            pltpu.make_async_copy(uk_hbm, uk_ref, u_sem.at[0]),
            pltpu.make_async_copy(uv_hbm, uv_ref, u_sem.at[1]),
        ]
        start_all(projections)
        lat_share(0).start()
        for dy in (1, 3, 2):
            lat_copy(4 - dy).wait_recv()
            lat_share(dy).start()
        for dy in (0, 1, 3, 2):
            lat_share(dy).wait()
        for dy in (1, 3, 2):
            lat_copy(dy).wait_send()
        own_q.wait()
        lax.fori_loop(0, CHUNKS, load_wo, 0)
        start_all(weights)

        wait_all(projections)
        lane = lax.broadcasted_iota(jnp.int32, (CHIP, 128), 1)

        def project(b, carry):
            rows = pl.ds(pl.multiple_of(b * CHIP, CHIP), CHIP)
            block = lat[pl.ds(b * 2, 2)].reshape(CHIP, LATW)
            latent = block[:, :KVL]
            rope = block[:, KVL:].astype(F32)
            rope_low = jnp.where(lane < 64, rope, 0.0).astype(BF)
            rope_high = pltpu.roll(rope, 64, 1)
            for h in range(8):
                nope = jnp.dot(latent, uk_ref[:, h * 128 : h * 128 + 128], preferred_element_type=F32)
                if h % 2 == 0:
                    kbuf[h, rows, 0:128] = nope.astype(BF)
                    kbuf[h, rows, 128:256] = rope_low
                else:
                    turned = pltpu.roll(nope, 64, 1)
                    kbuf[h, rows, 0:128] = jnp.where(lane < 64, 0.0, turned).astype(BF)
                    kbuf[h, rows, 128:256] = jnp.where(lane < 64, turned, rope_high).astype(BF)
            vbuf[rows, :] = jnp.dot(latent, uv_ref[...], preferred_element_type=F32).astype(BF)
            return carry

        lax.fori_loop(0, RING, project, 0)

        route_spots()
        pickers_in()
        factor = 1.0 / math.sqrt(NOPE + ROPE) * math.log2(math.e)
        row_at = lax.broadcasted_iota(jnp.int32, (CHIP, CHIP), 0)
        col_at = lax.broadcasted_iota(jnp.int32, (CHIP, CHIP), 1)
        causal = row_at >= col_at

        def attend(block):
            length = (block + 1) * CHIP

            def pair(p, carry):
                columns = pl.ds(pl.multiple_of(p * 384, 128), 384)
                q = qbuf[block * 2 : block * 2 + 2, :, columns].reshape(CHIP, 384)
                outs = []
                for odd in range(2):
                    query = q[:, odd * 128 : odd * 128 + 256]
                    head = p * 2 + odd
                    contract = (((1,), (1,)), ((), ()))
                    last = lax.dot_general(
                        query, kbuf[head, length - CHIP : length], contract, preferred_element_type=F32
                    )
                    last = jnp.where(causal, last, -jnp.inf)
                    peak = jnp.max(last, axis=1, keepdims=True)
                    if block:
                        first = lax.dot_general(
                            query, kbuf[head, 0 : length - CHIP], contract, preferred_element_type=F32
                        )
                        peak = jnp.maximum(peak, jnp.max(first, axis=1, keepdims=True))
                    values = pl.ds(pl.multiple_of(head * 128, 128), 128)
                    weight = jnp.exp2((last - peak) * factor)
                    total = jnp.sum(weight, axis=1, keepdims=True)
                    result = jnp.dot(
                        weight.astype(BF), vbuf[length - CHIP : length, values], preferred_element_type=F32
                    )
                    if block:
                        weight = jnp.exp2((first - peak) * factor)
                        total += jnp.sum(weight, axis=1, keepdims=True)
                        result += jnp.dot(
                            weight.astype(BF), vbuf[0 : length - CHIP, values], preferred_element_type=F32
                        )
                    outs.append((result / total).astype(BF))
                mixed[block * CHIP : (block + 1) * CHIP, pl.ds(pl.multiple_of(p * 256, 256), 256)] = (
                    jnp.concatenate(outs, axis=1)
                )
                return carry

            lax.fori_loop(0, 4, pair, 0)

        for dy in (0, 1, 3, 2):
            for dc in range(2):
                if (dy, dc) != (0, 0):
                    q_copy((4 - dy) % 4, dc).wait_recv()
            source = lax.rem(y + dy, RING)
            for block in range(RING):
                pl.when(source == block)(functools.partial(attend, block))
        for dy, dc in peers:
            q_copy(dy, dc).wait_send()

    pl.run_scoped(
        attention,
        pltpu.VMEM((8, LEN, 256), BF),
        pltpu.VMEM((LEN, 1024), BF),
        pltpu.VMEM((KVL, 1024), BF),
        pltpu.VMEM((KVL, 1024), BF),
        DMA((2,)),
    )
    stream_send.wait()

    def experts(units, squares):
        def one(j):
            return first_phase(j, spot, gs, t1, p1_s, p1_r, o1)

        def two(j):
            return second_phase(j, spot, t1, xbuf, lax.rem(j, ROWS_IN), p2_s, p2_r, o2)

        def project(j):
            for side in range(2):
                wo_copy(j, side).wait()
            own = late[j, 0, :, :, 0:64].reshape(1024, CW)
            other = late[j, 1, :, :, 0:64].reshape(1024, CW)
            both = jnp.concatenate([own, other], axis=1)

            def block(b, carry):
                rows = rows_of(b)
                product = jnp.dot(mixed[rows, :], both, preferred_element_type=F32).astype(BF)
                p_own[lax.rem(j, SLOTS), rows] = product[:, :CW]
                p_sib[lax.rem(j, 2), rows] = product[:, CW:]
                return carry

            lax.fori_loop(0, RING, block, 0)
            core_sum(j, c1_s, c1_r).start()

        def add_core(j):
            core_sum(j, c1_s, c1_r).wait()
            slot = lax.rem(j, SLOTS)
            p_own[slot] = (p_own[slot].astype(F32) + r_core[lax.rem(j, 2)].astype(F32)).astype(BF)
            start_all(scatter(j, rs_s, rs_r))

        def chip_total(j):
            slot = lax.rem(j, SLOTS)
            total = p_own[slot, rows_of(y)].astype(F32)
            for i in range(3):
                total += rs_buf[slot, i].astype(F32)
            return total

        def finish_hidden(j):
            wait_all(scatter(j, rs_s, rs_r))
            stream = sx[:, :, pl.ds(pl.multiple_of(j * CW, 128), CW)].reshape(CHIP, CW)
            hidden = (stream.astype(F32) + chip_total(j)).astype(BF)
            hbuf[j, core, y, :, 0:64] = hidden.reshape(RING, 64, CW)
            start_all(spread(j))

        def share(j):
            wait_all(spread(j))
            core_share(j).start()

        def pick(j):
            core_share(j).wait()
            for side, half in enumerate((core, 1 - core)):
                hown[j, side] = hbuf[j, half, y, pl.ds(core * 2, 2), 0:64].reshape(TOK, CW)
            both = jnp.concatenate(
                [hbuf[j, half, :, :, 0:64].reshape(1024, CW) for half in range(2)], axis=1
            )

            def block(b, carry):
                left = pickers[pl.ds(pl.multiple_of(b * 288, 16), 288), 0:LEN]
                picked = jnp.dot(left, both, preferred_element_type=F32).reshape(RING, ROWS, 2 * CW)
                gs[lax.rem(j, SLOTS), 0, b] = picked[:, :, :CW].astype(BF)
                gs[lax.rem(j, SLOTS), 1, b] = picked[:, :, CW:].astype(BF)
                return carry

            lax.fori_loop(0, RING, block, 0)
            start_all(one(j))

        def forward(j):
            wait_all(one(j))
            start_all(two(j))

        def drain(j):
            wait_all(two(j))

            @pl.when(j == 0)
            def _():
                wait_all(weights)

            gains = [gain_ref[pl.ds(half * CHUNKS + j, 1), :] for half in range(2)]
            firsts = [pl.ds(pl.multiple_of(half * HALF + j * CW, 128), CW) for half in range(2)]
            right_gate = jnp.concatenate([wg[rows, :] for rows in firsts], axis=0)
            right_up = jnp.concatenate([wu[rows, :] for rows in firsts], axis=0)

            def block(b, carry):
                rows = pl.ds(pl.multiple_of(b * 288, 16), 288)
                parts = [xbuf[lax.rem(j, ROWS_IN), half, b].astype(F32).reshape(288, CW) for half in range(2)]
                squares[rows, :] += parts[0] * parts[0] + parts[1] * parts[1]
                left = jnp.concatenate([(p * g).astype(BF) for p, g in zip(parts, gains)], axis=1)
                units[rows, 0:FF] += jnp.dot(left, right_gate, preferred_element_type=F32)
                units[rows, FF : 2 * FF] += jnp.dot(left, right_up, preferred_element_type=F32)
                return carry

            lax.fori_loop(0, RING, block, 0)

        def clear():
            units[...] = jnp.zeros((1152, 2 * FF), F32)
            squares[...] = jnp.zeros((1152, CW), F32)

        def prepare(j):
            pl.when(j == 2)(clear)

        pipeline(
            [
                (0, project),
                (1, add_core),
                (1, prepare),
                (3, finish_hidden),
                (5, share),
                (6, pick),
                (8, forward),
                (10, drain),
            ]
        )

        def hidden_units(b, carry):
            rows = pl.ds(pl.multiple_of(b * 144, 16), 144)
            total = jnp.sum(squares[rows, :], axis=1, keepdims=True)
            scale = lax.rsqrt(total * (1.0 / D) + 1e-06)
            gate = units[rows, 0:FF] * scale
            up = units[rows, FF : 2 * FF] * scale
            mixed[rows, 0:FF] = (gate / (1.0 + jnp.exp(-gate)) * up).astype(BF)
            return carry

        lax.fori_loop(0, 8, hidden_units, 0)

        def back_one(j):
            return first_phase(j, spot, gs, late, d1_s, d1_r, o3)

        def back_two(j):
            return second_phase(j, spot, late, hbuf, j, d2_s, d2_r, o4)

        def gather_back(j):
            slot = lax.rem(j, SLOTS)
            copies = []
            for i, (dy, dc) in enumerate(peers):
                yy, cc = step(y, dy), lax.rem(core + dc, 2)
                rows = pl.ds(pl.multiple_of((yy * 2 + cc) * TOK, TOK), TOK)
                copies.append(
                    remote(
                        p_own.at[slot, rows],
                        fs_buf.at[slot, i],
                        fs_s.at[j, i],
                        fs_r.at[j, i],
                        device(yy, cc, z, x),
                    )
                )
            return copies

        def down(j):
            both = jnp.concatenate([wd[:, columns(half, j)] for half in range(2)], axis=1)

            def block(b, carry):
                left = mixed[pl.ds(pl.multiple_of(b * 288, 16), 288), 0:FF]
                result = jnp.dot(left, both, preferred_element_type=F32).reshape(RING, ROWS, 2 * CW)
                gs[lax.rem(j, SLOTS), 0, b] = result[:, :, :CW].astype(BF)
                gs[lax.rem(j, SLOTS), 1, b] = result[:, :, CW:].astype(BF)
                return carry

            lax.fori_loop(0, RING, block, 0)
            start_all(back_one(j))

        def back_forward(j):
            wait_all(back_one(j))
            start_all(back_two(j))

        def combine(j):
            wait_all(back_two(j))
            both = jnp.concatenate(
                [
                    hbuf[j, core].astype(F32).reshape(1152, CW).astype(BF),
                    hbuf[j, 1 - core].astype(F32).reshape(1152, CW).astype(BF),
                ],
                axis=1,
            )

            def block(b, carry):
                rows = rows_of(b)
                product = jnp.dot(pickers[rows, :], both, preferred_element_type=F32).astype(BF)
                p_own[lax.rem(j, SLOTS), rows] = product[:, :CW]
                p_sib[lax.rem(j, 2), rows] = product[:, CW:]
                return carry

            lax.fori_loop(0, RING, block, 0)
            core_sum(j, c3_s, c3_r).start()

        def add_back(j):
            core_sum(j, c3_s, c3_r).wait()
            slot = lax.rem(j, SLOTS)
            p_own[slot] = (p_own[slot].astype(F32) + r_core[lax.rem(j, 2)].astype(F32)).astype(BF)
            start_all(gather_back(j))

        def finish(j):
            wait_all(gather_back(j))
            slot = lax.rem(j, SLOTS)
            mine = pl.ds(pl.multiple_of(me * TOK, TOK), TOK)
            totals = [p_own[slot, mine].astype(F32), jnp.zeros((TOK, CW), F32)]
            for i, (dy, dc) in enumerate(peers):
                totals[dc] += fs_buf[slot, i].astype(F32)
            for side, half in enumerate((core, 1 - core)):
                hidden = hown[j, side].astype(F32)
                out_ref[:, columns(half, j)] = (hidden + totals[side]).astype(BF)

        def prepare_back(j):
            pl.when(j == 0)(pickers_out)

        pipeline(
            [
                (0, down),
                (1, prepare_back),
                (2, back_forward),
                (4, combine),
                (5, add_back),
                (7, finish),
            ]
        )

    pl.run_scoped(experts, pltpu.VMEM((1152, 2 * FF), F32), pltpu.VMEM((1152, CW), F32))


def moe_call(queries, latents, w_uk, w_uv, w_o, stream, w_gate, w_up, w_down, gain, rope, ids, gates):
    grid_rows = (CHUNKS, 2, RING, RING, ROWS, CW)
    one = DMA((CHUNKS,))
    ring = DMA((CHUNKS, 4))
    phase = DMA((CHUNKS, 7))
    return pl.pallas_call(
        moe_kernel,
        out_shape=jax.ShapeDtypeStruct((TOK, D), BF),
        in_specs=[ANY] * 9 + [VM] * 4,
        out_specs=VM,
        scratch_shapes=[
            pltpu.VMEM((8, TOK, QW), BF),
            pltpu.VMEM((8, TOK, LATW), BF),
            pltpu.VMEM((128, TOK), F32),
            *[DMA((8,))] * 4,
            DMA((2,)),
            pltpu.VMEM((1152, 1024), BF),
            pltpu.VMEM(grid_rows, BF),
            pltpu.VMEM((SLOTS, LEN, CW), BF),
            pltpu.VMEM((2, LEN, CW), BF),
            pltpu.VMEM((2, LEN, CW), BF),
            pltpu.VMEM((SLOTS, 3, CHIP, CW), BF),
            pltpu.VMEM(grid_rows, BF),
            pltpu.VMEM((SLOTS, *grid_rows[1:]), BF),
            pltpu.VMEM(grid_rows, BF),
            pltpu.VMEM((ROWS_IN, *grid_rows[1:]), BF),
            pltpu.VMEM((1152, 1152), BF),
            pltpu.VMEM((D, FF), BF),
            pltpu.VMEM((D, FF), BF),
            pltpu.VMEM((FF, D), BF),
            pltpu.VMEM((2, TOK, HALF), BF),
            pltpu.VMEM((CHUNKS, 2, TOK, CW), BF),
            pltpu.VMEM((SLOTS, 7, TOK, CW), BF),
            pltpu.VMEM((2, LEN, 128), BF),
            DMA((2,)),
            DMA((CHUNKS, 2)),
            DMA((3,)),
            DMA((2,)),
            *[one, one, ring, ring, ring, ring, one, one],
            *[phase] * 8,
            *[one, one],
            *[DMA((CHUNKS, 7))] * 2,
            *[DMA((CHUNKS, 2))] * 4,
        ],
        compiler_params=pltpu.CompilerParams(
            collective_id=2, has_side_effects=True, vmem_limit_bytes=63 * 2**20
        ),
        name="moe",
    )(queries, latents, w_uk, w_uv, w_o, stream, w_gate, w_up, w_down, gain, rope, ids, gates)


def local(
    stream_in,
    queries,
    latents,
    key_rope,
    w_uk,
    w_uv,
    w_o,
    norm_gain,
    expert_ids,
    gate_weights,
    w_gate,
    w_up,
    w_down,
):
    blocks = w_o.reshape(RING, RING, 64, D)
    out = moe_call(
        queries[0],
        latents[0],
        w_uk,
        w_uv,
        blocks,
        stream_in[0],
        w_gate[0],
        w_up[0],
        w_down[0],
        norm_gain.reshape(2 * CHUNKS, CW),
        key_rope[0].T,
        jnp.transpose(expert_ids, (2, 0, 1)),
        jnp.transpose(gate_weights, (2, 0, 1)),
    )
    return out[None]


def solution(mesh):
    return jax.shard_map(
        local,
        mesh=mesh,
        in_specs=(
            P("exp", "ctx", None),
            P("exp", "ctx", None),
            P("exp", "ctx", None),
            P("exp", "ctx", None),
            P(None, "ctx"),
            P(None, "ctx"),
            P("ctx", None),
            P(),
            P("exp", "ctx", None),
            P("exp", "ctx", None),
            P(("ctx", "exp"), None, None),
            P(("ctx", "exp"), None, None),
            P(("ctx", "exp"), None, None),
        ),
        out_specs=P("exp", "ctx", None),
        check_vma=False,
    )
```

```python
import functools
import math

import jax
import jax.numpy as jnp
from jax import lax
from jax.experimental import pallas as pl
from jax.experimental.pallas import tpu as pltpu
from jax.sharding import PartitionSpec as P

NOPE = 128
ROPE = 64
VDIM = 128
KVL = 512
D = 2560
FF = 768
TOPK = 6
CAP = 9
TOK = 128
LEN = 1024
QW = 1536
RING = 4
ROWS = 72
CHUNKS = 10
CW = 128
SLOTS = 4
ROWS_IN = 5
HALF = 1280
CHIP = 256
LATW = 640
MESH = pl.DeviceIdType.MESH
BF = jnp.bfloat16
F32 = jnp.float32
ANY = pl.BlockSpec(memory_space=pl.ANY)
VM = pl.BlockSpec(memory_space=pltpu.VMEM)
DMA = pltpu.SemaphoreType.DMA


def place():
    c = lax.axis_index("ctx")
    e = lax.axis_index("exp")
    return c // 2, c % 2, e // RING, e % RING


def device(y, core, z, x):
    return (y * 2 + core, z * RING + x)


def step(v, d):
    return lax.rem(v + d, RING)


def remote(src, dst, send, recv, target):
    return pltpu.make_async_remote_copy(
        src_ref=src, dst_ref=dst, send_sem=send, recv_sem=recv, device_id=target, device_id_type=MESH
    )


def greet(targets, meanwhile):
    barrier = pltpu.get_barrier_semaphore()
    for target in targets:
        pl.semaphore_signal(barrier, inc=1, device_id=target, device_id_type=MESH)
    meanwhile()
    pl.semaphore_wait(barrier, len(targets))


def exp_targets(y, core, z, x):
    found = [device(y, 1 - core, z, x)]
    for d in (1, 2, 3):
        found.append(device(step(y, d), core, z, x))
        found.append(device(y, core, step(z, d), x))
        found.append(device(y, core, z, step(x, d)))
    return found


def first_phase(j, spot, src, mid, send, recv, own):
    y, core, z, x = spot
    cut = lax.rem(j, SLOTS)
    copies = []
    for d in (1, 3, 2):
        xx, zz = step(x, d), step(z, d)
        copies.append(
            remote(src.at[cut, 0, :, xx], mid.at[j, 0, x], send.at[j, d], recv.at[j, d], device(y, core, z, xx))
        )
        copies.append(
            remote(
                src.at[cut, 1, zz], mid.at[j, 1, z], send.at[j, 3 + d], recv.at[j, 3 + d], device(y, core, zz, x)
            )
        )
    copies.append(pltpu.make_async_copy(src.at[cut, 0, :, x], mid.at[j, 0, x], own.at[j, 0]))
    copies.append(pltpu.make_async_copy(src.at[cut, 1, z], mid.at[j, 1, z], own.at[j, 1]))
    return copies


def second_phase(j, spot, mid, dst, cut, send, recv, own):
    y, core, z, x = spot
    copies = []
    for d in (1, 3, 2):
        xx, zz = step(x, d), step(z, d)
        copies.append(
            remote(mid.at[j, 0, :, zz], dst.at[cut, 0, z], send.at[j, d], recv.at[j, d], device(y, core, zz, x))
        )
        copies.append(
            remote(
                mid.at[j, 1, :, xx],
                dst.at[cut, 1, :, x],
                send.at[j, 3 + d],
                recv.at[j, 3 + d],
                device(y, core, z, xx),
            )
        )
    copies.append(pltpu.make_async_copy(mid.at[j, 0, :, z], dst.at[cut, 0, z], own.at[j, 0]))
    copies.append(pltpu.make_async_copy(mid.at[j, 1, :, x], dst.at[cut, 1, :, x], own.at[j, 1]))
    return copies


def pipeline(stages):
    def turn(t, carry):
        for lag, stage in reversed(stages):
            j = t - lag

            @pl.when((j >= 0) & (j < CHUNKS))
            def _(stage=stage, j=j):
                stage(j)

        return carry

    lax.fori_loop(0, CHUNKS + stages[-1][0], turn, 0)


def start_all(copies):
    for copy in copies:
        copy.start()


def wait_all(copies):
    for copy in copies:
        copy.wait()


def moe_kernel(
    q_hbm, lat_hbm, uk_hbm, uv_hbm, wo_hbm, stream_hbm, wg_hbm, wu_hbm, wd_hbm,
    gain_ref, rope_ref, ids_ref, gates_ref, out_ref,
    qbuf, lat, turned, q_send, q_recv, l_send, l_recv, own_sem,
    mixed, late, p_own, p_sib, r_core, rs_buf, hbuf, gs, t1, xbuf, pickers, wg, wu, wd, sx, hown, fs_buf, spots,
    in_sem, wo_sem, w_sem, st_sem, c1_s, c1_r, rs_s, rs_r, ag_s, ag_r, c2_s, c2_r, p1_s, p1_r, p2_s, p2_r,
    d1_s, d1_r, d2_s, d2_r, c3_s, c3_r, fs_s, fs_r, o1, o2, o3, o4,
):
    spot = place()
    y, core, z, x = spot
    sibling = device(y, 1 - core, z, x)

    def columns(half, j):
        return pl.ds(pl.multiple_of(half * HALF + j * CW, 128), CW)

    def wo_copy(j, side):
        half = core if side == 0 else 1 - core
        return pltpu.make_async_copy(
            wo_hbm.at[:, :, :, columns(half, j)], late.at[j, side, :, :, 0:64], wo_sem.at[j, side]
        )

    def half_of(which):
        return pl.ds(pl.multiple_of(which * HALF, 128), HALF)

    stream_copy = pltpu.make_async_copy(stream_hbm.at[:, half_of(core)], sx.at[core], in_sem.at[1])
    weights = [
        pltpu.make_async_copy(wg_hbm, wg, w_sem.at[0]),
        pltpu.make_async_copy(wu_hbm, wu, w_sem.at[1]),
        pltpu.make_async_copy(wd_hbm, wd, w_sem.at[2]),
    ]
    me = y * 2 + core

    def lat_copy(dy):
        return remote(lat.at[me], lat.at[me], l_send.at[dy], l_recv.at[dy], device(step(y, dy), core, z, x))

    def lat_share(dy):
        block = lat.at[step(y, dy) * 2 + core]
        return remote(block, block, l_send.at[4 + dy], l_recv.at[4 + dy], device(y, 1 - core, z, x))

    def q_copy(dy, dc):
        i = dy * 2 + dc
        yy, cc = step(y, dy), lax.rem(core + dc, 2)
        columns = pl.ds(pl.multiple_of((yy * 2 + cc) * QW, 128), QW)
        return remote(q_hbm.at[:, columns], qbuf.at[me], q_send.at[i], q_recv.at[i], device(yy, cc, z, x))

    peers = [(dy, dc) for dy in (0, 1, 3, 2) for dc in (0, 1) if (dy, dc) != (0, 0)]
    own_lat = pltpu.make_async_copy(lat_hbm, lat.at[me, :, 0:KVL], own_sem.at[0])
    own_q = pltpu.make_async_copy(
        q_hbm.at[:, pl.ds(pl.multiple_of(me * QW, 128), QW)], qbuf.at[me], own_sem.at[1]
    )
    own_lat.start()
    own_q.start()

    def pack_side():
        turned[...] = jnp.zeros((128, TOK), F32)
        turned[0:ROPE, :] = rope_ref[...].astype(F32)
        for k in range(TOPK):
            turned[ROPE + k : ROPE + k + 1, :] = ids_ref[k].astype(F32)
            turned[ROPE + TOPK + k : ROPE + TOPK + k + 1, :] = gates_ref[k]
        lat[me, :, KVL:LATW] = jnp.transpose(turned[...]).astype(BF)
        own_lat.wait()

    greet(
        exp_targets(y, core, z, x) + [device(step(y, d), 1 - core, z, x) for d in (1, 2, 3)], pack_side
    )
    for dy in (1, 3, 2):
        lat_copy(dy).start()
    for dy, dc in peers:
        q_copy(dy, dc).start()
    stream_copy.start()

    def load_wo(j, carry):
        for side in range(2):
            wo_copy(j, side).start()
        return carry

    stream_send = remote(
        stream_hbm.at[:, half_of(1 - core)], sx.at[core], st_sem.at[0], st_sem.at[1], sibling
    )
    stream_send.start()
    stream_copy.wait()

    def rows_of(which):
        return pl.ds(pl.multiple_of(which * CHIP, CHIP), CHIP)

    def core_sum(j, send, recv):
        return remote(
            p_sib.at[lax.rem(j, 2)], r_core.at[lax.rem(j, SLOTS)], send.at[j], recv.at[j], sibling
        )

    def scatter(j, send, recv):
        return [
            remote(
                p_own.at[lax.rem(j, SLOTS), rows_of(step(y, d))],
                rs_buf.at[lax.rem(j, SLOTS), d - 1],
                send.at[j, d],
                recv.at[j, d],
                device(step(y, d), core, z, x),
            )
            for d in (1, 3, 2)
        ]

    def spread(j):
        block = hbuf.at[j, core, y, :, 0:64]
        return [
            remote(block, block, ag_s.at[j, d], ag_r.at[j, d], device(step(y, d), core, z, x))
            for d in (1, 3, 2)
        ]

    def core_share(j):
        block = hbuf.at[j, core, :, :, 0:64]
        return remote(block, block, c2_s.at[j], c2_r.at[j], sibling)

    def gather_row():
        row = lax.broadcasted_iota(jnp.int32, (1152, 128), 0)
        low = lax.broadcasted_iota(jnp.int32, (1152, 128), 1) * ROWS
        inside = (row >= low) & (row < low + ROWS)
        member = jnp.where(inside, 1.0, 0.0).astype(BF)
        at = jnp.sum(jnp.where(inside, row - low, 0).astype(F32), axis=1, keepdims=True)
        return member, at

    def route_spots():
        lane = lax.broadcasted_iota(jnp.int32, (TOK, 128), 1)
        first = ((y * 2 + core) * 16).astype(F32)
        wanted = jnp.where(lane < 16, lane.astype(F32) + first, -1.0)
        earlier = lax.broadcasted_iota(jnp.int32, (TOK, 128), 0) > lane
        earlier = jnp.where(earlier, 1.0, 0.0).astype(BF)
        for b in range(8):
            rows = slice(b * TOK, (b + 1) * TOK)
            route = lat[b, :, KVL:].astype(F32)
            named = jnp.zeros((TOK, 128), F32)
            gate = jnp.zeros((TOK, 128), F32)
            for k in range(TOPK):
                hit = route[:, 64 + k : 65 + k] == wanted
                named = jnp.where(hit, 1.0, named)
                gate = jnp.where(hit, route[:, 64 + TOPK + k : 65 + TOPK + k], gate)
            slot = jnp.dot(earlier, named.astype(BF), preferred_element_type=F32)
            spots[0, rows, :] = jnp.where(named > 0.0, slot + (b * CAP), -1.0).astype(BF)
            spots[1, rows, :] = gate.astype(BF)

    def pickers_in():
        member, at = gather_row()
        for b in range(RING):
            rows = slice(b * 288, (b + 1) * 288)
            wide = lax.dot_general(
                member[rows], spots[0], (((1,), (1,)), ((), ())), preferred_element_type=F32
            )
            pickers[rows, 0:LEN] = jnp.where(wide == at[rows], 1.0, 0.0).astype(BF)

    def pickers_out():
        low = lax.broadcasted_iota(jnp.int32, (128, 1152), 0) * ROWS
        row = lax.broadcasted_iota(jnp.int32, (128, 1152), 1)
        inside = (row >= low) & (row < low + ROWS)
        member = jnp.where(inside, 1.0, 0.0).astype(BF)
        at = jnp.sum(jnp.where(inside, row - low, 0).astype(F32), axis=0, keepdims=True)
        for b in range(RING):
            rows = slice(b * CHIP, (b + 1) * CHIP)
            wide = jnp.dot(spots[0, rows, :], member, preferred_element_type=F32)
            gate = jnp.dot(spots[1, rows, :], member, preferred_element_type=F32)
            pickers[rows, :] = jnp.where(wide == at, gate, 0.0).astype(BF)

    def attention(kbuf, vbuf, uk_ref, uv_ref, u_sem):
        projections = [
            pltpu.make_async_copy(uk_hbm, uk_ref, u_sem.at[0]),
            pltpu.make_async_copy(uv_hbm, uv_ref, u_sem.at[1]),
        ]
        start_all(projections)
        lat_share(0).start()
        for dy in (1, 3, 2):
            lat_copy(4 - dy).wait_recv()
            lat_share(dy).start()
        for dy in (0, 1, 3, 2):
            lat_share(dy).wait()
        for dy in (1, 3, 2):
            lat_copy(dy).wait_send()
        own_q.wait()
        lax.fori_loop(0, CHUNKS, load_wo, 0)
        start_all(weights)

        wait_all(projections)
        lane = lax.broadcasted_iota(jnp.int32, (CHIP, 128), 1)

        def project(b, carry):
            rows = pl.ds(pl.multiple_of(b * CHIP, CHIP), CHIP)
            block = lat[pl.ds(b * 2, 2)].reshape(CHIP, LATW)
            latent = block[:, :KVL]
            rope = block[:, KVL:].astype(F32)
            rope_low = jnp.where(lane < 64, rope, 0.0).astype(BF)
            rope_high = pltpu.roll(rope, 64, 1)
            for h in range(8):
                nope = jnp.dot(latent, uk_ref[:, h * 128 : h * 128 + 128], preferred_element_type=F32)
                if h % 2 == 0:
                    kbuf[h, rows, 0:128] = nope.astype(BF)
                    kbuf[h, rows, 128:256] = rope_low
                else:
                    turned = pltpu.roll(nope, 64, 1)
                    kbuf[h, rows, 0:128] = jnp.where(lane < 64, 0.0, turned).astype(BF)
                    kbuf[h, rows, 128:256] = jnp.where(lane < 64, turned, rope_high).astype(BF)
            vbuf[rows, :] = jnp.dot(latent, uv_ref[...], preferred_element_type=F32).astype(BF)
            return carry

        lax.fori_loop(0, RING, project, 0)

        route_spots()
        pickers_in()
        factor = 1.0 / math.sqrt(NOPE + ROPE) * math.log2(math.e)
        row_at = lax.broadcasted_iota(jnp.int32, (CHIP, CHIP), 0)
        col_at = lax.broadcasted_iota(jnp.int32, (CHIP, CHIP), 1)
        causal = row_at >= col_at

        def attend(block):
            length = (block + 1) * CHIP

            def pair(p, carry):
                columns = pl.ds(pl.multiple_of(p * 384, 128), 384)
                q = qbuf[block * 2 : block * 2 + 2, :, columns].reshape(CHIP, 384)
                outs = []
                for odd in range(2):
                    query = q[:, odd * 128 : odd * 128 + 256]
                    head = p * 2 + odd
                    contract = (((1,), (1,)), ((), ()))
                    last = lax.dot_general(
                        query, kbuf[head, length - CHIP : length], contract, preferred_element_type=F32
                    )
                    last = jnp.where(causal, last, -jnp.inf)
                    peak = jnp.max(last, axis=1, keepdims=True)
                    if block:
                        first = lax.dot_general(
                            query, kbuf[head, 0 : length - CHIP], contract, preferred_element_type=F32
                        )
                        peak = jnp.maximum(peak, jnp.max(first, axis=1, keepdims=True))
                    values = pl.ds(pl.multiple_of(head * 128, 128), 128)
                    weight = jnp.exp2((last - peak) * factor)
                    total = jnp.sum(weight, axis=1, keepdims=True)
                    result = jnp.dot(
                        weight.astype(BF), vbuf[length - CHIP : length, values], preferred_element_type=F32
                    )
                    if block:
                        weight = jnp.exp2((first - peak) * factor)
                        total += jnp.sum(weight, axis=1, keepdims=True)
                        result += jnp.dot(
                            weight.astype(BF), vbuf[0 : length - CHIP, values], preferred_element_type=F32
                        )
                    outs.append((result / total).astype(BF))
                mixed[block * CHIP : (block + 1) * CHIP, pl.ds(pl.multiple_of(p * 256, 256), 256)] = (
                    jnp.concatenate(outs, axis=1)
                )
                return carry

            lax.fori_loop(0, 4, pair, 0)

        for dy in (0, 1, 3, 2):
            for dc in range(2):
                if (dy, dc) != (0, 0):
                    q_copy((4 - dy) % 4, dc).wait_recv()
            source = lax.rem(y + dy, RING)
            for block in range(RING):
                pl.when(source == block)(functools.partial(attend, block))
        for dy, dc in peers:
            q_copy(dy, dc).wait_send()

    pl.run_scoped(
        attention,
        pltpu.VMEM((8, LEN, 256), BF),
        pltpu.VMEM((LEN, 1024), BF),
        pltpu.VMEM((KVL, 1024), BF),
        pltpu.VMEM((KVL, 1024), BF),
        DMA((2,)),
    )
    stream_send.wait()

    def experts(units, squares):
        def one(j):
            return first_phase(j, spot, gs, t1, p1_s, p1_r, o1)

        def two(j):
            return second_phase(j, spot, t1, xbuf, lax.rem(j, ROWS_IN), p2_s, p2_r, o2)

        def project(j):
            for side in range(2):
                wo_copy(j, side).wait()
            own = late[j, 0, :, :, 0:64].reshape(1024, CW)
            other = late[j, 1, :, :, 0:64].reshape(1024, CW)
            both = jnp.concatenate([own, other], axis=1)

            def block(b, carry):
                rows = rows_of(b)
                product = jnp.dot(mixed[rows, :], both, preferred_element_type=F32).astype(BF)
                p_own[lax.rem(j, SLOTS), rows] = product[:, :CW]
                p_sib[lax.rem(j, 2), rows] = product[:, CW:]
                return carry

            lax.fori_loop(0, RING, block, 0)
            core_sum(j, c1_s, c1_r).start()

        def add_core(j):
            core_sum(j, c1_s, c1_r).wait()
            slot = lax.rem(j, SLOTS)
            p_own[slot] = (p_own[slot].astype(F32) + r_core[slot].astype(F32)).astype(BF)
            start_all(scatter(j, rs_s, rs_r))

        def chip_total(j):
            slot = lax.rem(j, SLOTS)
            total = p_own[slot, rows_of(y)].astype(F32)
            for i in range(3):
                total += rs_buf[slot, i].astype(F32)
            return total

        def finish_hidden(j):
            wait_all(scatter(j, rs_s, rs_r))
            stream = sx[:, :, pl.ds(pl.multiple_of(j * CW, 128), CW)].reshape(CHIP, CW)
            hidden = (stream.astype(F32) + chip_total(j)).astype(BF)
            hbuf[j, core, y, :, 0:64] = hidden.reshape(RING, 64, CW)
            start_all(spread(j))

        def share(j):
            wait_all(spread(j))
            core_share(j).start()

        def pick(j):
            core_share(j).wait()
            for side, half in enumerate((core, 1 - core)):
                hown[j, side] = hbuf[j, half, y, pl.ds(core * 2, 2), 0:64].reshape(TOK, CW)
            both = jnp.concatenate(
                [hbuf[j, half, :, :, 0:64].reshape(1024, CW) for half in range(2)], axis=1
            )

            def block(b, carry):
                left = pickers[pl.ds(pl.multiple_of(b * 288, 16), 288), 0:LEN]
                picked = jnp.dot(left, both, preferred_element_type=F32).reshape(RING, ROWS, 2 * CW)
                gs[lax.rem(j, SLOTS), 0, b] = picked[:, :, :CW].astype(BF)
                gs[lax.rem(j, SLOTS), 1, b] = picked[:, :, CW:].astype(BF)
                return carry

            lax.fori_loop(0, RING, block, 0)
            start_all(one(j))

        def forward(j):
            wait_all(one(j))
            start_all(two(j))

        def drain(j):
            wait_all(two(j))

            @pl.when(j == 0)
            def _():
                wait_all(weights)

            gains = [gain_ref[pl.ds(half * CHUNKS + j, 1), :] for half in range(2)]
            firsts = [pl.ds(pl.multiple_of(half * HALF + j * CW, 128), CW) for half in range(2)]
            right_gate = jnp.concatenate([wg[rows, :] for rows in firsts], axis=0)
            right_up = jnp.concatenate([wu[rows, :] for rows in firsts], axis=0)

            def block(b, carry):
                rows = pl.ds(pl.multiple_of(b * 288, 16), 288)
                parts = [xbuf[lax.rem(j, ROWS_IN), half, b].astype(F32).reshape(288, CW) for half in range(2)]
                squares[rows, :] += parts[0] * parts[0] + parts[1] * parts[1]
                left = jnp.concatenate([(p * g).astype(BF) for p, g in zip(parts, gains)], axis=1)
                units[rows, 0:FF] += jnp.dot(left, right_gate, preferred_element_type=F32)
                units[rows, FF : 2 * FF] += jnp.dot(left, right_up, preferred_element_type=F32)
                return carry

            lax.fori_loop(0, RING, block, 0)

        def clear():
            units[...] = jnp.zeros((1152, 2 * FF), F32)
            squares[...] = jnp.zeros((1152, CW), F32)

        def prepare(j):
            pl.when(j == 8)(clear)

        pipeline(
            [
                (0, project),
                (1, add_core),
                (1, prepare),
                (3, finish_hidden),
                (5, share),
                (6, pick),
                (8, forward),
                (10, drain),
            ]
        )

        def hidden_units(b, carry):
            rows = pl.ds(pl.multiple_of(b * 144, 16), 144)
            total = jnp.sum(squares[rows, :], axis=1, keepdims=True)
            scale = lax.rsqrt(total * (1.0 / D) + 1e-06)
            gate = units[rows, 0:FF] * scale
            up = units[rows, FF : 2 * FF] * scale
            mixed[rows, 0:FF] = (gate / (1.0 + jnp.exp(-gate)) * up).astype(BF)
            return carry

        lax.fori_loop(0, 8, hidden_units, 0)

        def back_one(j):
            return first_phase(j, spot, gs, late, d1_s, d1_r, o3)

        def back_two(j):
            return second_phase(j, spot, late, hbuf, j, d2_s, d2_r, o4)

        def gather_back(j):
            slot = lax.rem(j, SLOTS)
            copies = []
            for i, (dy, dc) in enumerate(peers):
                yy, cc = step(y, dy), lax.rem(core + dc, 2)
                rows = pl.ds(pl.multiple_of((yy * 2 + cc) * TOK, TOK), TOK)
                copies.append(
                    remote(
                        p_own.at[slot, rows],
                        fs_buf.at[slot, i],
                        fs_s.at[j, i],
                        fs_r.at[j, i],
                        device(yy, cc, z, x),
                    )
                )
            return copies

        def down(j):
            both = jnp.concatenate([wd[:, columns(half, j)] for half in range(2)], axis=1)

            def block(b, carry):
                left = mixed[pl.ds(pl.multiple_of(b * 288, 16), 288), 0:FF]
                result = jnp.dot(left, both, preferred_element_type=F32).reshape(RING, ROWS, 2 * CW)
                gs[lax.rem(j, SLOTS), 0, b] = result[:, :, :CW].astype(BF)
                gs[lax.rem(j, SLOTS), 1, b] = result[:, :, CW:].astype(BF)
                return carry

            lax.fori_loop(0, RING, block, 0)
            start_all(back_one(j))

        def back_forward(j):
            wait_all(back_one(j))
            start_all(back_two(j))

        def combine(j):
            wait_all(back_two(j))
            both = jnp.concatenate(
                [
                    hbuf[j, core].astype(F32).reshape(1152, CW).astype(BF),
                    hbuf[j, 1 - core].astype(F32).reshape(1152, CW).astype(BF),
                ],
                axis=1,
            )

            def block(b, carry):
                rows = rows_of(b)
                product = jnp.dot(pickers[rows, :], both, preferred_element_type=F32).astype(BF)
                p_own[lax.rem(j, SLOTS), rows] = product[:, :CW]
                p_sib[lax.rem(j, 2), rows] = product[:, CW:]
                return carry

            lax.fori_loop(0, RING, block, 0)
            core_sum(j, c3_s, c3_r).start()

        def add_back(j):
            core_sum(j, c3_s, c3_r).wait()
            slot = lax.rem(j, SLOTS)
            p_own[slot] = (p_own[slot].astype(F32) + r_core[slot].astype(F32)).astype(BF)
            start_all(gather_back(j))

        def finish(j):
            wait_all(gather_back(j))
            slot = lax.rem(j, SLOTS)
            mine = pl.ds(pl.multiple_of(me * TOK, TOK), TOK)
            totals = [p_own[slot, mine].astype(F32), jnp.zeros((TOK, CW), F32)]
            for i, (dy, dc) in enumerate(peers):
                totals[dc] += fs_buf[slot, i].astype(F32)
            for side, half in enumerate((core, 1 - core)):
                hidden = hown[j, side].astype(F32)
                out_ref[:, columns(half, j)] = (hidden + totals[side]).astype(BF)

        def prepare_back(j):
            pl.when(j == 0)(pickers_out)

        pipeline(
            [
                (0, down),
                (1, prepare_back),
                (3, back_forward),
                (5, combine),
                (7, add_back),
                (9, finish),
            ]
        )

    pl.run_scoped(experts, pltpu.VMEM((1152, 2 * FF), F32), pltpu.VMEM((1152, CW), F32))


def moe_call(queries, latents, w_uk, w_uv, w_o, stream, w_gate, w_up, w_down, gain, rope, ids, gates):
    grid_rows = (CHUNKS, 2, RING, RING, ROWS, CW)
    one = DMA((CHUNKS,))
    ring = DMA((CHUNKS, 4))
    phase = DMA((CHUNKS, 7))
    return pl.pallas_call(
        moe_kernel,
        out_shape=jax.ShapeDtypeStruct((TOK, D), BF),
        in_specs=[ANY] * 9 + [VM] * 4,
        out_specs=VM,
        scratch_shapes=[
            pltpu.VMEM((8, TOK, QW), BF),
            pltpu.VMEM((8, TOK, LATW), BF),
            pltpu.VMEM((128, TOK), F32),
            *[DMA((8,))] * 4,
            DMA((2,)),
            pltpu.VMEM((1152, 1024), BF),
            pltpu.VMEM(grid_rows, BF),
            pltpu.VMEM((SLOTS, LEN, CW), BF),
            pltpu.VMEM((2, LEN, CW), BF),
            pltpu.VMEM((SLOTS, LEN, CW), BF),
            pltpu.VMEM((SLOTS, 3, CHIP, CW), BF),
            pltpu.VMEM(grid_rows, BF),
            pltpu.VMEM((SLOTS, *grid_rows[1:]), BF),
            pltpu.VMEM(grid_rows, BF),
            pltpu.VMEM((ROWS_IN, *grid_rows[1:]), BF),
            pltpu.VMEM((1152, 1152), BF),
            pltpu.VMEM((D, FF), BF),
            pltpu.VMEM((D, FF), BF),
            pltpu.VMEM((FF, D), BF),
            pltpu.VMEM((2, TOK, HALF), BF),
            pltpu.VMEM((CHUNKS, 2, TOK, CW), BF),
            pltpu.VMEM((SLOTS, 7, TOK, CW), BF),
            pltpu.VMEM((2, LEN, 128), BF),
            DMA((2,)),
            DMA((CHUNKS, 2)),
            DMA((3,)),
            DMA((2,)),
            *[one, one, ring, ring, ring, ring, one, one],
            *[phase] * 8,
            *[one, one],
            *[DMA((CHUNKS, 7))] * 2,
            *[DMA((CHUNKS, 2))] * 4,
        ],
        compiler_params=pltpu.CompilerParams(
            collective_id=2, has_side_effects=True, vmem_limit_bytes=63 * 2**20
        ),
        name="moe",
    )(queries, latents, w_uk, w_uv, w_o, stream, w_gate, w_up, w_down, gain, rope, ids, gates)


def local(
    stream_in,
    queries,
    latents,
    key_rope,
    w_uk,
    w_uv,
    w_o,
    norm_gain,
    expert_ids,
    gate_weights,
    w_gate,
    w_up,
    w_down,
):
    blocks = w_o.reshape(RING, RING, 64, D)
    out = moe_call(
        queries[0],
        latents[0],
        w_uk,
        w_uv,
        blocks,
        stream_in[0],
        w_gate[0],
        w_up[0],
        w_down[0],
        norm_gain.reshape(2 * CHUNKS, CW),
        key_rope[0].T,
        jnp.transpose(expert_ids, (2, 0, 1)),
        jnp.transpose(gate_weights, (2, 0, 1)),
    )
    return out[None]


def solution(mesh):
    return jax.shard_map(
        local,
        mesh=mesh,
        in_specs=(
            P("exp", "ctx", None),
            P("exp", "ctx", None),
            P("exp", "ctx", None),
            P("exp", "ctx", None),
            P(None, "ctx"),
            P(None, "ctx"),
            P("ctx", None),
            P(),
            P("exp", "ctx", None),
            P("exp", "ctx", None),
            P(("ctx", "exp"), None, None),
            P(("ctx", "exp"), None, None),
            P(("ctx", "exp"), None, None),
        ),
        out_specs=P("exp", "ctx", None),
        check_vma=False,
    )
```

```python
import functools
import math

import jax
import jax.numpy as jnp
from jax import lax
from jax.experimental import pallas as pl
from jax.experimental.pallas import tpu as pltpu
from jax.sharding import PartitionSpec as P

NOPE = 128
ROPE = 64
VDIM = 128
KVL = 512
D = 2560
FF = 768
TOPK = 6
CAP = 9
TOK = 128
LEN = 1024
QW = 1536
RING = 4
ROWS = 72
CHUNKS = 10
CW = 128
SLOTS = 4
ROWS_IN = 5
HALF = 1280
CHIP = 256
LATW = 640
MESH = pl.DeviceIdType.MESH
BF = jnp.bfloat16
F32 = jnp.float32
ANY = pl.BlockSpec(memory_space=pl.ANY)
VM = pl.BlockSpec(memory_space=pltpu.VMEM)
DMA = pltpu.SemaphoreType.DMA


def place():
    c = lax.axis_index("ctx")
    e = lax.axis_index("exp")
    return c // 2, c % 2, e // RING, e % RING


def device(y, core, z, x):
    return (y * 2 + core, z * RING + x)


def step(v, d):
    return lax.rem(v + d, RING)


def remote(src, dst, send, recv, target):
    return pltpu.make_async_remote_copy(
        src_ref=src, dst_ref=dst, send_sem=send, recv_sem=recv, device_id=target, device_id_type=MESH
    )


def greet(targets, meanwhile):
    barrier = pltpu.get_barrier_semaphore()
    for target in targets:
        pl.semaphore_signal(barrier, inc=1, device_id=target, device_id_type=MESH)
    meanwhile()
    pl.semaphore_wait(barrier, len(targets))


def exp_targets(y, core, z, x):
    found = [device(y, 1 - core, z, x)]
    for d in (1, 2, 3):
        found.append(device(step(y, d), core, z, x))
        found.append(device(y, core, step(z, d), x))
        found.append(device(y, core, z, step(x, d)))
    return found


def first_phase(j, spot, src, mid, send, recv, own):
    y, core, z, x = spot
    cut = lax.rem(j, SLOTS)
    copies = []
    for d in (1, 3, 2):
        xx, zz = step(x, d), step(z, d)
        copies.append(
            remote(src.at[cut, 0, :, xx], mid.at[j, 0, x], send.at[j, d], recv.at[j, d], device(y, core, z, xx))
        )
        copies.append(
            remote(
                src.at[cut, 1, zz], mid.at[j, 1, z], send.at[j, 3 + d], recv.at[j, 3 + d], device(y, core, zz, x)
            )
        )
    copies.append(pltpu.make_async_copy(src.at[cut, 0, :, x], mid.at[j, 0, x], own.at[j, 0]))
    copies.append(pltpu.make_async_copy(src.at[cut, 1, z], mid.at[j, 1, z], own.at[j, 1]))
    return copies


def second_phase(j, spot, mid, dst, cut, send, recv, own):
    y, core, z, x = spot
    copies = []
    for d in (1, 3, 2):
        xx, zz = step(x, d), step(z, d)
        copies.append(
            remote(mid.at[j, 0, :, zz], dst.at[cut, 0, z], send.at[j, d], recv.at[j, d], device(y, core, zz, x))
        )
        copies.append(
            remote(
                mid.at[j, 1, :, xx],
                dst.at[cut, 1, :, x],
                send.at[j, 3 + d],
                recv.at[j, 3 + d],
                device(y, core, z, xx),
            )
        )
    copies.append(pltpu.make_async_copy(mid.at[j, 0, :, z], dst.at[cut, 0, z], own.at[j, 0]))
    copies.append(pltpu.make_async_copy(mid.at[j, 1, :, x], dst.at[cut, 1, :, x], own.at[j, 1]))
    return copies


def pipeline(stages):
    def turn(t, carry):
        for lag, stage in reversed(stages):
            j = t - lag

            @pl.when((j >= 0) & (j < CHUNKS))
            def _(stage=stage, j=j):
                stage(j)

        return carry

    lax.fori_loop(0, CHUNKS + stages[-1][0], turn, 0)


def start_all(copies):
    for copy in copies:
        copy.start()


def wait_all(copies):
    for copy in copies:
        copy.wait()


def moe_kernel(
    q_hbm, lat_hbm, uk_hbm, uv_hbm, wo_hbm, stream_hbm, wg_hbm, wu_hbm, wd_hbm,
    gain_ref, rope_ref, ids_ref, gates_ref, out_ref,
    qbuf, lat, turned, q_send, q_recv, l_send, l_recv, own_sem,
    mixed, late, p_own, p_sib, r_core, rs_buf, hbuf, gs, t1, xbuf, pickers, wg, wu, wd, sx, hown, fs_buf, spots,
    in_sem, wo_sem, w_sem, st_sem, c1_s, c1_r, rs_s, rs_r, ag_s, ag_r, c2_s, c2_r, p1_s, p1_r, p2_s, p2_r,
    d1_s, d1_r, d2_s, d2_r, c3_s, c3_r, fs_s, fs_r, o1, o2, o3, o4,
):
    spot = place()
    y, core, z, x = spot
    sibling = device(y, 1 - core, z, x)

    def columns(half, j):
        return pl.ds(pl.multiple_of(half * HALF + j * CW, 128), CW)

    def wo_copy(j, side):
        half = core if side == 0 else 1 - core
        return pltpu.make_async_copy(
            wo_hbm.at[:, :, :, columns(half, j)], late.at[j, side, :, :, 0:64], wo_sem.at[j, side]
        )

    def half_of(which):
        return pl.ds(pl.multiple_of(which * HALF, 128), HALF)

    stream_copy = pltpu.make_async_copy(stream_hbm.at[:, half_of(core)], sx.at[core], in_sem.at[1])
    weights = [
        pltpu.make_async_copy(wg_hbm, wg, w_sem.at[0]),
        pltpu.make_async_copy(wu_hbm, wu, w_sem.at[1]),
        pltpu.make_async_copy(wd_hbm, wd, w_sem.at[2]),
    ]
    me = y * 2 + core

    def lat_copy(dy):
        return remote(lat.at[me], lat.at[me], l_send.at[dy], l_recv.at[dy], device(step(y, dy), core, z, x))

    def lat_share(dy):
        block = lat.at[step(y, dy) * 2 + core]
        return remote(block, block, l_send.at[4 + dy], l_recv.at[4 + dy], device(y, 1 - core, z, x))

    def q_copy(dy, dc):
        i = dy * 2 + dc
        yy, cc = step(y, dy), lax.rem(core + dc, 2)
        columns = pl.ds(pl.multiple_of((yy * 2 + cc) * QW, 128), QW)
        return remote(q_hbm.at[:, columns], qbuf.at[me], q_send.at[i], q_recv.at[i], device(yy, cc, z, x))

    peers = [(dy, dc) for dy in (0, 1, 3, 2) for dc in (0, 1) if (dy, dc) != (0, 0)]
    own_lat = pltpu.make_async_copy(lat_hbm, lat.at[me, :, 0:KVL], own_sem.at[0])
    own_q = pltpu.make_async_copy(
        q_hbm.at[:, pl.ds(pl.multiple_of(me * QW, 128), QW)], qbuf.at[me], own_sem.at[1]
    )
    own_lat.start()
    own_q.start()

    def pack_side():
        turned[...] = jnp.zeros((128, TOK), F32)
        turned[0:ROPE, :] = rope_ref[...].astype(F32)
        for k in range(TOPK):
            turned[ROPE + k : ROPE + k + 1, :] = ids_ref[k].astype(F32)
            turned[ROPE + TOPK + k : ROPE + TOPK + k + 1, :] = gates_ref[k]
        lat[me, :, KVL:LATW] = jnp.transpose(turned[...]).astype(BF)
        own_lat.wait()

    greet(
        exp_targets(y, core, z, x) + [device(step(y, d), 1 - core, z, x) for d in (1, 2, 3)], pack_side
    )
    for dy in (1, 3, 2):
        lat_copy(dy).start()
    for dy, dc in peers:
        q_copy(dy, dc).start()
    stream_copy.start()

    def load_wo(j, carry):
        for side in range(2):
            wo_copy(j, side).start()
        return carry

    stream_send = remote(
        stream_hbm.at[:, half_of(1 - core)], sx.at[core], st_sem.at[0], st_sem.at[1], sibling
    )
    stream_send.start()
    stream_copy.wait()

    def rows_of(which):
        return pl.ds(pl.multiple_of(which * CHIP, CHIP), CHIP)

    def core_sum(j, send, recv):
        slot = lax.rem(j, 2)
        return remote(p_sib.at[slot], r_core.at[slot], send.at[j], recv.at[j], sibling)

    def scatter(j, send, recv):
        return [
            remote(
                p_own.at[lax.rem(j, SLOTS), rows_of(step(y, d))],
                rs_buf.at[lax.rem(j, SLOTS), d - 1],
                send.at[j, d],
                recv.at[j, d],
                device(step(y, d), core, z, x),
            )
            for d in (1, 3, 2)
        ]

    def spread(j):
        block = hbuf.at[j, core, y, :, 0:64]
        return [
            remote(block, block, ag_s.at[j, d], ag_r.at[j, d], device(step(y, d), core, z, x))
            for d in (1, 3, 2)
        ]

    def core_share(j):
        block = hbuf.at[j, core, :, :, 0:64]
        return remote(block, block, c2_s.at[j], c2_r.at[j], sibling)

    def gather_row():
        row = lax.broadcasted_iota(jnp.int32, (1152, 128), 0)
        low = lax.broadcasted_iota(jnp.int32, (1152, 128), 1) * ROWS
        inside = (row >= low) & (row < low + ROWS)
        member = jnp.where(inside, 1.0, 0.0).astype(BF)
        at = jnp.sum(jnp.where(inside, row - low, 0).astype(F32), axis=1, keepdims=True)
        return member, at

    def route_spots():
        lane = lax.broadcasted_iota(jnp.int32, (TOK, 128), 1)
        first = ((y * 2 + core) * 16).astype(F32)
        wanted = jnp.where(lane < 16, lane.astype(F32) + first, -1.0)
        earlier = lax.broadcasted_iota(jnp.int32, (TOK, 128), 0) > lane
        earlier = jnp.where(earlier, 1.0, 0.0).astype(BF)
        for b in range(8):
            rows = slice(b * TOK, (b + 1) * TOK)
            route = lat[b, :, KVL:].astype(F32)
            named = jnp.zeros((TOK, 128), F32)
            gate = jnp.zeros((TOK, 128), F32)
            for k in range(TOPK):
                hit = route[:, 64 + k : 65 + k] == wanted
                named = jnp.where(hit, 1.0, named)
                gate = jnp.where(hit, route[:, 64 + TOPK + k : 65 + TOPK + k], gate)
            slot = jnp.dot(earlier, named.astype(BF), preferred_element_type=F32)
            spots[0, rows, :] = jnp.where(named > 0.0, slot + (b * CAP), -1.0).astype(BF)
            spots[1, rows, :] = gate.astype(BF)

    def pickers_in():
        member, at = gather_row()
        for b in range(RING):
            rows = slice(b * 288, (b + 1) * 288)
            wide = lax.dot_general(
                member[rows], spots[0], (((1,), (1,)), ((), ())), preferred_element_type=F32
            )
            pickers[rows, 0:LEN] = jnp.where(wide == at[rows], 1.0, 0.0).astype(BF)

    def pickers_out():
        low = lax.broadcasted_iota(jnp.int32, (128, 1152), 0) * ROWS
        row = lax.broadcasted_iota(jnp.int32, (128, 1152), 1)
        inside = (row >= low) & (row < low + ROWS)
        member = jnp.where(inside, 1.0, 0.0).astype(BF)
        at = jnp.sum(jnp.where(inside, row - low, 0).astype(F32), axis=0, keepdims=True)
        for b in range(RING):
            rows = slice(b * CHIP, (b + 1) * CHIP)
            wide = jnp.dot(spots[0, rows, :], member, preferred_element_type=F32)
            gate = jnp.dot(spots[1, rows, :], member, preferred_element_type=F32)
            pickers[rows, :] = jnp.where(wide == at, gate, 0.0).astype(BF)

    def attention(kbuf, vbuf, uk_ref, uv_ref, u_sem):
        projections = [
            pltpu.make_async_copy(uk_hbm, uk_ref, u_sem.at[0]),
            pltpu.make_async_copy(uv_hbm, uv_ref, u_sem.at[1]),
        ]
        start_all(projections)
        lat_share(0).start()
        for dy in (1, 3, 2):
            lat_copy(4 - dy).wait_recv()
            lat_share(dy).start()
        for dy in (0, 1, 3, 2):
            lat_share(dy).wait()
        for dy in (1, 3, 2):
            lat_copy(dy).wait_send()
        own_q.wait()
        lax.fori_loop(0, CHUNKS, load_wo, 0)
        start_all(weights)

        wait_all(projections)
        lane = lax.broadcasted_iota(jnp.int32, (CHIP, 128), 1)

        def project(b, carry):
            rows = pl.ds(pl.multiple_of(b * CHIP, CHIP), CHIP)
            block = lat[pl.ds(b * 2, 2)].reshape(CHIP, LATW)
            latent = block[:, :KVL]
            rope = block[:, KVL:].astype(F32)
            rope_low = jnp.where(lane < 64, rope, 0.0).astype(BF)
            rope_high = pltpu.roll(rope, 64, 1)
            for h in range(8):
                nope = jnp.dot(latent, uk_ref[:, h * 128 : h * 128 + 128], preferred_element_type=F32)
                if h % 2 == 0:
                    kbuf[h, rows, 0:128] = nope.astype(BF)
                    kbuf[h, rows, 128:256] = rope_low
                else:
                    turned = pltpu.roll(nope, 64, 1)
                    kbuf[h, rows, 0:128] = jnp.where(lane < 64, 0.0, turned).astype(BF)
                    kbuf[h, rows, 128:256] = jnp.where(lane < 64, turned, rope_high).astype(BF)
            vbuf[rows, :] = jnp.dot(latent, uv_ref[...], preferred_element_type=F32).astype(BF)
            return carry

        lax.fori_loop(0, RING, project, 0)

        factor = 1.0 / math.sqrt(NOPE + ROPE) * math.log2(math.e)
        row_at = lax.broadcasted_iota(jnp.int32, (CHIP, CHIP), 0)
        col_at = lax.broadcasted_iota(jnp.int32, (CHIP, CHIP), 1)
        causal = row_at >= col_at

        def attend(block):
            length = (block + 1) * CHIP

            def pair(p, carry):
                columns = pl.ds(pl.multiple_of(p * 384, 128), 384)
                q = qbuf[block * 2 : block * 2 + 2, :, columns].reshape(CHIP, 384)
                outs = []
                for odd in range(2):
                    query = q[:, odd * 128 : odd * 128 + 256]
                    head = p * 2 + odd
                    contract = (((1,), (1,)), ((), ()))
                    last = lax.dot_general(
                        query, kbuf[head, length - CHIP : length], contract, preferred_element_type=F32
                    )
                    last = jnp.where(causal, last, -jnp.inf)
                    peak = jnp.max(last, axis=1, keepdims=True)
                    if block:
                        first = lax.dot_general(
                            query, kbuf[head, 0 : length - CHIP], contract, preferred_element_type=F32
                        )
                        peak = jnp.maximum(peak, jnp.max(first, axis=1, keepdims=True))
                    values = pl.ds(pl.multiple_of(head * 128, 128), 128)
                    weight = jnp.exp2((last - peak) * factor)
                    total = jnp.sum(weight, axis=1, keepdims=True)
                    result = jnp.dot(
                        weight.astype(BF), vbuf[length - CHIP : length, values], preferred_element_type=F32
                    )
                    if block:
                        weight = jnp.exp2((first - peak) * factor)
                        total += jnp.sum(weight, axis=1, keepdims=True)
                        result += jnp.dot(
                            weight.astype(BF), vbuf[0 : length - CHIP, values], preferred_element_type=F32
                        )
                    outs.append((result / total).astype(BF))
                mixed[block * CHIP : (block + 1) * CHIP, pl.ds(pl.multiple_of(p * 256, 256), 256)] = (
                    jnp.concatenate(outs, axis=1)
                )
                return carry

            lax.fori_loop(0, 4, pair, 0)

        for dy in (0, 1, 3, 2):
            for dc in range(2):
                if (dy, dc) != (0, 0):
                    q_copy((4 - dy) % 4, dc).wait_recv()
            source = lax.rem(y + dy, RING)
            for block in range(RING):
                pl.when(source == block)(functools.partial(attend, block))
        for dy, dc in peers:
            q_copy(dy, dc).wait_send()

    pl.run_scoped(
        attention,
        pltpu.VMEM((8, LEN, 256), BF),
        pltpu.VMEM((LEN, 1024), BF),
        pltpu.VMEM((KVL, 1024), BF),
        pltpu.VMEM((KVL, 1024), BF),
        DMA((2,)),
    )
    stream_send.wait()

    def experts(units, squares):
        def one(j):
            return first_phase(j, spot, gs, t1, p1_s, p1_r, o1)

        def two(j):
            return second_phase(j, spot, t1, xbuf, lax.rem(j, ROWS_IN), p2_s, p2_r, o2)

        def project(j):
            for side in range(2):
                wo_copy(j, side).wait()
            own = late[j, 0, :, :, 0:64].reshape(1024, CW)
            other = late[j, 1, :, :, 0:64].reshape(1024, CW)
            both = jnp.concatenate([own, other], axis=1)

            def block(b, carry):
                rows = rows_of(b)
                product = jnp.dot(mixed[rows, :], both, preferred_element_type=F32).astype(BF)
                p_own[lax.rem(j, SLOTS), rows] = product[:, :CW]
                p_sib[lax.rem(j, 2), rows] = product[:, CW:]
                return carry

            lax.fori_loop(0, RING, block, 0)
            core_sum(j, c1_s, c1_r).start()

        def add_core(j):
            core_sum(j, c1_s, c1_r).wait()
            slot = lax.rem(j, SLOTS)
            p_own[slot] = (p_own[slot].astype(F32) + r_core[lax.rem(j, 2)].astype(F32)).astype(BF)
            start_all(scatter(j, rs_s, rs_r))

        def chip_total(j):
            slot = lax.rem(j, SLOTS)
            total = p_own[slot, rows_of(y)].astype(F32)
            for i in range(3):
                total += rs_buf[slot, i].astype(F32)
            return total

        def finish_hidden(j):
            wait_all(scatter(j, rs_s, rs_r))
            stream = sx[:, :, pl.ds(pl.multiple_of(j * CW, 128), CW)].reshape(CHIP, CW)
            hidden = (stream.astype(F32) + chip_total(j)).astype(BF)
            hbuf[j, core, y, :, 0:64] = hidden.reshape(RING, 64, CW)
            start_all(spread(j))

        def share(j):
            wait_all(spread(j))
            core_share(j).start()

        def pick(j):
            core_share(j).wait()
            for side, half in enumerate((core, 1 - core)):
                hown[j, side] = hbuf[j, half, y, pl.ds(core * 2, 2), 0:64].reshape(TOK, CW)
            both = jnp.concatenate(
                [hbuf[j, half, :, :, 0:64].reshape(1024, CW) for half in range(2)], axis=1
            )

            def block(b, carry):
                left = pickers[pl.ds(pl.multiple_of(b * 288, 16), 288), 0:LEN]
                picked = jnp.dot(left, both, preferred_element_type=F32).reshape(RING, ROWS, 2 * CW)
                gs[lax.rem(j, SLOTS), 0, b] = picked[:, :, :CW].astype(BF)
                gs[lax.rem(j, SLOTS), 1, b] = picked[:, :, CW:].astype(BF)
                return carry

            lax.fori_loop(0, RING, block, 0)
            start_all(one(j))

        def forward(j):
            wait_all(one(j))
            start_all(two(j))

        def drain(j):
            wait_all(two(j))

            @pl.when(j == 0)
            def _():
                wait_all(weights)

            gains = [gain_ref[pl.ds(half * CHUNKS + j, 1), :] for half in range(2)]
            firsts = [pl.ds(pl.multiple_of(half * HALF + j * CW, 128), CW) for half in range(2)]
            right_gate = jnp.concatenate([wg[rows, :] for rows in firsts], axis=0)
            right_up = jnp.concatenate([wu[rows, :] for rows in firsts], axis=0)

            def block(b, carry):
                rows = pl.ds(pl.multiple_of(b * 288, 16), 288)
                parts = [xbuf[lax.rem(j, ROWS_IN), half, b].astype(F32).reshape(288, CW) for half in range(2)]
                squares[rows, :] += parts[0] * parts[0] + parts[1] * parts[1]
                left = jnp.concatenate([(p * g).astype(BF) for p, g in zip(parts, gains)], axis=1)
                units[rows, 0:FF] += jnp.dot(left, right_gate, preferred_element_type=F32)
                units[rows, FF : 2 * FF] += jnp.dot(left, right_up, preferred_element_type=F32)
                return carry

            lax.fori_loop(0, RING, block, 0)

        def clear():
            units[...] = jnp.zeros((1152, 2 * FF), F32)
            squares[...] = jnp.zeros((1152, CW), F32)

        def prepare(j):
            pl.when(j == 0)(route_spots)
            pl.when(j == 4)(pickers_in)
            pl.when(j == 8)(clear)

        pipeline(
            [
                (0, project),
                (1, add_core),
                (1, prepare),
                (3, finish_hidden),
                (5, share),
                (6, pick),
                (8, forward),
                (10, drain),
            ]
        )

        def hidden_units(b, carry):
            rows = pl.ds(pl.multiple_of(b * 144, 16), 144)
            total = jnp.sum(squares[rows, :], axis=1, keepdims=True)
            scale = lax.rsqrt(total * (1.0 / D) + 1e-06)
            gate = units[rows, 0:FF] * scale
            up = units[rows, FF : 2 * FF] * scale
            mixed[rows, 0:FF] = (gate / (1.0 + jnp.exp(-gate)) * up).astype(BF)
            return carry

        lax.fori_loop(0, 8, hidden_units, 0)

        def back_one(j):
            return first_phase(j, spot, gs, late, d1_s, d1_r, o3)

        def back_two(j):
            return second_phase(j, spot, late, hbuf, j, d2_s, d2_r, o4)

        def gather_back(j):
            slot = lax.rem(j, SLOTS)
            copies = []
            for i, (dy, dc) in enumerate(peers):
                yy, cc = step(y, dy), lax.rem(core + dc, 2)
                rows = pl.ds(pl.multiple_of((yy * 2 + cc) * TOK, TOK), TOK)
                copies.append(
                    remote(
                        p_own.at[slot, rows],
                        fs_buf.at[slot, i],
                        fs_s.at[j, i],
                        fs_r.at[j, i],
                        device(yy, cc, z, x),
                    )
                )
            return copies

        def down(j):
            both = jnp.concatenate([wd[:, columns(half, j)] for half in range(2)], axis=1)

            def block(b, carry):
                left = mixed[pl.ds(pl.multiple_of(b * 288, 16), 288), 0:FF]
                result = jnp.dot(left, both, preferred_element_type=F32).reshape(RING, ROWS, 2 * CW)
                gs[lax.rem(j, SLOTS), 0, b] = result[:, :, :CW].astype(BF)
                gs[lax.rem(j, SLOTS), 1, b] = result[:, :, CW:].astype(BF)
                return carry

            lax.fori_loop(0, RING, block, 0)
            start_all(back_one(j))

        def back_forward(j):
            wait_all(back_one(j))
            start_all(back_two(j))

        def combine(j):
            wait_all(back_two(j))
            both = jnp.concatenate(
                [
                    hbuf[j, core].astype(F32).reshape(1152, CW).astype(BF),
                    hbuf[j, 1 - core].astype(F32).reshape(1152, CW).astype(BF),
                ],
                axis=1,
            )

            def block(b, carry):
                rows = rows_of(b)
                product = jnp.dot(pickers[rows, :], both, preferred_element_type=F32).astype(BF)
                p_own[lax.rem(j, SLOTS), rows] = product[:, :CW]
                p_sib[lax.rem(j, 2), rows] = product[:, CW:]
                return carry

            lax.fori_loop(0, RING, block, 0)
            core_sum(j, c3_s, c3_r).start()

        def add_back(j):
            core_sum(j, c3_s, c3_r).wait()
            slot = lax.rem(j, SLOTS)
            p_own[slot] = (p_own[slot].astype(F32) + r_core[lax.rem(j, 2)].astype(F32)).astype(BF)
            start_all(gather_back(j))

        def finish(j):
            wait_all(gather_back(j))
            slot = lax.rem(j, SLOTS)
            mine = pl.ds(pl.multiple_of(me * TOK, TOK), TOK)
            totals = [p_own[slot, mine].astype(F32), jnp.zeros((TOK, CW), F32)]
            for i, (dy, dc) in enumerate(peers):
                totals[dc] += fs_buf[slot, i].astype(F32)
            for side, half in enumerate((core, 1 - core)):
                hidden = hown[j, side].astype(F32)
                out_ref[:, columns(half, j)] = (hidden + totals[side]).astype(BF)

        def prepare_back(j):
            pl.when(j == 0)(pickers_out)

        pipeline(
            [
                (0, down),
                (1, prepare_back),
                (2, back_forward),
                (4, combine),
                (5, add_back),
                (7, finish),
            ]
        )

    pl.run_scoped(experts, pltpu.VMEM((1152, 2 * FF), F32), pltpu.VMEM((1152, CW), F32))


def moe_call(queries, latents, w_uk, w_uv, w_o, stream, w_gate, w_up, w_down, gain, rope, ids, gates):
    grid_rows = (CHUNKS, 2, RING, RING, ROWS, CW)
    one = DMA((CHUNKS,))
    ring = DMA((CHUNKS, 4))
    phase = DMA((CHUNKS, 7))
    return pl.pallas_call(
        moe_kernel,
        out_shape=jax.ShapeDtypeStruct((TOK, D), BF),
        in_specs=[ANY] * 9 + [VM] * 4,
        out_specs=VM,
        scratch_shapes=[
            pltpu.VMEM((8, TOK, QW), BF),
            pltpu.VMEM((8, TOK, LATW), BF),
            pltpu.VMEM((128, TOK), F32),
            *[DMA((8,))] * 4,
            DMA((2,)),
            pltpu.VMEM((1152, 1024), BF),
            pltpu.VMEM(grid_rows, BF),
            pltpu.VMEM((SLOTS, LEN, CW), BF),
            pltpu.VMEM((2, LEN, CW), BF),
            pltpu.VMEM((2, LEN, CW), BF),
            pltpu.VMEM((SLOTS, 3, CHIP, CW), BF),
            pltpu.VMEM(grid_rows, BF),
            pltpu.VMEM((SLOTS, *grid_rows[1:]), BF),
            pltpu.VMEM(grid_rows, BF),
            pltpu.VMEM((ROWS_IN, *grid_rows[1:]), BF),
            pltpu.VMEM((1152, 1152), BF),
            pltpu.VMEM((D, FF), BF),
            pltpu.VMEM((D, FF), BF),
            pltpu.VMEM((FF, D), BF),
            pltpu.VMEM((2, TOK, HALF), BF),
            pltpu.VMEM((CHUNKS, 2, TOK, CW), BF),
            pltpu.VMEM((SLOTS, 7, TOK, CW), BF),
            pltpu.VMEM((2, LEN, 128), BF),
            DMA((2,)),
            DMA((CHUNKS, 2)),
            DMA((3,)),
            DMA((2,)),
            *[one, one, ring, ring, ring, ring, one, one],
            *[phase] * 8,
            *[one, one],
            *[DMA((CHUNKS, 7))] * 2,
            *[DMA((CHUNKS, 2))] * 4,
        ],
        compiler_params=pltpu.CompilerParams(
            collective_id=2, has_side_effects=True, vmem_limit_bytes=63 * 2**20
        ),
        name="moe",
    )(queries, latents, w_uk, w_uv, w_o, stream, w_gate, w_up, w_down, gain, rope, ids, gates)


def local(
    stream_in,
    queries,
    latents,
    key_rope,
    w_uk,
    w_uv,
    w_o,
    norm_gain,
    expert_ids,
    gate_weights,
    w_gate,
    w_up,
    w_down,
):
    blocks = w_o.reshape(RING, RING, 64, D)
    out = moe_call(
        queries[0],
        latents[0],
        w_uk,
        w_uv,
        blocks,
        stream_in[0],
        w_gate[0],
        w_up[0],
        w_down[0],
        norm_gain.reshape(2 * CHUNKS, CW),
        key_rope[0].T,
        jnp.transpose(expert_ids, (2, 0, 1)),
        jnp.transpose(gate_weights, (2, 0, 1)),
    )
    return out[None]


def solution(mesh):
    return jax.shard_map(
        local,
        mesh=mesh,
        in_specs=(
            P("exp", "ctx", None),
            P("exp", "ctx", None),
            P("exp", "ctx", None),
            P("exp", "ctx", None),
            P(None, "ctx"),
            P(None, "ctx"),
            P("ctx", None),
            P(),
            P("exp", "ctx", None),
            P("exp", "ctx", None),
            P(("ctx", "exp"), None, None),
            P(("ctx", "exp"), None, None),
            P(("ctx", "exp"), None, None),
        ),
        out_specs=P("exp", "ctx", None),
        check_vma=False,
    )
```
